256 devices in a mesh: shots: 32 (over z, y_hi, core), depth: 8 (over x, y_lo).
Axes of the slice: x: 4, y: 4 (y_hi: 2, y_lo: 2; y = y_hi * 2 + y_lo), z: 8, core: 2. Of those that a mesh axis runs over, the one named last changes fastest.
Arguments:
- model: float32 [32, 512, 512], P('depth', 'shots'), may hold values from 1.5 to 4.5
- offsets_x: int32 [32], replicated, may hold values from 0 to 448
- offsets_y: int32 [32], replicated, may hold values from 0 to 256
- ckpt_prev: float32 [32, 32, 64, 256], P('shots', 'depth'), may hold values from -6 to 6
- ckpt_cur: float32 [32, 32, 64, 256], P('shots', 'depth'), may hold values from -6 to 6
- wavelet: float32 [32, 4], P('shots'), may hold values from -128 to 128
- source: int32 [32], P('shots'), may hold values from 0 to 524287
- receivers: int32 [32, 4096], P('shots'), may hold values from 0 to 524287
- traces: float32 [32, 4, 4096], P('shots'), may hold values from -6 to 6
Outputs:
- gradient: float32 [32, 512, 512], P('depth', 'shots')
The draws below stay inside these ranges and needn't reach their ends.
All inputs are finite; a program needn't handle non-finite values.
Results may differ from the reference program's by a relative error of at most 0.0003.
Values sent between devices are 32-bit elements; how exact they have to be, the bound alone decides.
A program may use at most 64 MiB of HBM per device.

```python
import jax
import jax.numpy as jnp
from jax import lax

AX = 64
AY = 256
GY = 512
NREC = 4096
STEPS = 4
GX = 512
GZ = 32
N_SHOTS = 32


def place_ends(values, own_key, least, top_value):
    spot = [jax.random.randint(jax.random.fold_in(own_key, axis), (), 0, length) for axis, length in enumerate(values.shape)]
    widest = values.shape.index(max(values.shape))
    beside = spot[:widest] + [(spot[widest] + 1) % values.shape[widest]] + spot[widest + 1:]
    return values.at[tuple(spot)].set(least).at[tuple(beside)].set(top_value)


def levels(rng, shape, cuts, smallest, high):
    def one(position, parts):
        draws = jax.random.uniform(jax.random.fold_in(jax.random.fold_in(rng, 6), position), (parts,), jnp.float32, smallest / len(cuts), high / len(cuts))
        return jnp.repeat(jnp.exp(draws), shape[position] // parts).reshape((-1,) + (1,) * (len(shape) - position - 1))

    loudness = one(*cuts[0])
    for cut in cuts[1:]:
        loudness = loudness * one(*cut)
    return loudness


def bell_draw(own_key, shape, scale, limit, shards=(), kind=jnp.bfloat16):
    drawn = scale * jax.random.normal(own_key, shape, jnp.float32)
    if shards:
        drawn = drawn * levels(own_key, shape, shards, -0.22, 0.18)
    return jnp.clip(drawn, -limit, limit).astype(kind)


def setup_inputs(seed: int = 0) -> dict:
    splits = jax.random.split(jax.random.key(seed), 10)
    model = jnp.clip(1.5 + 3.0 * jax.random.uniform(splits[0], (GZ, GX, GY), jnp.float32) ** levels(splits[0], (GZ, GX, GY), ((0, 8), (1, 32)), -0.2, 0.2), 1.5, 4.5)
    offsets_x = place_ends(jax.random.randint(splits[1], (N_SHOTS,), 0, GX - AX + 1), jax.random.fold_in(splits[1], 1), 0, GX - AX).astype(jnp.int32)
    offsets_y = place_ends(jax.random.randint(splits[2], (N_SHOTS,), 0, GY - AY + 1), jax.random.fold_in(splits[2], 1), 0, GY - AY).astype(jnp.int32)
    ckpt_prev = bell_draw(splits[3], (N_SHOTS, GZ, AX, AY), 1.0, 6.0, ((0, 32), (1, 8)), jnp.float32)
    ckpt_cur = bell_draw(splits[4], (N_SHOTS, GZ, AX, AY), 1.0, 6.0, ((0, 32), (1, 8)), jnp.float32)
    wavelet = bell_draw(splits[5], (N_SHOTS, STEPS), 24.0, 128.0, ((0, 32),), jnp.float32)
    source = place_ends(jax.random.randint(splits[6], (N_SHOTS,), 0, GZ * AX * AY), jax.random.fold_in(splits[6], 1), 0, (GZ * AX * AY) - 1).astype(jnp.int32)
    receivers = place_ends(jax.random.randint(splits[7], (N_SHOTS, NREC), 0, GZ * AX * AY), jax.random.fold_in(splits[7], 1), 0, (GZ * AX * AY) - 1).astype(jnp.int32)
    traces = bell_draw(splits[8], (N_SHOTS, STEPS, NREC), 1.0, 6.0, ((0, 32),), jnp.float32)
    return {"model": model, "offsets_x": offsets_x, "offsets_y": offsets_y, "ckpt_prev": ckpt_prev, "ckpt_cur": ckpt_cur, "wavelet": wavelet, "source": source, "receivers": receivers, "traces": traces}


stencil_weights = (-205.0 / 72.0, 8.0 / 5.0, -1.0 / 5.0, 8.0 / 315.0, -1.0 / 560.0)
courant = 0.095
lower_bound = 1.0
upper_bound = 5.0
barrier_weight = 0.5


def laplace(field):
    depth_n, rows_n, cols_n = field.shape
    padded = jnp.pad(field, 4)
    total = 3.0 * stencil_weights[0] * field
    for step in range(1, 5):
        part = padded[4 + step:4 + step + depth_n, 4:4 + rows_n, 4:4 + cols_n]
        part = part + padded[4 - step:4 - step + depth_n, 4:4 + rows_n, 4:4 + cols_n]
        part = part + padded[4:4 + depth_n, 4 + step:4 + step + rows_n, 4:4 + cols_n]
        part = part + padded[4:4 + depth_n, 4 - step:4 - step + rows_n, 4:4 + cols_n]
        part = part + padded[4:4 + depth_n, 4:4 + rows_n, 4 + step:4 + step + cols_n]
        part = part + padded[4:4 + depth_n, 4:4 + rows_n, 4 - step:4 - step + cols_n]
        total = total + stencil_weights[step] * part
    return total


def inject(field, places, values):
    return field.reshape(-1).at[places].add(values).reshape(field.shape)


def one_shot(model, start_x, start_y, prev, cur, pulse, place, listing, record):
    zero = jnp.zeros((), jnp.int32)
    speed = lax.dynamic_slice(model, (zero, start_x.astype(jnp.int32), start_y.astype(jnp.int32)), (GZ, AX, AY))
    c2v = (courant * speed) ** 2
    accels = []
    for step in range(STEPS):
        accel = inject(c2v * laplace(cur), place[None], pulse[step][None])
        accels.append(accel)
        prev, cur = cur, 2.0 * cur - prev + accel
    older = jnp.zeros_like(cur)
    adjoint = inject(jnp.zeros_like(cur), listing, record[0])
    partial_value = adjoint * accels[STEPS - 1]
    for step in range(1, STEPS):
        newer = 2.0 * adjoint - older + c2v * laplace(adjoint)
        newer = inject(newer, listing, record[step])
        partial_value = partial_value + newer * accels[STEPS - 1 - step]
        older, adjoint = adjoint, newer
    return partial_value * 2.0 / speed


def reference(model, offsets_x, offsets_y, ckpt_prev, ckpt_cur, wavelet, source, receivers, traces):
    zero = jnp.zeros((), jnp.int32)

    def accumulate(total, items):
        start_x, start_y, prev, cur, pulse, place, listing, record = items
        partial_value = one_shot(model, start_x, start_y, prev, cur, pulse, place, listing, record)
        where = (zero, start_x.astype(jnp.int32), start_y.astype(jnp.int32))
        window = lax.dynamic_slice(total, where, partial_value.shape)
        return lax.dynamic_update_slice(total, window + partial_value, where), None

    summed, _ = lax.scan(accumulate, jnp.zeros(model.shape, jnp.float32),
                         (offsets_x, offsets_y, ckpt_prev, ckpt_cur, wavelet, source, receivers, traces))
    scaling = (model - lower_bound) * (upper_bound - model) / (upper_bound - lower_bound)
    barrier = barrier_weight / (upper_bound - model) - barrier_weight / (model - lower_bound)
    return scaling * (summed + barrier)
```

```python
import functools

import jax
import jax.numpy as jnp
from jax import lax
from jax.experimental import pallas as pl
from jax.experimental.pallas import tpu as pltpu
from jax.sharding import PartitionSpec as P

MESH = pl.DeviceIdType.MESH
F32 = jnp.float32
BF16 = jnp.bfloat16
STEPS = 4

stencil_weights = (-205.0 / 72.0, 8.0 / 5.0, -1.0 / 5.0, 8.0 / 315.0, -1.0 / 560.0)
courant = 0.095
lower_bound = 1.0
upper_bound = 5.0
barrier_weight = 0.5

PARTS = 8
LOCAL = 4
PLANES = 16
SPAN = 64
LANES = 128
ROWS = 16
HALO = 16
OWN = 32
CHUNK = 512
PAD = 8


def iota(shape, dim):
    return lax.broadcasted_iota(jnp.int32, shape, dim)


def window(first, second, part):
    rows = first[0].shape[0]
    lane = iota((rows, LANES), 1)
    zero = jnp.zeros((rows, LANES), F32)
    start = OWN * part - HALO
    tile, at = start // LANES, start % LANES

    def pick(tiles, k):
        return tiles[k] if 0 <= k < 2 else zero

    half = lane - at if at <= 64 else lane - at + LANES
    if at <= 64:
        low = pick(first, tile)
        in_low = (lane >= at) & (lane < at + 64)
        own = (lane + 64) % LANES
        high = jnp.where(own >= at, pick(second, tile), pick(second, tile + 1))
        if at == 0:
            high = pick(second, tile)
    else:
        low = jnp.where(lane >= at, pick(first, tile), pick(first, tile + 1))
        in_low = (lane >= at) | (lane < at - 64)
        own = (lane + 64) % LANES
        high = jnp.where(own >= at, pick(second, tile), pick(second, tile + 1))
    del half
    both = jnp.where(in_low, low, high)
    return pltpu.roll(both, (LANES - at) % LANES, 1) if at else both


def kernel(
    near,
    offx, offy, pulse, place, model, prev, cur, listing, record,
    out,
    gathered, stage, fields, lams, shifted, onto, summed_r, windows, arrived, speeds, c2v, first_lap, accels, partial,
    packed, outgoing, landed, placed, totals, ring_p, ring_m,
    gp_send, gp_recv, gm_send, gm_recv, ck_send, ck_recv, w_send, w_recv, o_send, o_recv,
    rp_send, rp_recv, rm_send, rm_recv,
):
    shot = lax.axis_index("shots")
    part = lax.axis_index("depth")
    level = lax.div(shot, LOCAL)
    group = lax.rem(shot, LOCAL)
    me = group * PARTS + part
    peers = LOCAL * PARTS
    up = lax.rem(level + 1, near)
    down = lax.rem(level + near - 1, near)
    lane = iota((SPAN, LANES), 1)
    lower = lane < 64

    def device(k):
        return (LOCAL * level + lax.div(k, PARTS), lax.rem(k, PARTS))

    barrier = pltpu.get_barrier_semaphore()

    def greet(k, carry):
        pl.semaphore_signal(barrier, inc=1, device_id=device(lax.rem(me + k, peers)), device_id_type=MESH)
        return carry

    for other in (up, down):
        pl.semaphore_signal(barrier, inc=1, device_id=(LOCAL * other + group, part), device_id_type=MESH)
    lax.fori_loop(1, peers, greet, 0)

    for tile in range(4):
        gathered[level, :, tile] = model[:, :, pl.ds(LANES * tile, LANES)]
    for which, source in ((0, cur), (1, prev)):
        for i in range(2):
            low = [source[0, i, :, pl.ds(LANES * k, LANES)] for k in range(2)]
            high = [pltpu.roll(source[0, 2 + i, :, pl.ds(LANES * k, LANES)], 64, 1) for k in range(2)]
            for to in range(PARTS):
                stage[which, to, i] = window(low, high, to)

    pl.semaphore_wait(barrier, peers + 1)

    def ring_copy(m, sign, send, recv):
        origin = lax.rem(level + near - sign * lax.div(m, 2) + near, near)
        chunk = lax.rem(m, 2) if sign > 0 else 1 - lax.rem(m, 2)
        where = gathered.at[origin, pl.ds(2 * chunk, 2)]
        to = up if sign > 0 else down
        return pltpu.make_async_remote_copy(
            src_ref=where, dst_ref=where, send_sem=send.at[m], recv_sem=recv.at[m],
            device_id=(LOCAL * to + group, part), device_id_type=MESH,
        )

    def ring_wait(m, sign, send, recv):
        origin = lax.rem(level + near - sign * (lax.div(m, 2) + 1) + near, near)
        chunk = lax.rem(m, 2) if sign > 0 else 1 - lax.rem(m, 2)
        where = gathered.at[origin, pl.ds(2 * chunk, 2)]
        to = up if sign > 0 else down
        pltpu.make_async_remote_copy(
            src_ref=where, dst_ref=where, send_sem=send.at[m], recv_sem=recv.at[m],
            device_id=(LOCAL * to + group, part), device_id_type=MESH,
        ).wait_recv()

    def ckpt_copy(which, to, origin):
        return pltpu.make_async_remote_copy(
            src_ref=stage.at[which, to],
            dst_ref=fields.at[which, pl.ds(2 + 2 * origin, 2), pl.ds(PAD, SPAN)],
            send_sem=ck_send.at[which, to], recv_sem=ck_recv.at[which, origin],
            device_id=(shot, to), device_id_type=MESH,
        )

    ring_copy(0, 1, gp_send, gp_recv).start()
    ring_copy(0, -1, gm_send, gm_recv).start()
    ring_copy(1, 1, gp_send, gp_recv).start()
    ring_copy(1, -1, gm_send, gm_recv).start()

    def ckpt_start(k, carry):
        to = lax.rem(part + k, PARTS)
        ckpt_copy(0, to, part).start()
        ckpt_copy(1, to, part).start()
        return carry

    lax.fori_loop(1, PARTS, ckpt_start, 0)

    for ref, slots in ((fields, 2), (lams, 3)):
        for slot in range(slots):
            for edge in (0, 1, PLANES + 2, PLANES + 3):
                ref[slot, edge] = jnp.zeros((SPAN + 2 * PAD, LANES), F32)
            for edge in range(2, PLANES + 2):
                ref[slot, edge, pl.ds(0, PAD)] = jnp.zeros((PAD, LANES), F32)
                ref[slot, edge, pl.ds(PAD + SPAN, PAD)] = jnp.zeros((PAD, LANES), F32)
    for which in range(2):
        fields[which, pl.ds(2 + 2 * part, 2), pl.ds(PAD, SPAN)] = stage[which, part]
    for b in range(LOCAL):
        for tile in (0, 1, 5):
            placed[b, :, tile] = jnp.zeros((4, ROWS, LANES), F32)

    summed_r[...] = jnp.zeros(summed_r.shape, F32)

    def receivers(step):
        at = pl.ds(pl.multiple_of(step * CHUNK, CHUNK), CHUNK)
        flat = listing[:, at]
        zc = lax.shift_right_logical(flat, 14)
        x = lax.shift_right_logical(flat, 8) & 63
        y = (flat & 255) - (OWN * part - HALO)
        row = (lax.shift_right_logical(zc, 2) * 2 + (zc & 1)) * SPAN + x
        column = jnp.where((y >= 0) & (y < 64), (lax.shift_right_logical(zc, 1) & 1) * 64 + y, -1)
        hot = (iota((PLANES * SPAN, CHUNK), 0) == row).astype(F32).astype(BF16)
        match = iota((LANES, CHUNK), 0) == column
        for k in range(STEPS):
            value = record[0, pl.ds(k, 1), at]
            high = value.astype(BF16).astype(F32)
            rest = value - high
            onto[pl.ds(LANES * k, LANES), pl.ds(0, CHUNK)] = jnp.where(match, high, 0.0).astype(BF16)
            onto[pl.ds(LANES * k, LANES), pl.ds(CHUNK, CHUNK)] = jnp.where(match, rest, 0.0).astype(BF16)
        dims = (((1,), (1,)), ((), ()))
        total = lax.dot_general(hot, onto[:, pl.ds(0, CHUNK)], dims, preferred_element_type=F32)
        total = total + lax.dot_general(hot, onto[:, pl.ds(CHUNK, CHUNK)], dims, preferred_element_type=F32)
        summed_r[...] += total

    def ring_step(m, carry):
        ring_wait(m - 2, 1, gp_send, gp_recv)
        ring_copy(m, 1, gp_send, gp_recv).start()
        ring_wait(m - 2, -1, gm_send, gm_recv)
        ring_copy(m, -1, gm_send, gm_recv).start()
        receivers(m)
        return carry

    def two_first(m, carry):
        receivers(m)
        return carry

    lax.fori_loop(0, 2, two_first, 0)
    lax.fori_loop(2, 7, ring_step, 0)
    receivers(7)

    def laplace(field, slot, e):
        result = []
        at = 2 + 2 * e

        def own(k):
            return field[slot, at + k, pl.ds(PAD, SPAN)]

        def other(k):
            return shifted[at + k]

        along_z = (
            ((own(1), other(-1)), (other(0), other(-2)), (other(1), own(-1)), (own(2), own(-2))),
            ((other(0), own(0)), (other(1), other(-1)), (own(2), other(-2)), (own(3), own(-1))),
        )
        for i in range(2):
            middle = own(i)
            total = 3.0 * stencil_weights[0] * middle
            for k in range(1, 5):
                some = along_z[i][k - 1][0] + along_z[i][k - 1][1]
                some = some + field[slot, at + i, pl.ds(PAD + k, SPAN)]
                some = some + field[slot, at + i, pl.ds(PAD - k, SPAN)]
                some = some + pltpu.roll(middle, k, 1)
                some = some + pltpu.roll(middle, LANES - k, 1)
                total = total + stencil_weights[k] * some
            result.append(total)
        return result

    def shift(field, slot):
        def one(p, carry):
            both = jnp.where(lower, field[slot, p + 2, pl.ds(PAD, SPAN)], field[slot, p, pl.ds(PAD, SPAN)])
            shifted[p] = pltpu.roll(both, 64, 1)
            return carry

        lax.fori_loop(0, PLANES + 2, one, 0)

    def residual(k, p):
        return summed_r[pl.ds(pl.multiple_of(p * SPAN, SPAN), SPAN), pl.ds(LANES * k, LANES)]

    def to_lam(p, carry):
        lams[0, p + 2, pl.ds(PAD, SPAN)] = residual(0, p)
        return carry

    lax.fori_loop(0, PLANES, to_lam, 0)

    def ckpt_wait(k, carry):
        origin = lax.rem(part + k, PARTS)
        ckpt_copy(0, part, origin).wait_recv()
        ckpt_copy(1, part, origin).wait_recv()
        return carry

    lax.fori_loop(1, PARTS, ckpt_wait, 0)

    def keep_lap(field, slot, which):
        shift(field, slot)

        def one(e, carry):
            for i, value in enumerate(laplace(field, slot, e)):
                first_lap[which, 2 * e + i] = value
            return carry

        lax.fori_loop(0, PARTS, one, 0)

    keep_lap(fields, 0, 0)
    keep_lap(lams, 0, 1)

    for m in (5, 6):
        ring_wait(m, 1, gp_send, gp_recv)
        ring_wait(m, -1, gm_send, gm_recv)

    small = iota((ROWS, LANES), 1)
    row16 = iota((ROWS, LANES), 0)

    def window_copy(to, origin):
        return pltpu.make_async_remote_copy(
            src_ref=windows.at[to],
            dst_ref=arrived.at[pl.ds(2 * lax.rem(origin, PARTS), 2), pl.ds(ROWS * lax.div(origin, PARTS), ROWS)],
            send_sem=w_send.at[to], recv_sem=w_recv.at[origin],
            device_id=device(to), device_id_type=MESH,
        )

    def spot(b):
        ox = offx[LOCAL * level + b]
        oy = offy[LOCAL * level + b]
        t = ox - ROWS * group + SPAN
        return lax.shift_right_logical(t, 6) - 1, t & 63, lax.shift_right_logical(oy, 7), oy & 127

    def cut(b, carry):
        block, rest, tile, at = spot(b)
        upper_rows = row16 >= rest
        q0 = jnp.maximum(block, 0)
        q1 = jnp.minimum(block + 1, near - 1)
        back = lax.rem(LANES - at, LANES)
        keep = small < LANES - at
        planes = []
        for plane in range(4):
            turned_tiles = []
            for k in range(3):
                t = jnp.minimum(tile + k, 3)
                mixed = jnp.where(upper_rows, gathered[q0, plane, t], gathered[q1, plane, t])
                turned_tiles.append(pltpu.roll(mixed, back, 1))
            planes.append([jnp.where(keep, turned_tiles[k], turned_tiles[k + 1]) for k in range(2)])
        for i in range(2):
            high = [pltpu.roll(v, 64, 1) for v in planes[2 + i]]
            for to in range(PARTS):
                windows[b * PARTS + to, i] = window(planes[i], high, to)
        for to in range(PARTS):
            @pl.when(b * PARTS + to != me)
            def _():
                window_copy(b * PARTS + to, me).start()
        return carry

    lax.fori_loop(0, LOCAL, cut, 0)
    arrived[pl.ds(2 * part, 2), pl.ds(ROWS * group, ROWS)] = windows[me]

    def window_wait(k, carry):
        window_copy(me, lax.rem(me + k, peers)).wait_recv()
        return carry

    lax.fori_loop(1, peers, window_wait, 0)

    turn = offx[shot] & 63

    def make_c2v(p, carry):
        arrived[p, pl.ds(SPAN, SPAN)] = arrived[p, pl.ds(0, SPAN)]
        speed = arrived[p, pl.ds(turn, SPAN)]
        speeds[p] = speed
        scaled = courant * speed
        c2v[p] = scaled * scaled
        return carry

    lax.fori_loop(0, PLANES, make_c2v, 0)

    flat = place[0]
    zc = lax.shift_right_logical(flat, 14)
    sy = (flat & 255) - (OWN * part - HALO)
    s_plane = lax.shift_right_logical(zc, 2) * 2 + (zc & 1)
    s_lane = jnp.where((sy >= 0) & (sy < 64), (lax.shift_right_logical(zc, 1) & 1) * 64 + sy, -1)
    at_source = (lane == s_lane) & (iota((SPAN, LANES), 0) == (lax.shift_right_logical(flat, 8) & 63))

    def accel_of(value, p, n):
        strength = jnp.where(p == s_plane, pulse[0, n], 0.0)
        return c2v[p] * value + jnp.where(at_source, strength, 0.0)

    inner = pl.ds(PAD, SPAN)

    for n in range(STEPS):
        now, old = n % 2, 1 - n % 2
        if n:
            shift(fields, now)

        def forward(e, carry, n=n, now=now, old=old):
            laps = laplace(fields, now, e) if n else [first_lap[0, 2 * e + i] for i in range(2)]
            for i in range(2):
                p = 2 * e + i
                accel = accel_of(laps[i], p, n)
                accels[n, p] = accel
                if n < STEPS - 1:
                    fields[old, p + 2, inner] = (
                        2.0 * fields[now, p + 2, inner] - fields[old, p + 2, inner] + accel
                    )
            return carry

        lax.fori_loop(0, PARTS, forward, 0)

    def out_copy(to, origin):
        return pltpu.make_async_remote_copy(
            src_ref=outgoing.at[lax.rem(to, PARTS), pl.ds(ROWS * lax.div(to, PARTS), ROWS)],
            dst_ref=landed.at[origin],
            send_sem=o_send.at[to], recv_sem=o_recv.at[origin],
            device_id=device(to), device_id_type=MESH,
        )

    for k in range(1, STEPS):
        now, old, new = (k - 1) % 3, (k - 2) % 3, k % 3
        if k > 1:
            shift(lams, now)

        def adjoint(e, carry, k=k, now=now, old=old, new=new):
            laps = laplace(lams, now, e) if k > 1 else [first_lap[1, 2 * e + i] for i in range(2)]
            parts = []
            for i in range(2):
                p = 2 * e + i
                lam = lams[now, p + 2, inner]
                newer = 2.0 * lam + c2v[p] * laps[i] + residual(k, p)
                if k > 1:
                    newer = newer - lams[old, p + 2, inner]
                    so_far = partial[p]
                else:
                    so_far = lam * accels[STEPS - 1, p]
                so_far = so_far + newer * accels[STEPS - 1 - k, p]
                if k < STEPS - 1:
                    lams[new, p + 2, inner] = newer
                    partial[p] = so_far
                else:
                    parts.append(so_far * 2.0 / speeds[p])
            if k == STEPS - 1:
                both = jnp.where(
                    (lane & 63) < OWN, pltpu.roll(parts[0], LANES - HALO, 1), pltpu.roll(parts[1], OWN - HALO, 1)
                )
                packed[e, pl.ds(0, SPAN)] = both
                packed[e, pl.ds(SPAN, SPAN)] = both
                outgoing[e] = packed[e, pl.ds((SPAN - turn) & 63, SPAN)]
                for b in range(LOCAL):
                    @pl.when(b * PARTS + e != me)
                    def _():
                        out_copy(b * PARTS + e, me).start()
            return carry

        lax.fori_loop(0, PARTS, adjoint, 0)

    landed[me] = outgoing[part, pl.ds(pl.multiple_of(ROWS * group, ROWS), ROWS)]

    def out_wait(k, carry):
        out_copy(me, lax.rem(me + k, peers)).wait_recv()
        return carry

    lax.fori_loop(1, peers, out_wait, 0)

    def put(b, carry):
        block, rest, tile, at = spot(b)
        group_of = lax.shift_right_logical(small, 5)
        keep = small >= at
        for plane in range(4):
            halves = []
            for k in range(2):
                total = None
                for c in range(4):
                    piece = landed[b * PARTS + 4 * k + c]
                    by = (OWN * (c - plane)) % LANES
                    if by:
                        piece = pltpu.roll(piece, by, 1)
                    total = piece if total is None else jnp.where(group_of == c, piece, total)
                halves.append(pltpu.roll(total, at, 1))
            placed[b, plane, 2] = jnp.where(keep, halves[0], 0.0)
            placed[b, plane, 3] = jnp.where(keep, halves[1], halves[0])
            placed[b, plane, 4] = jnp.where(keep, 0.0, halves[1])
        return carry

    lax.fori_loop(0, LOCAL, put, 0)

    spots = [spot(b) for b in range(LOCAL)]
    blocks = [jnp.where(iota((4, ROWS, LANES), 1) >= s[1], s[0], s[0] + 1) for s in spots]

    def add_up(plane, carry):
        cells = [
            placed[b, plane, pl.ds(2 - spots[b][2], 4)]
            for b in range(LOCAL)
        ]

        def one(q, carry):
            total = jnp.where(blocks[0] == q, cells[0], 0.0)
            for b in range(1, LOCAL):
                total = total + jnp.where(blocks[b] == q, cells[b], 0.0)
            totals[q, plane] = total
            return carry

        return lax.fori_loop(0, near, one, carry)

    lax.fori_loop(0, 4, add_up, 0)

    half = near // 2

    def sum_chunk(m, sign):
        odd = m % 2
        return odd if sign > 0 else 1 - odd

    def sum_copy(m, sign, ring, send, recv):
        target = lax.rem(level + near + sign * (half - (m + 1) // 2), near)
        to = up if sign > 0 else down
        return pltpu.make_async_remote_copy(
            src_ref=totals.at[target, pl.ds(2 * sum_chunk(m, sign), 2)], dst_ref=ring.at[m],
            send_sem=send.at[m], recv_sem=recv.at[m],
            device_id=(LOCAL * to + group, part), device_id_type=MESH,
        )

    ways = ((1, ring_p, rp_send, rp_recv), (-1, ring_m, rm_send, rm_recv))
    for m in range(near - 1):
        for sign, ring, send, recv in ways:
            if m >= 2:
                sum_copy(m - 2, sign, ring, send, recv).wait_recv()
                target = lax.rem(level + near + sign * (half - (m + 1) // 2), near)
                where = pl.ds(2 * sum_chunk(m, sign), 2)
                totals[target, where] = totals[target, where] + ring[m - 2]
            sum_copy(m, sign, ring, send, recv).start()
    for m in (near - 3, near - 2):
        for sign, ring, send, recv in ways:
            sum_copy(m, sign, ring, send, recv).wait_recv()
    for c in range(2):
        where = pl.ds(2 * c, 2)
        total = totals[level, where]
        for sign, ring, send, recv in ways:
            for m in (near - 3, near - 2):
                if sum_chunk(m, sign) == c:
                    total = total + ring[m]
        speed = model[where]
        total = jnp.concatenate([total[:, tile] for tile in range(4)], axis=-1)
        scaling = (speed - lower_bound) * (upper_bound - speed) / (upper_bound - lower_bound)
        limit = barrier_weight / (upper_bound - speed) - barrier_weight / (speed - lower_bound)
        out[where] = scaling * (total + limit)

    for m in range(near - 1):
        ring_copy(m, 1, gp_send, gp_recv).wait_send()
        ring_copy(m, -1, gm_send, gm_recv).wait_send()
        for sign, ring, send, recv in ways:
            sum_copy(m, sign, ring, send, recv).wait_send()

    def ckpt_sent(k, carry):
        to = lax.rem(part + k, PARTS)
        ckpt_copy(0, to, part).wait_send()
        ckpt_copy(1, to, part).wait_send()
        return carry

    lax.fori_loop(1, PARTS, ckpt_sent, 0)

    def blocks_sent(k, carry):
        to = lax.rem(me + k, peers)
        window_copy(to, me).wait_send()
        out_copy(to, me).wait_send()
        return carry

    lax.fori_loop(1, peers, blocks_sent, 0)


def on_device(near, model, offsets_x, offsets_y, ckpt_prev, ckpt_cur, wavelet, source, receivers, traces):
    peers = LOCAL * PARTS
    vmem = pl.BlockSpec(memory_space=pltpu.VMEM)
    smem = pl.BlockSpec(memory_space=pltpu.SMEM)
    padded = (PLANES + 4, SPAN + 2 * PAD, LANES)
    plain = (PLANES, SPAN, LANES)
    dma = pltpu.SemaphoreType.DMA
    return pl.pallas_call(
        functools.partial(kernel, near),
        out_shape=jax.ShapeDtypeStruct(model.shape, F32),
        in_specs=[smem] * 4 + [vmem] * 5,
        out_specs=vmem,
        scratch_shapes=[
            pltpu.VMEM((near, 4, 4, ROWS, LANES), F32),
            pltpu.VMEM((2, PARTS, 2, SPAN, LANES), F32),
            pltpu.VMEM((2,) + padded, F32),
            pltpu.VMEM((3,) + padded, F32),
            pltpu.VMEM((PLANES + 2, SPAN, LANES), F32),
            pltpu.VMEM((STEPS * LANES, 2 * CHUNK), BF16),
            pltpu.VMEM((PLANES * SPAN, STEPS * LANES), F32),
            pltpu.VMEM((peers, 2, ROWS, LANES), F32),
            pltpu.VMEM((PLANES, 2 * SPAN, LANES), F32),
            pltpu.VMEM(plain, F32),
            pltpu.VMEM(plain, F32),
            pltpu.VMEM((2,) + plain, F32),
            pltpu.VMEM((STEPS,) + plain, F32),
            pltpu.VMEM(plain, F32),
            pltpu.VMEM((PARTS, 2 * SPAN, LANES), F32),
            pltpu.VMEM((PARTS, SPAN, LANES), F32),
            pltpu.VMEM((peers, ROWS, LANES), F32),
            pltpu.VMEM((LOCAL, 4, 6, ROWS, LANES), F32),
            pltpu.VMEM((near, 4, 4, ROWS, LANES), F32),
            pltpu.VMEM((near - 1, 2, 4, ROWS, LANES), F32),
            pltpu.VMEM((near - 1, 2, 4, ROWS, LANES), F32),
            dma((near - 1,)), dma((near - 1,)), dma((near - 1,)), dma((near - 1,)),
            dma((2, PARTS)), dma((2, PARTS)),
            dma((peers,)), dma((peers,)), dma((peers,)), dma((peers,)),
            dma((near - 1,)), dma((near - 1,)), dma((near - 1,)), dma((near - 1,)),
        ],
        compiler_params=pltpu.CompilerParams(
            collective_id=0, has_side_effects=True, vmem_limit_bytes=48 * 1024 * 1024
        ),
    )(offsets_x, offsets_y, wavelet, source, model, ckpt_prev, ckpt_cur, receivers, traces)


def solution(mesh):
    placed = (
        P("depth", "shots", None),
        P(),
        P(),
        P("shots", "depth", None, None),
        P("shots", "depth", None, None),
        P("shots", None),
        P("shots"),
        P("shots", None),
        P("shots", None, None),
    )
    near = mesh.shape["shots"] // LOCAL
    return jax.shard_map(
        functools.partial(on_device, near),
        mesh=mesh, in_specs=placed, out_specs=P("depth", "shots", None), check_vma=False,
    )
```

```python
import functools

import jax
import jax.numpy as jnp
import numpy as np
from jax import lax
from jax.experimental import pallas as pl
from jax.experimental.pallas import tpu as pltpu
from jax.sharding import PartitionSpec as P

MESH = pl.DeviceIdType.MESH
F32 = jnp.float32
BF16 = jnp.bfloat16
STEPS = 4

stencil_weights = (-205.0 / 72.0, 8.0 / 5.0, -1.0 / 5.0, 8.0 / 315.0, -1.0 / 560.0)
courant = 0.095
lower_bound = 1.0
upper_bound = 5.0
barrier_weight = 0.5

PARTS = 8
LOCAL = 4
PLANES = 16
SPAN = 64
LANES = 128
ROWS = 16
HALO = 16
OWN = 32
CHUNK = 256
PAD = 8
RING = 14
FIRST = 3


def iota(shape, dim):
    return lax.broadcasted_iota(jnp.int32, shape, dim)


def window(first, second, part):
    rows = first[0].shape[0]
    lane = iota((rows, LANES), 1)
    zero = jnp.zeros((rows, LANES), F32)
    start = OWN * part - HALO
    tile, at = start // LANES, start % LANES

    def pick(tiles, k):
        return tiles[k] if 0 <= k < 2 else zero

    if at <= 64:
        low = pick(first, tile)
        in_low = (lane >= at) & (lane < at + 64)
        high = pick(second, tile)
    else:
        low = jnp.where(lane >= at, pick(first, tile), pick(first, tile + 1))
        in_low = (lane >= at) | (lane < at - 64)
        own = (lane + 64) % LANES
        high = jnp.where(own >= at, pick(second, tile), pick(second, tile + 1))
    both = jnp.where(in_low, low, high)
    return pltpu.roll(both, (LANES - at) % LANES, 1) if at else both


def make_bands(bands):
    r, c = iota((LANES, LANES), 0), iota((LANES, LANES), 1)
    distance = jnp.where((r < 64) == (c < 64), jnp.abs(r - c), LANES)
    main = jnp.zeros((LANES, LANES), F32)
    rest = main
    for k, weight in enumerate(stencil_weights):
        rounded = float(np.float32(weight).astype(BF16))
        main = jnp.where(distance == k, rounded, main)
        rest = jnp.where(distance == k, float(np.float32(weight)) - rounded, rest)
    swap = (jnp.abs(r - c) == 64).astype(F32).astype(BF16)
    for half in range(2):
        bands[pl.ds(LANES * half, LANES), pl.ds(0, LANES)] = main.astype(BF16)
        bands[pl.ds(LANES * half, LANES), pl.ds(LANES, LANES)] = swap
    bands[pl.ds(2 * LANES, LANES), pl.ds(0, LANES)] = rest.astype(BF16)
    bands[pl.ds(2 * LANES, LANES), pl.ds(LANES, LANES)] = jnp.zeros((LANES, LANES), BF16)


def kernel(
    near,
    offx, offy, pulse, place, model_in, prev_in, cur_in, listing_in, record_in,
    out,
    model, prev, cur, listing, record,
    gathered, stage, fields, lams, bands, along_y, halves, onto, summed_r, windows, arrived, speeds, c2v, first_lap,
    accels, partial, packed, outgoing, landed, placed, totals, ring_p, ring_m,
    in_sems,
    gp_send, gp_recv, gm_send, gm_recv, ck_send, ck_recv, w_send, w_recv, o_send, o_recv,
    rp_send, rp_recv, rm_send, rm_recv,
):
    shot = lax.axis_index("shots")
    part = lax.axis_index("depth")
    level = lax.div(shot, LOCAL)
    group = lax.rem(shot, LOCAL)
    me = group * PARTS + part
    peers = LOCAL * PARTS
    up = lax.rem(level + 1, near)
    down = lax.rem(level + near - 1, near)
    lane = iota((SPAN, LANES), 1)
    lower = lane < 64

    def device(k):
        return (LOCAL * level + lax.div(k, PARTS), lax.rem(k, PARTS))

    inputs = [
        pltpu.make_async_copy(model_in, model, in_sems.at[0]),
        pltpu.make_async_copy(cur_in, cur, in_sems.at[1]),
        pltpu.make_async_copy(prev_in, prev, in_sems.at[2]),
        pltpu.make_async_copy(listing_in, listing, in_sems.at[3]),
        pltpu.make_async_copy(record_in, record, in_sems.at[4]),
    ]
    for copy in inputs:
        copy.start()

    barrier = pltpu.get_barrier_semaphore()

    def greet(k, carry):
        pl.semaphore_signal(barrier, inc=1, device_id=device(lax.rem(me + k, peers)), device_id_type=MESH)
        return carry

    for other in (up, down):
        pl.semaphore_signal(barrier, inc=1, device_id=(LOCAL * other + group, part), device_id_type=MESH)
    lax.fori_loop(1, peers, greet, 0)

    make_bands(bands)
    inputs[0].wait()
    for tile in range(4):
        gathered[level, :, tile] = model[:, :, pl.ds(LANES * tile, LANES)]
    for which, source in ((0, cur), (1, prev)):
        inputs[1 + which].wait()
        for i in range(2):
            low = [source[0, i, :, pl.ds(LANES * k, LANES)] for k in range(2)]
            high = [pltpu.roll(source[0, 2 + i, :, pl.ds(LANES * k, LANES)], 64, 1) for k in range(2)]
            for to in range(PARTS):
                stage[which, to, i] = window(low, high, to)

    pl.semaphore_wait(barrier, peers + 1)

    def ring_copy(m, sign, send, recv):
        origin = lax.rem(level + near - sign * lax.div(m, 4) + near, near)
        chunk = lax.rem(m + (0 if sign > 0 else 2), 4)
        where = gathered.at[origin, chunk]
        to = up if sign > 0 else down
        return pltpu.make_async_remote_copy(
            src_ref=where, dst_ref=where, send_sem=send.at[m], recv_sem=recv.at[m],
            device_id=(LOCAL * to + group, part), device_id_type=MESH,
        )

    def ring_wait(m, sign, send, recv):
        origin = lax.rem(level + near - sign * (lax.div(m, 4) + 1) + near, near)
        chunk = lax.rem(m + (0 if sign > 0 else 2), 4)
        where = gathered.at[origin, chunk]
        to = up if sign > 0 else down
        pltpu.make_async_remote_copy(
            src_ref=where, dst_ref=where, send_sem=send.at[m], recv_sem=recv.at[m],
            device_id=(LOCAL * to + group, part), device_id_type=MESH,
        ).wait_recv()

    def ckpt_copy(which, to, origin):
        return pltpu.make_async_remote_copy(
            src_ref=stage.at[which, to],
            dst_ref=fields.at[which, pl.ds(2 + 2 * origin, 2), pl.ds(PAD, SPAN)],
            send_sem=ck_send.at[which, to], recv_sem=ck_recv.at[which, origin],
            device_id=(shot, to), device_id_type=MESH,
        )

    for m in range(4):
        ring_copy(m, 1, gp_send, gp_recv).start()
        ring_copy(m, -1, gm_send, gm_recv).start()

    def ckpt_start(k, carry):
        to = lax.rem(part + k, PARTS)
        ckpt_copy(0, to, part).start()
        ckpt_copy(1, to, part).start()
        return carry

    lax.fori_loop(1, PARTS, ckpt_start, 0)

    for edge in (0, 1, PLANES + 2, PLANES + 3):
        halves[edge] = jnp.zeros((SPAN, LANES), F32)
    for ref, slots in ((fields, 2), (lams, 3)):
        for slot in range(slots):
            for edge in (0, 1, PLANES + 2, PLANES + 3):
                ref[slot, edge] = jnp.zeros((SPAN + 2 * PAD, LANES), F32)
            for edge in range(2, PLANES + 2):
                ref[slot, edge, pl.ds(0, PAD)] = jnp.zeros((PAD, LANES), F32)
                ref[slot, edge, pl.ds(PAD + SPAN, PAD)] = jnp.zeros((PAD, LANES), F32)
    for which in range(2):
        fields[which, pl.ds(2 + 2 * part, 2), pl.ds(PAD, SPAN)] = stage[which, part]
    for b in range(LOCAL):
        for tile in (0, 1, 5):
            placed[b, :, tile] = jnp.zeros((4, ROWS, LANES), F32)

    summed_r[...] = jnp.zeros(summed_r.shape, F32)

    def receivers(step):
        at = pl.ds(pl.multiple_of(step * CHUNK, CHUNK), CHUNK)
        flat = listing[:, at]
        zc = lax.shift_right_logical(flat, 14)
        x = lax.shift_right_logical(flat, 8) & 63
        y = (flat & 255) - (OWN * part - HALO)
        row = (lax.shift_right_logical(zc, 2) * 2 + (zc & 1)) * SPAN + x
        column = jnp.where((y >= 0) & (y < 64), (lax.shift_right_logical(zc, 1) & 1) * 64 + y, -1)
        hot = (iota((PLANES * SPAN, CHUNK), 0) == row).astype(F32).astype(BF16)
        match = iota((LANES, CHUNK), 0) == column
        for k in range(STEPS):
            value = record[0, pl.ds(k, 1), at]
            high = value.astype(BF16).astype(F32)
            rest = value - high
            onto[pl.ds(LANES * k, LANES), pl.ds(0, CHUNK)] = jnp.where(match, high, 0.0).astype(BF16)
            onto[pl.ds(LANES * k, LANES), pl.ds(CHUNK, CHUNK)] = jnp.where(match, rest, 0.0).astype(BF16)
        dims = (((1,), (1,)), ((), ()))
        both = jnp.concatenate([hot, hot], axis=1)
        summed_r[...] += lax.dot_general(both, onto[...], dims, preferred_element_type=F32)

    def ring_step(m, carry):
        ring_wait(m - 4, 1, gp_send, gp_recv)
        ring_copy(m, 1, gp_send, gp_recv).start()
        ring_wait(m - 4, -1, gm_send, gm_recv)
        ring_copy(m, -1, gm_send, gm_recv).start()
        receivers(m - 4 + FIRST)
        return carry

    def no_ring(m, carry):
        receivers(m)
        return carry

    inputs[3].wait()
    inputs[4].wait()
    lax.fori_loop(0, FIRST, no_ring, 0)
    lax.fori_loop(4, RING, ring_step, 0)
    lax.fori_loop(RING - 4 + FIRST, listing.shape[1] // CHUNK, no_ring, 0)

    def prepare(field, slot):
        value = field[slot, pl.ds(2, PLANES), pl.ds(PAD, SPAN)].reshape(PLANES * SPAN, LANES)
        high = value.astype(BF16)
        rest = (value - high.astype(F32)).astype(BF16)
        dims = (((1,), (0,)), ((), ()))
        main = lax.dot_general(
            jnp.concatenate([high, rest], axis=1), bands[pl.ds(0, 2 * LANES)], dims, preferred_element_type=F32
        )
        minor = lax.dot_general(high, bands[pl.ds(2 * LANES, LANES), pl.ds(0, LANES)], dims, preferred_element_type=F32)
        along_y[...] = (main[:, :LANES] + minor).reshape(PLANES, SPAN, LANES)
        halves[pl.ds(2, PLANES)] = main[:, LANES:].reshape(PLANES, SPAN, LANES)

    def laplace(field, slot, e):
        result = []
        at = 2 + 2 * e

        def own(k):
            return field[slot, at + k, pl.ds(PAD, SPAN)]

        other = {k: jnp.where(lower, halves[at + k], halves[at + k + 2]) for k in (-2, -1, 0, 1)}
        along_z = (
            ((own(1), other[-1]), (other[0], other[-2]), (other[1], own(-1)), (own(2), own(-2))),
            ((other[0], own(0)), (other[1], other[-1]), (own(2), other[-2]), (own(3), own(-1))),
        )
        for i in range(2):
            total = 2.0 * stencil_weights[0] * own(i) + along_y[at + i - 2]
            for k in range(1, 5):
                some = along_z[i][k - 1][0] + along_z[i][k - 1][1]
                some = some + field[slot, at + i, pl.ds(PAD + k, SPAN)]
                some = some + field[slot, at + i, pl.ds(PAD - k, SPAN)]
                total = total + stencil_weights[k] * some
            result.append(total)
        return result

    def residual(k, p):
        return summed_r[pl.ds(pl.multiple_of(p * SPAN, SPAN), SPAN), pl.ds(LANES * k, LANES)]

    def to_lam(p, carry):
        lams[0, p + 2, pl.ds(PAD, SPAN)] = residual(0, p)
        return carry

    lax.fori_loop(0, PLANES, to_lam, 0)

    def ckpt_wait(k, carry):
        origin = lax.rem(part + k, PARTS)
        ckpt_copy(0, part, origin).wait_recv()
        ckpt_copy(1, part, origin).wait_recv()
        return carry

    lax.fori_loop(1, PARTS, ckpt_wait, 0)

    def keep_lap(field, slot, which):
        prepare(field, slot)

        def one(e, carry):
            for i, value in enumerate(laplace(field, slot, e)):
                first_lap[which, 2 * e + i] = value
            return carry

        lax.fori_loop(0, PARTS, one, 0)

    keep_lap(fields, 0, 0)
    keep_lap(lams, 0, 1)

    for m in range(RING - 4, RING):
        ring_wait(m, 1, gp_send, gp_recv)
        ring_wait(m, -1, gm_send, gm_recv)

    small = iota((ROWS, LANES), 1)
    row16 = iota((ROWS, LANES), 0)

    def window_copy(to, origin):
        return pltpu.make_async_remote_copy(
            src_ref=windows.at[to],
            dst_ref=arrived.at[pl.ds(2 * lax.rem(origin, PARTS), 2), pl.ds(ROWS * lax.div(origin, PARTS), ROWS)],
            send_sem=w_send.at[to], recv_sem=w_recv.at[origin],
            device_id=device(to), device_id_type=MESH,
        )

    def spot(b):
        ox = offx[LOCAL * level + b]
        oy = offy[LOCAL * level + b]
        t = ox - ROWS * group + SPAN
        return lax.shift_right_logical(t, 6) - 1, t & 63, lax.shift_right_logical(oy, 7), oy & 127

    def cut(b, carry):
        block, rest, tile, at = spot(b)
        upper_rows = row16 >= rest
        q0 = jnp.maximum(block, 0)
        q1 = jnp.minimum(block + 1, near - 1)
        back = lax.rem(LANES - at, LANES)
        keep = small < LANES - at
        planes = []
        for plane in range(4):
            turned_tiles = []
            for k in range(3):
                t = jnp.minimum(tile + k, 3)
                mixed = jnp.where(upper_rows, gathered[q0, plane, t], gathered[q1, plane, t])
                turned_tiles.append(pltpu.roll(mixed, back, 1))
            planes.append([jnp.where(keep, turned_tiles[k], turned_tiles[k + 1]) for k in range(2)])
        for i in range(2):
            high = [pltpu.roll(v, 64, 1) for v in planes[2 + i]]
            for to in range(PARTS):
                windows[b * PARTS + to, i] = window(planes[i], high, to)
        for to in range(PARTS):
            @pl.when(b * PARTS + to != me)
            def _():
                window_copy(b * PARTS + to, me).start()
        return carry

    lax.fori_loop(0, LOCAL, cut, 0)
    arrived[pl.ds(2 * part, 2), pl.ds(ROWS * group, ROWS)] = windows[me]

    def window_wait(k, carry):
        window_copy(me, lax.rem(me + k, peers)).wait_recv()
        return carry

    lax.fori_loop(1, peers, window_wait, 0)

    turn = offx[shot] & 63

    def make_c2v(p, carry):
        arrived[p, pl.ds(SPAN, SPAN)] = arrived[p, pl.ds(0, SPAN)]
        speed = arrived[p, pl.ds(turn, SPAN)]
        speeds[p] = speed
        scaled = courant * speed
        c2v[p] = scaled * scaled
        return carry

    lax.fori_loop(0, PLANES, make_c2v, 0)

    flat = place[0]
    zc = lax.shift_right_logical(flat, 14)
    sy = (flat & 255) - (OWN * part - HALO)
    s_plane = lax.shift_right_logical(zc, 2) * 2 + (zc & 1)
    s_lane = jnp.where((sy >= 0) & (sy < 64), (lax.shift_right_logical(zc, 1) & 1) * 64 + sy, -1)
    at_source = (lane == s_lane) & (iota((SPAN, LANES), 0) == (lax.shift_right_logical(flat, 8) & 63))

    def accel_of(value, p, n):
        strength = jnp.where(p == s_plane, pulse[0, n], 0.0)
        return c2v[p] * value + jnp.where(at_source, strength, 0.0)

    inner = pl.ds(PAD, SPAN)

    for n in range(STEPS):
        now, old = n % 2, 1 - n % 2
        if n:
            prepare(fields, now)

        def forward(e, carry, n=n, now=now, old=old):
            laps = laplace(fields, now, e) if n else [first_lap[0, 2 * e + i] for i in range(2)]
            for i in range(2):
                p = 2 * e + i
                accel = accel_of(laps[i], p, n)
                accels[n, p] = accel
                if n < STEPS - 1:
                    fields[old, p + 2, inner] = (
                        2.0 * fields[now, p + 2, inner] - fields[old, p + 2, inner] + accel
                    )
            return carry

        lax.fori_loop(0, PARTS, forward, 0)

    def out_copy(to, origin):
        return pltpu.make_async_remote_copy(
            src_ref=outgoing.at[lax.rem(to, PARTS), pl.ds(ROWS * lax.div(to, PARTS), ROWS)],
            dst_ref=landed.at[origin],
            send_sem=o_send.at[to], recv_sem=o_recv.at[origin],
            device_id=device(to), device_id_type=MESH,
        )

    for k in range(1, STEPS):
        now, old, new = (k - 1) % 3, (k - 2) % 3, k % 3
        if k > 1:
            prepare(lams, now)

        def adjoint(e, carry, k=k, now=now, old=old, new=new):
            laps = laplace(lams, now, e) if k > 1 else [first_lap[1, 2 * e + i] for i in range(2)]
            parts = []
            for i in range(2):
                p = 2 * e + i
                lam = lams[now, p + 2, inner]
                newer = 2.0 * lam + c2v[p] * laps[i] + residual(k, p)
                if k > 1:
                    newer = newer - lams[old, p + 2, inner]
                    so_far = partial[p]
                else:
                    so_far = lam * accels[STEPS - 1, p]
                so_far = so_far + newer * accels[STEPS - 1 - k, p]
                if k < STEPS - 1:
                    lams[new, p + 2, inner] = newer
                    partial[p] = so_far
                else:
                    parts.append(so_far * 2.0 / speeds[p])
            if k == STEPS - 1:
                both = jnp.where(
                    (lane & 63) < OWN, pltpu.roll(parts[0], LANES - HALO, 1), pltpu.roll(parts[1], OWN - HALO, 1)
                )
                packed[e, pl.ds(0, SPAN)] = both
                packed[e, pl.ds(SPAN, SPAN)] = both
                outgoing[e] = packed[e, pl.ds((SPAN - turn) & 63, SPAN)]
                for b in range(LOCAL):
                    @pl.when(b * PARTS + e != me)
                    def _():
                        out_copy(b * PARTS + e, me).start()
            return carry

        lax.fori_loop(0, PARTS, adjoint, 0)

    landed[me] = outgoing[part, pl.ds(pl.multiple_of(ROWS * group, ROWS), ROWS)]

    def out_wait(k, carry):
        out_copy(me, lax.rem(me + k, peers)).wait_recv()
        return carry

    lax.fori_loop(1, peers, out_wait, 0)

    def put(b, carry):
        block, rest, tile, at = spot(b)
        group_of = lax.shift_right_logical(small, 5)
        keep = small >= at
        for plane in range(4):
            halves = []
            for k in range(2):
                total = None
                for c in range(4):
                    piece = landed[b * PARTS + 4 * k + c]
                    by = (OWN * (c - plane)) % LANES
                    if by:
                        piece = pltpu.roll(piece, by, 1)
                    total = piece if total is None else jnp.where(group_of == c, piece, total)
                halves.append(pltpu.roll(total, at, 1))
            placed[b, plane, 2] = jnp.where(keep, halves[0], 0.0)
            placed[b, plane, 3] = jnp.where(keep, halves[1], halves[0])
            placed[b, plane, 4] = jnp.where(keep, 0.0, halves[1])
        return carry

    lax.fori_loop(0, LOCAL, put, 0)

    spots = [spot(b) for b in range(LOCAL)]
    blocks = [jnp.where(iota((4, ROWS, LANES), 1) >= s[1], s[0], s[0] + 1) for s in spots]

    def add_up(plane, carry):
        cells = [
            placed[b, plane, pl.ds(2 - spots[b][2], 4)]
            for b in range(LOCAL)
        ]

        def one(q, carry):
            total = jnp.where(blocks[0] == q, cells[0], 0.0)
            for b in range(1, LOCAL):
                total = total + jnp.where(blocks[b] == q, cells[b], 0.0)
            totals[q, plane] = total
            return carry

        return lax.fori_loop(0, near, one, carry)

    lax.fori_loop(0, 4, add_up, 0)

    half = near // 2

    def sum_place(m, sign):
        pair = m // 2
        plane = (pair % 2 * 2 + m % 2 + (0 if sign > 0 else 2)) % 4
        return lax.rem(level + near + sign * (half - (pair + 1) // 2), near), plane

    def sum_copy(m, sign, ring, send, recv):
        to = up if sign > 0 else down
        return pltpu.make_async_remote_copy(
            src_ref=totals.at[sum_place(m, sign)], dst_ref=ring.at[m],
            send_sem=send.at[m], recv_sem=recv.at[m],
            device_id=(LOCAL * to + group, part), device_id_type=MESH,
        )

    ways = ((1, ring_p, rp_send, rp_recv), (-1, ring_m, rm_send, rm_recv))
    for m in range(RING):
        for sign, ring, send, recv in ways:
            if m >= 4:
                sum_copy(m - 4, sign, ring, send, recv).wait_recv()
                target, plane = sum_place(m, sign)
                totals[target, plane] = totals[target, plane] + ring[m - 4]
            sum_copy(m, sign, ring, send, recv).start()
    for m in range(RING - 4, RING):
        for sign, ring, send, recv in ways:
            sum_copy(m, sign, ring, send, recv).wait_recv()
    for plane in range(4):
        total = totals[level, plane]
        for sign, ring, send, recv in ways:
            for m in range(RING - 4, RING):
                if sum_place(m, sign)[1] == plane:
                    total = total + ring[m]
        speed = model[plane]
        total = jnp.concatenate([total[tile] for tile in range(4)], axis=-1)
        scaling = (speed - lower_bound) * (upper_bound - speed) / (upper_bound - lower_bound)
        limit = barrier_weight / (upper_bound - speed) - barrier_weight / (speed - lower_bound)
        out[plane] = scaling * (total + limit)

    for m in range(RING):
        ring_copy(m, 1, gp_send, gp_recv).wait_send()
        ring_copy(m, -1, gm_send, gm_recv).wait_send()
        for sign, ring, send, recv in ways:
            sum_copy(m, sign, ring, send, recv).wait_send()

    def ckpt_sent(k, carry):
        to = lax.rem(part + k, PARTS)
        ckpt_copy(0, to, part).wait_send()
        ckpt_copy(1, to, part).wait_send()
        return carry

    lax.fori_loop(1, PARTS, ckpt_sent, 0)

    def blocks_sent(k, carry):
        to = lax.rem(me + k, peers)
        window_copy(to, me).wait_send()
        out_copy(to, me).wait_send()
        return carry

    lax.fori_loop(1, peers, blocks_sent, 0)


def on_device(near, model, offsets_x, offsets_y, ckpt_prev, ckpt_cur, wavelet, source, receivers, traces):
    peers = LOCAL * PARTS
    vmem = pl.BlockSpec(memory_space=pltpu.VMEM)
    smem = pl.BlockSpec(memory_space=pltpu.SMEM)
    padded = (PLANES + 4, SPAN + 2 * PAD, LANES)
    plain = (PLANES, SPAN, LANES)
    dma = pltpu.SemaphoreType.DMA
    return pl.pallas_call(
        functools.partial(kernel, near),
        out_shape=jax.ShapeDtypeStruct(model.shape, F32),
        in_specs=[smem] * 4 + [pl.BlockSpec(memory_space=pltpu.HBM)] * 5,
        out_specs=vmem,
        scratch_shapes=[
            *(pltpu.VMEM(a.shape, a.dtype) for a in (model, ckpt_prev, ckpt_cur, receivers, traces)),
            pltpu.VMEM((near, 4, 4, ROWS, LANES), F32),
            pltpu.VMEM((2, PARTS, 2, SPAN, LANES), F32),
            pltpu.VMEM((2,) + padded, F32),
            pltpu.VMEM((3,) + padded, F32),
            pltpu.VMEM((3 * LANES, 2 * LANES), BF16),
            pltpu.VMEM(plain, F32),
            pltpu.VMEM((PLANES + 4, SPAN, LANES), F32),
            pltpu.VMEM((STEPS * LANES, 2 * CHUNK), BF16),
            pltpu.VMEM((PLANES * SPAN, STEPS * LANES), F32),
            pltpu.VMEM((peers, 2, ROWS, LANES), F32),
            pltpu.VMEM((PLANES, 2 * SPAN, LANES), F32),
            pltpu.VMEM(plain, F32),
            pltpu.VMEM(plain, F32),
            pltpu.VMEM((2,) + plain, F32),
            pltpu.VMEM((STEPS,) + plain, F32),
            pltpu.VMEM(plain, F32),
            pltpu.VMEM((PARTS, 2 * SPAN, LANES), F32),
            pltpu.VMEM((PARTS, SPAN, LANES), F32),
            pltpu.VMEM((peers, ROWS, LANES), F32),
            pltpu.VMEM((LOCAL, 4, 6, ROWS, LANES), F32),
            pltpu.VMEM((near, 4, 4, ROWS, LANES), F32),
            pltpu.VMEM((RING, 4, ROWS, LANES), F32),
            pltpu.VMEM((RING, 4, ROWS, LANES), F32),
            dma((5,)),
            dma((RING,)), dma((RING,)), dma((RING,)), dma((RING,)),
            dma((2, PARTS)), dma((2, PARTS)),
            dma((peers,)), dma((peers,)), dma((peers,)), dma((peers,)),
            dma((RING,)), dma((RING,)), dma((RING,)), dma((RING,)),
        ],
        compiler_params=pltpu.CompilerParams(
            collective_id=0, has_side_effects=True, vmem_limit_bytes=48 * 1024 * 1024
        ),
    )(offsets_x, offsets_y, wavelet, source, model, ckpt_prev, ckpt_cur, receivers, traces)


def solution(mesh):
    placed = (
        P("depth", "shots", None),
        P(),
        P(),
        P("shots", "depth", None, None),
        P("shots", "depth", None, None),
        P("shots", None),
        P("shots"),
        P("shots", None),
        P("shots", None, None),
    )
    near = mesh.shape["shots"] // LOCAL
    return jax.shard_map(
        functools.partial(on_device, near),
        mesh=mesh, in_specs=placed, out_specs=P("depth", "shots", None), check_vma=False,
    )
```

```python
import functools

import jax
import jax.numpy as jnp
import numpy as np
from jax import lax
from jax.experimental import pallas as pl
from jax.experimental.pallas import tpu as pltpu
from jax.sharding import PartitionSpec as P

MESH = pl.DeviceIdType.MESH
F32 = jnp.float32
BF16 = jnp.bfloat16
STEPS = 4

stencil_weights = (-205.0 / 72.0, 8.0 / 5.0, -1.0 / 5.0, 8.0 / 315.0, -1.0 / 560.0)
courant = 0.095
lower_bound = 1.0
upper_bound = 5.0
barrier_weight = 0.5

PARTS = 8
LOCAL = 4
PLANES = 16
SPAN = 64
LANES = 128
ROWS = 16
HALO = 16
OWN = 32
CHUNK = 256
PAD = 8
FAR_FIRST = (4, 3, 5, 2, 6, 1, 7)
FIRST = 7


def iota(shape, dim):
    return lax.broadcasted_iota(jnp.int32, shape, dim)


def window(first, second, part):
    rows = first[0].shape[0]
    lane = iota((rows, LANES), 1)
    zero = jnp.zeros((rows, LANES), F32)
    start = OWN * part - HALO
    tile, at = start // LANES, start % LANES

    def pick(tiles, k):
        return tiles[k] if 0 <= k < 2 else zero

    if at <= 64:
        low = pick(first, tile)
        in_low = (lane >= at) & (lane < at + 64)
        high = pick(second, tile)
    else:
        low = jnp.where(lane >= at, pick(first, tile), pick(first, tile + 1))
        in_low = (lane >= at) | (lane < at - 64)
        own = (lane + 64) % LANES
        high = jnp.where(own >= at, pick(second, tile), pick(second, tile + 1))
    both = jnp.where(in_low, low, high)
    return pltpu.roll(both, (LANES - at) % LANES, 1) if at else both


def make_bands(bands):
    r, c = iota((LANES, LANES), 0), iota((LANES, LANES), 1)
    distance = jnp.where((r < 64) == (c < 64), jnp.abs(r - c), LANES)
    main = jnp.zeros((LANES, LANES), F32)
    rest = main
    for k, weight in enumerate(stencil_weights):
        rounded = float(np.float32(weight).astype(BF16))
        main = jnp.where(distance == k, rounded, main)
        rest = jnp.where(distance == k, float(np.float32(weight)) - rounded, rest)
    swap = (jnp.abs(r - c) == 64).astype(F32).astype(BF16)
    for half in range(2):
        bands[pl.ds(LANES * half, LANES), pl.ds(0, LANES)] = main.astype(BF16)
        bands[pl.ds(LANES * half, LANES), pl.ds(LANES, LANES)] = swap
    bands[pl.ds(2 * LANES, LANES), pl.ds(0, LANES)] = rest.astype(BF16)
    bands[pl.ds(2 * LANES, LANES), pl.ds(LANES, LANES)] = jnp.zeros((LANES, LANES), BF16)


def kernel(
    near,
    offx, offy, pulse, place, model_in, prev_in, cur_in, listing_in, record_in,
    out,
    model, prev, cur, listing, record,
    m_out, cyclic, rows_out, rows_in, rows_16, stage, fields, lams, bands, along_y, halves, onto, summed_r, windows, arrived, speeds, c2v, first_lap,
    accels, partial, packed, outgoing, z_out, z_in, outgoing_2, landed, by_shot, placed, totals, sums, final,
    in_sems,
    m_send, m_recv, r_send, r_recv, ck_send, ck_recv, w_send, w_recv, o_send, o_recv,
    z_send, z_recv, s_send, s_recv,
):
    shot = lax.axis_index("shots")
    part = lax.axis_index("depth")
    level = lax.div(shot, LOCAL)
    group = lax.rem(shot, LOCAL)
    me = group * PARTS + part
    peers = LOCAL * PARTS
    lane = iota((SPAN, LANES), 1)
    lower = lane < 64

    def along(step):
        return lax.rem(level + step, near)

    def device(k):
        return (LOCAL * level + lax.div(k, PARTS), lax.rem(k, PARTS))

    inputs = [
        pltpu.make_async_copy(model_in, model, in_sems.at[0]),
        pltpu.make_async_copy(cur_in, cur, in_sems.at[1]),
        pltpu.make_async_copy(prev_in, prev, in_sems.at[2]),
        pltpu.make_async_copy(listing_in, listing, in_sems.at[3]),
        pltpu.make_async_copy(record_in, record, in_sems.at[4]),
    ]
    for copy in inputs:
        copy.start()

    barrier = pltpu.get_barrier_semaphore()

    def greet(k, carry):
        pl.semaphore_signal(barrier, inc=1, device_id=device(lax.rem(me + k, peers)), device_id_type=MESH)
        return carry

    for step in FAR_FIRST:
        pl.semaphore_signal(barrier, inc=1, device_id=(LOCAL * along(step) + group, part), device_id_type=MESH)
    lax.fori_loop(1, peers, greet, 0)

    make_bands(bands)
    inputs[0].wait()
    for to in range(near):
        for tile in range(4):
            for plane in range(4):
                m_out[to, tile, pl.ds(2 * plane, 2)] = model[plane, pl.ds(2 * to, 2), pl.ds(LANES * tile, LANES)]
    for which, source in ((0, cur), (1, prev)):
        inputs[1 + which].wait()
        for i in range(2):
            low = [source[0, i, :, pl.ds(LANES * k, LANES)] for k in range(2)]
            high = [pltpu.roll(source[0, 2 + i, :, pl.ds(LANES * k, LANES)], 64, 1) for k in range(2)]
            for to in range(PARTS):
                stage[which, to, i] = window(low, high, to)

    pl.semaphore_wait(barrier, peers - 1 + len(FAR_FIRST))

    def model_copy(to, origin):
        return pltpu.make_async_remote_copy(
            src_ref=m_out.at[to], dst_ref=cyclic.at[origin],
            send_sem=m_send.at[to], recv_sem=m_recv.at[origin],
            device_id=(LOCAL * to + group, part), device_id_type=MESH,
        )

    def rows_copy(to, origin):
        return pltpu.make_async_remote_copy(
            src_ref=rows_out.at[to], dst_ref=rows_in.at[pl.ds(SPAN * origin, SPAN)],
            send_sem=r_send.at[to], recv_sem=r_recv.at[origin],
            device_id=(LOCAL * to + group, part), device_id_type=MESH,
        )

    def ckpt_copy(which, to, origin):
        return pltpu.make_async_remote_copy(
            src_ref=stage.at[which, to],
            dst_ref=fields.at[which, pl.ds(2 + 2 * origin, 2), pl.ds(PAD, SPAN)],
            send_sem=ck_send.at[which, to], recv_sem=ck_recv.at[which, origin],
            device_id=(shot, to), device_id_type=MESH,
        )

    for step in FAR_FIRST:
        model_copy(along(step), level).start()
    cyclic[level] = m_out[level]

    def ckpt_start(k, carry):
        to = lax.rem(part + k, PARTS)
        ckpt_copy(0, to, part).start()
        ckpt_copy(1, to, part).start()
        return carry

    lax.fori_loop(1, PARTS, ckpt_start, 0)

    for edge in (0, 1, PLANES + 2, PLANES + 3):
        for which in range(2):
            halves[which, edge] = jnp.zeros((SPAN, LANES), F32)
    for ref, slots in ((fields, 2), (lams, 3)):
        for slot in range(slots):
            for edge in (0, 1, PLANES + 2, PLANES + 3):
                ref[slot, edge] = jnp.zeros((SPAN + 2 * PAD, LANES), F32)
            for edge in range(2, PLANES + 2):
                ref[slot, edge, pl.ds(0, PAD)] = jnp.zeros((PAD, LANES), F32)
                ref[slot, edge, pl.ds(PAD + SPAN, PAD)] = jnp.zeros((PAD, LANES), F32)
    for which in range(2):
        fields[which, pl.ds(2 + 2 * part, 2), pl.ds(PAD, SPAN)] = stage[which, part]
    for tile in (0, 1, 5):
        placed[:, tile] = jnp.zeros((LOCAL * near, 8, LANES), F32)

    summed_r[...] = jnp.zeros(summed_r.shape, F32)

    def receivers(step):
        at = pl.ds(pl.multiple_of(step * CHUNK, CHUNK), CHUNK)
        flat = listing[:, at]
        zc = lax.shift_right_logical(flat, 14)
        x = lax.shift_right_logical(flat, 8) & 63
        y = (flat & 255) - (OWN * part - HALO)
        row = (lax.shift_right_logical(zc, 2) * 2 + (zc & 1)) * SPAN + x
        column = jnp.where((y >= 0) & (y < 64), (lax.shift_right_logical(zc, 1) & 1) * 64 + y, -1)
        hot = (iota((PLANES * SPAN, CHUNK), 0) == row).astype(F32).astype(BF16)
        match = iota((LANES, CHUNK), 0) == column
        for k in range(STEPS):
            value = record[0, pl.ds(k, 1), at]
            high = value.astype(BF16).astype(F32)
            rest = value - high
            onto[pl.ds(LANES * k, LANES), pl.ds(0, CHUNK)] = jnp.where(match, high, 0.0).astype(BF16)
            onto[pl.ds(LANES * k, LANES), pl.ds(CHUNK, CHUNK)] = jnp.where(match, rest, 0.0).astype(BF16)
        dims = (((1,), (1,)), ((), ()))
        both = jnp.concatenate([hot, hot], axis=1)
        summed_r[...] += lax.dot_general(both, onto[...], dims, preferred_element_type=F32)

    def more(step, carry):
        receivers(step)
        return carry

    inputs[3].wait()
    inputs[4].wait()
    lax.fori_loop(0, FIRST, more, 0)

    for step in FAR_FIRST:
        model_copy(level, along(step)).wait_recv()

    tile_lane = iota((8, LANES), 1)
    odd = iota((8, LANES), 0) & 1

    def spot(shot_k):
        t = offx[shot_k] - (ROWS * group + 2 * level) + SPAN
        oy = offy[shot_k]
        return lax.shift_right_logical(t, 6) - 1, t & 63, lax.shift_right_logical(oy, 7), oy & 127

    def cut(step, carry):
        to = lax.rem(level + near + lax.div(near - step, 2) * (1 - 2 * lax.rem(step, 2)), near)
        for b in range(LOCAL):
            block, rest, tile, at = spot(LOCAL * to + b)
            upper_rows = odd >= rest
            q0, q1 = jnp.maximum(block, 0), jnp.minimum(block + 1, near - 1)
            back = lax.rem(LANES - at, LANES)
            keep = tile_lane < LANES - at
            turned = []
            for k in range(3):
                t = jnp.minimum(tile + k, 3)
                turned.append(pltpu.roll(jnp.where(upper_rows, cyclic[q0, t], cyclic[q1, t]), back, 1))
            for k in range(2):
                rows_out[to, pl.ds(8 * (2 * b + k), 8)] = jnp.where(keep, turned[k], turned[k + 1])
        @pl.when(to != level)
        def _():
            rows_copy(to, level).start()
        return carry

    lax.fori_loop(0, near, cut, 0)
    rows_in[pl.ds(pl.multiple_of(SPAN * level, SPAN), SPAN)] = rows_out[level]
    lax.fori_loop(FIRST, listing.shape[1] // CHUNK, more, 0)
    for step in FAR_FIRST:
        rows_copy(level, along(step)).wait_recv()

    def window_copy(to, origin):
        return pltpu.make_async_remote_copy(
            src_ref=windows.at[to],
            dst_ref=arrived.at[pl.ds(2 * lax.rem(origin, PARTS), 2), pl.ds(ROWS * lax.div(origin, PARTS), ROWS)],
            send_sem=w_send.at[to], recv_sem=w_recv.at[origin],
            device_id=device(to), device_id_type=MESH,
        )

    def share(b, carry):
        for plane in range(4):
            for k in range(2):
                for j in range(2):
                    rows_16[plane, k, pl.ds(j, 8, stride=2)] = (
                        rows_in[pl.ds(8 * (2 * b + k) + 2 * plane + j, 8, stride=SPAN)]
                    )
        for i in range(2):
            low = [rows_16[i, k] for k in range(2)]
            high = [pltpu.roll(rows_16[2 + i, k], 64, 1) for k in range(2)]
            for to in range(PARTS):
                windows[b * PARTS + to, i] = window(low, high, to)
        for to in range(PARTS):
            @pl.when(b * PARTS + to != me)
            def _():
                window_copy(b * PARTS + to, me).start()
        return carry

    lax.fori_loop(0, LOCAL, share, 0)
    arrived[pl.ds(2 * part, 2), pl.ds(ROWS * group, ROWS)] = windows[me]

    def prepare(field, slot, which):
        value = field[slot, pl.ds(2, PLANES), pl.ds(PAD, SPAN)].reshape(PLANES * SPAN, LANES)
        high = value.astype(BF16)
        rest = (value - high.astype(F32)).astype(BF16)
        dims = (((1,), (0,)), ((), ()))
        main = lax.dot_general(
            jnp.concatenate([high, rest], axis=1), bands[pl.ds(0, 2 * LANES)], dims, preferred_element_type=F32
        )
        minor = lax.dot_general(high, bands[pl.ds(2 * LANES, LANES), pl.ds(0, LANES)], dims, preferred_element_type=F32)
        along_y[which] = (main[:, :LANES] + minor).reshape(PLANES, SPAN, LANES)
        halves[which, pl.ds(2, PLANES)] = main[:, LANES:].reshape(PLANES, SPAN, LANES)

    def laplace(field, slot, which, e):
        result = []
        at = 2 + 2 * e

        def own(k):
            return field[slot, at + k, pl.ds(PAD, SPAN)]

        other = {k: jnp.where(lower, halves[which, at + k], halves[which, at + k + 2]) for k in (-2, -1, 0, 1)}
        along_z = (
            ((own(1), other[-1]), (other[0], other[-2]), (other[1], own(-1)), (own(2), own(-2))),
            ((other[0], own(0)), (other[1], other[-1]), (own(2), other[-2]), (own(3), own(-1))),
        )
        for i in range(2):
            total = 2.0 * stencil_weights[0] * own(i) + along_y[which, at + i - 2]
            for k in range(1, 5):
                some = along_z[i][k - 1][0] + along_z[i][k - 1][1]
                some = some + field[slot, at + i, pl.ds(PAD + k, SPAN)]
                some = some + field[slot, at + i, pl.ds(PAD - k, SPAN)]
                total = total + stencil_weights[k] * some
            result.append(total)
        return result

    def residual(k, p):
        return summed_r[pl.ds(pl.multiple_of(p * SPAN, SPAN), SPAN), pl.ds(LANES * k, LANES)]

    def to_lam(p, carry):
        lams[0, p + 2, pl.ds(PAD, SPAN)] = residual(0, p)
        return carry

    lax.fori_loop(0, PLANES, to_lam, 0)

    def ckpt_wait(k, carry):
        origin = lax.rem(part + k, PARTS)
        ckpt_copy(0, part, origin).wait_recv()
        ckpt_copy(1, part, origin).wait_recv()
        return carry

    lax.fori_loop(1, PARTS, ckpt_wait, 0)

    prepare(fields, 0, 0)
    prepare(lams, 0, 1)

    def first(e, carry):
        for which, field in ((0, fields), (1, lams)):
            for i, value in enumerate(laplace(field, 0, which, e)):
                first_lap[which, 2 * e + i] = value
        return carry

    lax.fori_loop(0, PARTS, first, 0)

    def window_wait(k, carry):
        window_copy(me, lax.rem(me + k, peers)).wait_recv()
        return carry

    lax.fori_loop(1, peers, window_wait, 0)

    turn = offx[shot] & 63

    def make_c2v(p, carry):
        arrived[p, pl.ds(SPAN, SPAN)] = arrived[p, pl.ds(0, SPAN)]
        speed = arrived[p, pl.ds(turn, SPAN)]
        speeds[p] = speed
        scaled = courant * speed
        c2v[p] = scaled * scaled
        return carry

    lax.fori_loop(0, PLANES, make_c2v, 0)

    flat = place[0]
    zc = lax.shift_right_logical(flat, 14)
    sy = (flat & 255) - (OWN * part - HALO)
    s_plane = lax.shift_right_logical(zc, 2) * 2 + (zc & 1)
    s_lane = jnp.where((sy >= 0) & (sy < 64), (lax.shift_right_logical(zc, 1) & 1) * 64 + sy, -1)
    at_source = (lane == s_lane) & (iota((SPAN, LANES), 0) == (lax.shift_right_logical(flat, 8) & 63))

    def accel_of(value, p, n):
        strength = jnp.where(p == s_plane, pulse[0, n], 0.0)
        return c2v[p] * value + jnp.where(at_source, strength, 0.0)

    inner = pl.ds(PAD, SPAN)

    def step_loop(n):
        now, old = n % 2, 1 - n % 2
        if n:
            prepare(fields, now, 0)
            if n < STEPS - 1:
                prepare(lams, n, 1)

        def step(e, carry):
            laps = laplace(fields, now, 0, e) if n else [first_lap[0, 2 * e + i] for i in range(2)]
            accel = [accel_of(laps[i], 2 * e + i, n) for i in range(2)]
            if n < STEPS - 1:
                laps = laplace(lams, n, 1, e) if n else [first_lap[1, 2 * e + i] for i in range(2)]
            for i in range(2):
                p = 2 * e + i
                if n < STEPS - 1:
                    fields[old, p + 2, inner] = (
                        2.0 * fields[now, p + 2, inner] - fields[old, p + 2, inner] + accel[i]
                    )
                    lam = lams[n, p + 2, inner]
                    newer = 2.0 * lam + c2v[p] * laps[i] + residual(n + 1, p)
                    if n:
                        newer = newer - lams[n - 1, p + 2, inner]
                if n < STEPS - 2:
                    accels[n, p] = accel[i]
                    lams[n + 1, p + 2, inner] = newer
                elif n == STEPS - 2:
                    partial[p] = newer * accels[0, p] + lam * accels[1, p] + lams[1, p + 2, inner] * accel[i]
            if n == STEPS - 1:
                send_parts(e, [
                    (partial[2 * e + i] + lams[0, 2 * e + i + 2, inner] * accel[i]) * 2.0 / speeds[2 * e + i]
                    for i in range(2)
                ])
            return carry

        lax.fori_loop(0, PARTS, step, 0)

    def send_parts(e, parts):
        both = jnp.where((lane & 63) < OWN, pltpu.roll(parts[0], LANES - HALO, 1), pltpu.roll(parts[1], OWN - HALO, 1))
        packed[e, pl.ds(0, SPAN)] = both
        packed[e, pl.ds(SPAN, SPAN)] = both
        outgoing[e] = packed[e, pl.ds((SPAN - turn) & 63, SPAN)]
        for to in range(near):
            for j in range(2):
                z_out[to, pl.ds(8 * e + 4 * j, 4)] = outgoing[e, pl.ds(2 * to + j, 4, stride=ROWS)]

    for n in range(STEPS):
        step_loop(n)

    def z_copy(to, origin):
        return pltpu.make_async_remote_copy(
            src_ref=z_out.at[to], dst_ref=z_in.at[pl.ds(SPAN * origin, SPAN)],
            send_sem=z_send.at[to], recv_sem=z_recv.at[origin],
            device_id=(LOCAL * to + group, part), device_id_type=MESH,
        )

    for step in FAR_FIRST:
        z_copy(along(step), level).start()
    z_in[pl.ds(pl.multiple_of(SPAN * level, SPAN), SPAN)] = z_out[level]
    for step in FAR_FIRST:
        z_copy(level, along(step)).wait_recv()

    def out_copy(to, origin):
        return pltpu.make_async_remote_copy(
            src_ref=outgoing_2.at[to], dst_ref=landed.at[origin],
            send_sem=o_send.at[to], recv_sem=o_recv.at[origin],
            device_id=device(to), device_id_type=MESH,
        )

    def out_start(e, carry):
        for b in range(LOCAL):
            for j in range(2):
                outgoing_2[b * PARTS + e, pl.ds(8 * j, 8)] = z_in[pl.ds(8 * e + 4 * j + b, 8, stride=SPAN)]
            @pl.when(b * PARTS + e != me)
            def _():
                out_copy(b * PARTS + e, me).start()
        return carry

    lax.fori_loop(0, PARTS, out_start, 0)
    landed[me] = outgoing_2[me]

    def out_wait(k, carry):
        out_copy(me, lax.rem(me + k, peers)).wait_recv()
        return carry

    lax.fori_loop(1, peers, out_wait, 0)

    group_of = lax.shift_right_logical(tile_lane, 5)

    def put(b, carry):
        for j in range(2):
            for k in range(2):
                pieces = [landed[b * PARTS + 4 * k + c, pl.ds(8 * j, 8)] for c in range(4)]
                for plane in range(4):
                    total = None
                    for c in range(4):
                        by = (OWN * (c - plane)) % LANES
                        piece = pltpu.roll(pieces[c], by, 1) if by else pieces[c]
                        total = piece if total is None else jnp.where(group_of == c, piece, total)
                    by_shot[k, pl.ds(8 * (2 * plane + j), 8)] = total
        for z in range(near):
            at = offy[LOCAL * z + b] & 127
            keep = tile_lane >= at
            first, second = (pltpu.roll(by_shot[k, pl.ds(z, 8, stride=8)], at, 1) for k in range(2))
            placed[b * near + z, 2] = jnp.where(keep, first, 0.0)
            placed[b * near + z, 3] = jnp.where(keep, second, first)
            placed[b * near + z, 4] = jnp.where(keep, 0.0, second)
        return carry

    lax.fori_loop(0, LOCAL, put, 0)

    def add_up(k, sums):
        block, rest, tile, _ = spot(LOCAL * lax.rem(k, near) + lax.div(k, near))
        block = jnp.where(odd >= rest, block, block + 1)
        cells = placed[k, pl.ds(2 - tile, 4)]
        return tuple(total + jnp.where(block == q, cells, 0.0) for q, total in enumerate(sums))

    zero = jnp.zeros((4, 8, LANES), F32)
    for q, total in enumerate(lax.fori_loop(0, LOCAL * near, add_up, (zero,) * near)):
        totals[q] = total

    def sum_copy(to, origin):
        return pltpu.make_async_remote_copy(
            src_ref=totals.at[to], dst_ref=sums.at[origin],
            send_sem=s_send.at[to], recv_sem=s_recv.at[origin],
            device_id=(LOCAL * to + group, part), device_id_type=MESH,
        )

    for step in FAR_FIRST:
        sum_copy(along(step), level).start()
    sums[level] = totals[level]
    for step in FAR_FIRST:
        sum_copy(level, along(step)).wait_recv()
    for plane in range(4):
        for tile in range(4):
            for j in range(2):
                for z in range(near):
                    final[plane, tile, pl.ds(2 * z + j, 1)] = sums[z, tile, pl.ds(2 * plane + j, 1)]
        speed = model[plane]
        total = jnp.concatenate([final[plane, tile] for tile in range(4)], axis=-1)
        scaling = (speed - lower_bound) * (upper_bound - speed) / (upper_bound - lower_bound)
        limit = barrier_weight / (upper_bound - speed) - barrier_weight / (speed - lower_bound)
        out[plane] = scaling * (total + limit)

    for step in FAR_FIRST:
        model_copy(along(step), level).wait_send()
        rows_copy(along(step), level).wait_send()
        z_copy(along(step), level).wait_send()
        sum_copy(along(step), level).wait_send()

    def ckpt_sent(k, carry):
        to = lax.rem(part + k, PARTS)
        ckpt_copy(0, to, part).wait_send()
        ckpt_copy(1, to, part).wait_send()
        return carry

    lax.fori_loop(1, PARTS, ckpt_sent, 0)

    def blocks_sent(k, carry):
        to = lax.rem(me + k, peers)
        window_copy(to, me).wait_send()
        out_copy(to, me).wait_send()
        return carry

    lax.fori_loop(1, peers, blocks_sent, 0)


def on_device(near, model, offsets_x, offsets_y, ckpt_prev, ckpt_cur, wavelet, source, receivers, traces):
    peers = LOCAL * PARTS
    vmem = pl.BlockSpec(memory_space=pltpu.VMEM)
    smem = pl.BlockSpec(memory_space=pltpu.SMEM)
    padded = (PLANES + 4, SPAN + 2 * PAD, LANES)
    plain = (PLANES, SPAN, LANES)
    dma = pltpu.SemaphoreType.DMA
    return pl.pallas_call(
        functools.partial(kernel, near),
        out_shape=jax.ShapeDtypeStruct(model.shape, F32),
        in_specs=[smem] * 4 + [pl.BlockSpec(memory_space=pltpu.HBM)] * 5,
        out_specs=vmem,
        scratch_shapes=[
            *(pltpu.VMEM(a.shape, a.dtype) for a in (model, ckpt_prev, ckpt_cur, receivers, traces)),
            pltpu.VMEM((near, 4, 8, LANES), F32),
            pltpu.VMEM((near, 4, 8, LANES), F32),
            pltpu.VMEM((near, SPAN, LANES), F32),
            pltpu.VMEM((near * SPAN, LANES), F32),
            pltpu.VMEM((4, 2, ROWS, LANES), F32),
            pltpu.VMEM((2, PARTS, 2, SPAN, LANES), F32),
            pltpu.VMEM((2,) + padded, F32),
            pltpu.VMEM((3,) + padded, F32),
            pltpu.VMEM((3 * LANES, 2 * LANES), BF16),
            pltpu.VMEM((2,) + plain, F32),
            pltpu.VMEM((2, PLANES + 4, SPAN, LANES), F32),
            pltpu.VMEM((STEPS * LANES, 2 * CHUNK), BF16),
            pltpu.VMEM((PLANES * SPAN, STEPS * LANES), F32),
            pltpu.VMEM((peers, 2, ROWS, LANES), F32),
            pltpu.VMEM((PLANES, 2 * SPAN, LANES), F32),
            pltpu.VMEM(plain, F32),
            pltpu.VMEM(plain, F32),
            pltpu.VMEM((2,) + plain, F32),
            pltpu.VMEM((2,) + plain, F32),
            pltpu.VMEM(plain, F32),
            pltpu.VMEM((PARTS, 2 * SPAN, LANES), F32),
            pltpu.VMEM((PARTS, SPAN, LANES), F32),
            pltpu.VMEM((near, SPAN, LANES), F32),
            pltpu.VMEM((near * SPAN, LANES), F32),
            pltpu.VMEM((peers, ROWS, LANES), F32),
            pltpu.VMEM((peers, ROWS, LANES), F32),
            pltpu.VMEM((2, SPAN, LANES), F32),
            pltpu.VMEM((LOCAL * near, 6, 8, LANES), F32),
            pltpu.VMEM((near, 4, 8, LANES), F32),
            pltpu.VMEM((near, 4, 8, LANES), F32),
            pltpu.VMEM((4, 4, ROWS, LANES), F32),
            dma((5,)),
            dma((near,)), dma((near,)), dma((near,)), dma((near,)),
            dma((2, PARTS)), dma((2, PARTS)),
            dma((peers,)), dma((peers,)), dma((peers,)), dma((peers,)),
            dma((near,)), dma((near,)), dma((near,)), dma((near,)),
        ],
        compiler_params=pltpu.CompilerParams(
            collective_id=0, has_side_effects=True, vmem_limit_bytes=62 * 1024 * 1024
        ),
    )(offsets_x, offsets_y, wavelet, source, model, ckpt_prev, ckpt_cur, receivers, traces)


def solution(mesh):
    placed = (
        P("depth", "shots", None),
        P(),
        P(),
        P("shots", "depth", None, None),
        P("shots", "depth", None, None),
        P("shots", None),
        P("shots"),
        P("shots", None),
        P("shots", None, None),
    )
    near = mesh.shape["shots"] // LOCAL
    return jax.shard_map(
        functools.partial(on_device, near),
        mesh=mesh, in_specs=placed, out_specs=P("depth", "shots", None), check_vma=False,
    )
```

```python
import functools

import jax
import jax.numpy as jnp
import numpy as np
from jax import lax
from jax.experimental import pallas as pl
from jax.experimental.pallas import tpu as pltpu
from jax.sharding import PartitionSpec as P

MESH = pl.DeviceIdType.MESH
F32 = jnp.float32
BF16 = jnp.bfloat16
STEPS = 4

stencil_weights = (-205.0 / 72.0, 8.0 / 5.0, -1.0 / 5.0, 8.0 / 315.0, -1.0 / 560.0)
courant = 0.095
lower_bound = 1.0
upper_bound = 5.0
barrier_weight = 0.5

PARTS = 8
LOCAL = 4
PLANES = 16
SPAN = 64
LANES = 128
ROWS = 16
HALO = 16
OWN = 32
CHUNK = 256
PAD = 8
FAR_FIRST = (4, 3, 5, 2, 6, 1, 7)
FIRST = 4
SECOND = 8


def iota(shape, dim):
    return lax.broadcasted_iota(jnp.int32, shape, dim)


def window(first, second, part):
    rows = first[0].shape[0]
    lane = iota((rows, LANES), 1)
    zero = jnp.zeros((rows, LANES), F32)
    start = OWN * part - HALO
    tile, at = start // LANES, start % LANES

    def pick(tiles, k):
        return tiles[k] if 0 <= k < 2 else zero

    if at <= 64:
        low = pick(first, tile)
        in_low = (lane >= at) & (lane < at + 64)
        high = pick(second, tile)
    else:
        low = jnp.where(lane >= at, pick(first, tile), pick(first, tile + 1))
        in_low = (lane >= at) | (lane < at - 64)
        own = (lane + 64) % LANES
        high = jnp.where(own >= at, pick(second, tile), pick(second, tile + 1))
    both = jnp.where(in_low, low, high)
    return pltpu.roll(both, (LANES - at) % LANES, 1) if at else both


def make_bands(bands):
    r, c = iota((LANES, LANES), 0), iota((LANES, LANES), 1)
    distance = jnp.where((r < 64) == (c < 64), jnp.abs(r - c), LANES)
    main = jnp.zeros((LANES, LANES), F32)
    rest = main
    for k, weight in enumerate(stencil_weights):
        rounded = float(np.float32(weight).astype(BF16))
        main = jnp.where(distance == k, rounded, main)
        rest = jnp.where(distance == k, float(np.float32(weight)) - rounded, rest)
    swap = (jnp.abs(r - c) == 64).astype(F32).astype(BF16)
    for half in range(2):
        bands[pl.ds(LANES * half, LANES), pl.ds(0, LANES)] = main.astype(BF16)
        bands[pl.ds(LANES * half, LANES), pl.ds(LANES, LANES)] = swap
    bands[pl.ds(2 * LANES, LANES), pl.ds(0, LANES)] = rest.astype(BF16)
    bands[pl.ds(2 * LANES, LANES), pl.ds(LANES, LANES)] = jnp.zeros((LANES, LANES), BF16)


def kernel(
    near,
    offx, offy, pulse, place, model_in, prev_in, cur_in, listing_in, record_in,
    out,
    model, prev, cur, listing, record,
    m_out, cyclic, rows_out, rows_in, rows_16, stage, fields, lams, bands, along_y, halves, onto, summed_r, windows, arrived, speeds, c2v, first_lap,
    accels, partial, packed, outgoing, z_out, z_in, outgoing_2, landed, by_shot, placed, totals, sums, final,
    in_sems,
    m_send, m_recv, r_send, r_recv, ck_send, ck_recv, w_send, w_recv, o_send, o_recv,
    z_send, z_recv, s_send, s_recv,
):
    shot = lax.axis_index("shots")
    part = lax.axis_index("depth")
    level = lax.div(shot, LOCAL)
    group = lax.rem(shot, LOCAL)
    me = group * PARTS + part
    peers = LOCAL * PARTS
    lane = iota((SPAN, LANES), 1)
    lower = lane < 64

    def along(step):
        return lax.rem(level + step, near)

    def device(k):
        return (LOCAL * level + lax.div(k, PARTS), lax.rem(k, PARTS))

    inputs = [
        pltpu.make_async_copy(model_in, model, in_sems.at[0]),
        pltpu.make_async_copy(cur_in, cur, in_sems.at[1]),
        pltpu.make_async_copy(prev_in, prev, in_sems.at[2]),
        pltpu.make_async_copy(listing_in, listing, in_sems.at[3]),
        pltpu.make_async_copy(record_in, record, in_sems.at[4]),
    ]
    for copy in inputs:
        copy.start()

    barrier = pltpu.get_barrier_semaphore()

    def greet(k, carry):
        pl.semaphore_signal(barrier, inc=1, device_id=device(lax.rem(me + k, peers)), device_id_type=MESH)
        return carry

    for step in FAR_FIRST:
        pl.semaphore_signal(barrier, inc=1, device_id=(LOCAL * along(step) + group, part), device_id_type=MESH)
    lax.fori_loop(1, peers, greet, 0)

    make_bands(bands)
    inputs[0].wait()
    for to in range(near):
        for tile in range(4):
            for plane in range(4):
                m_out[to, tile, pl.ds(2 * plane, 2)] = model[plane, pl.ds(2 * to, 2), pl.ds(LANES * tile, LANES)]
    for which, source in ((0, cur), (1, prev)):
        inputs[1 + which].wait()
        for i in range(2):
            low = [source[0, i, :, pl.ds(LANES * k, LANES)] for k in range(2)]
            high = [pltpu.roll(source[0, 2 + i, :, pl.ds(LANES * k, LANES)], 64, 1) for k in range(2)]
            for to in range(PARTS):
                stage[which, to, i] = window(low, high, to)

    pl.semaphore_wait(barrier, peers - 1 + len(FAR_FIRST))

    def model_copy(to, origin):
        return pltpu.make_async_remote_copy(
            src_ref=m_out.at[to], dst_ref=cyclic.at[origin],
            send_sem=m_send.at[to], recv_sem=m_recv.at[origin],
            device_id=(LOCAL * to + group, part), device_id_type=MESH,
        )

    def rows_copy(to, origin):
        return pltpu.make_async_remote_copy(
            src_ref=rows_out.at[to], dst_ref=rows_in.at[pl.ds(SPAN * origin, SPAN)],
            send_sem=r_send.at[to], recv_sem=r_recv.at[origin],
            device_id=(LOCAL * to + group, part), device_id_type=MESH,
        )

    def ckpt_copy(which, to, origin):
        return pltpu.make_async_remote_copy(
            src_ref=stage.at[which, to],
            dst_ref=fields.at[which, pl.ds(2 + 2 * origin, 2), pl.ds(PAD, SPAN)],
            send_sem=ck_send.at[which, to], recv_sem=ck_recv.at[which, origin],
            device_id=(shot, to), device_id_type=MESH,
        )

    for step in FAR_FIRST:
        model_copy(along(step), level).start()
    cyclic[level] = m_out[level]

    def ckpt_start(k, carry):
        to = lax.rem(part + k, PARTS)
        ckpt_copy(0, to, part).start()
        ckpt_copy(1, to, part).start()
        return carry

    lax.fori_loop(1, PARTS, ckpt_start, 0)

    for edge in (0, 1, PLANES + 2, PLANES + 3):
        for which in range(2):
            halves[which, edge] = jnp.zeros((SPAN, LANES), F32)
    for ref, slots in ((fields, 2), (lams, 3)):
        for slot in range(slots):
            for edge in (0, 1, PLANES + 2, PLANES + 3):
                ref[slot, edge] = jnp.zeros((SPAN + 2 * PAD, LANES), F32)
            for edge in range(2, PLANES + 2):
                ref[slot, edge, pl.ds(0, PAD)] = jnp.zeros((PAD, LANES), F32)
                ref[slot, edge, pl.ds(PAD + SPAN, PAD)] = jnp.zeros((PAD, LANES), F32)
    for which in range(2):
        fields[which, pl.ds(2 + 2 * part, 2), pl.ds(PAD, SPAN)] = stage[which, part]
    for tile in (0, 1, 5):
        placed[:, tile] = jnp.zeros((LOCAL * near, 8, LANES), F32)

    summed_r[...] = jnp.zeros(summed_r.shape, F32)

    def receivers(step):
        at = pl.ds(pl.multiple_of(step * CHUNK, CHUNK), CHUNK)
        flat = listing[:, at]
        zc = lax.shift_right_logical(flat, 14)
        x = lax.shift_right_logical(flat, 8) & 63
        y = (flat & 255) - (OWN * part - HALO)
        row = (lax.shift_right_logical(zc, 2) * 2 + (zc & 1)) * SPAN + x
        column = jnp.where((y >= 0) & (y < 64), (lax.shift_right_logical(zc, 1) & 1) * 64 + y, -1)
        hot = (iota((PLANES * SPAN, CHUNK), 0) == row).astype(F32).astype(BF16)
        match = iota((LANES, CHUNK), 0) == column
        for k in range(STEPS):
            value = record[0, pl.ds(k, 1), at]
            high = value.astype(BF16).astype(F32)
            rest = value - high
            onto[pl.ds(LANES * k, LANES), pl.ds(0, CHUNK)] = jnp.where(match, high, 0.0).astype(BF16)
            onto[pl.ds(LANES * k, LANES), pl.ds(CHUNK, CHUNK)] = jnp.where(match, rest, 0.0).astype(BF16)
        dims = (((1,), (1,)), ((), ()))
        both = jnp.concatenate([hot, hot], axis=1)
        summed_r[...] += lax.dot_general(both, onto[...], dims, preferred_element_type=F32)

    def more(step, carry):
        receivers(step)
        return carry

    inputs[3].wait()
    inputs[4].wait()
    lax.fori_loop(0, FIRST, more, 0)

    for step in FAR_FIRST:
        model_copy(level, along(step)).wait_recv()

    tile_lane = iota((8, LANES), 1)
    odd = iota((8, LANES), 0) & 1

    def spot(shot_k):
        t = offx[shot_k] - (ROWS * group + 2 * level) + SPAN
        oy = offy[shot_k]
        return lax.shift_right_logical(t, 6) - 1, t & 63, lax.shift_right_logical(oy, 7), oy & 127

    def cut(step, carry):
        to = lax.rem(level + near + lax.div(near - step, 2) * (1 - 2 * lax.rem(step, 2)), near)
        for b in range(LOCAL):
            block, rest, tile, at = spot(LOCAL * to + b)
            upper_rows = odd >= rest
            q0, q1 = jnp.maximum(block, 0), jnp.minimum(block + 1, near - 1)
            back = lax.rem(LANES - at, LANES)
            keep = tile_lane < LANES - at
            turned = []
            for k in range(3):
                t = jnp.minimum(tile + k, 3)
                turned.append(pltpu.roll(jnp.where(upper_rows, cyclic[q0, t], cyclic[q1, t]), back, 1))
            for k in range(2):
                rows_out[to, pl.ds(8 * (2 * b + k), 8)] = jnp.where(keep, turned[k], turned[k + 1])
        @pl.when(to != level)
        def _():
            rows_copy(to, level).start()
        return carry

    lax.fori_loop(0, near, cut, 0)
    rows_in[pl.ds(pl.multiple_of(SPAN * level, SPAN), SPAN)] = rows_out[level]
    lax.fori_loop(FIRST, SECOND, more, 0)
    for step in FAR_FIRST:
        rows_copy(level, along(step)).wait_recv()

    def window_copy(to, origin):
        return pltpu.make_async_remote_copy(
            src_ref=windows.at[to],
            dst_ref=arrived.at[pl.ds(2 * lax.rem(origin, PARTS), 2), pl.ds(ROWS * lax.div(origin, PARTS), ROWS)],
            send_sem=w_send.at[to], recv_sem=w_recv.at[origin],
            device_id=device(to), device_id_type=MESH,
        )

    def share(b, carry):
        for plane in range(4):
            for k in range(2):
                for j in range(2):
                    rows_16[plane, k, pl.ds(j, 8, stride=2)] = (
                        rows_in[pl.ds(8 * (2 * b + k) + 2 * plane + j, 8, stride=SPAN)]
                    )
        for i in range(2):
            low = [rows_16[i, k] for k in range(2)]
            high = [pltpu.roll(rows_16[2 + i, k], 64, 1) for k in range(2)]
            for to in range(PARTS):
                windows[b * PARTS + to, i] = window(low, high, to)
        for to in range(PARTS):
            @pl.when(b * PARTS + to != me)
            def _():
                window_copy(b * PARTS + to, me).start()
        return carry

    lax.fori_loop(0, LOCAL, share, 0)
    arrived[pl.ds(2 * part, 2), pl.ds(ROWS * group, ROWS)] = windows[me]
    lax.fori_loop(SECOND, listing.shape[1] // CHUNK, more, 0)

    def prepare(field, slot, which):
        value = field[slot, pl.ds(2, PLANES), pl.ds(PAD, SPAN)].reshape(PLANES * SPAN, LANES)
        high = value.astype(BF16)
        rest = (value - high.astype(F32)).astype(BF16)
        dims = (((1,), (0,)), ((), ()))
        main = lax.dot_general(
            jnp.concatenate([high, rest], axis=1), bands[pl.ds(0, 2 * LANES)], dims, preferred_element_type=F32
        )
        minor = lax.dot_general(high, bands[pl.ds(2 * LANES, LANES), pl.ds(0, LANES)], dims, preferred_element_type=F32)
        along_y[which] = (main[:, :LANES] + minor).reshape(PLANES, SPAN, LANES)
        halves[which, pl.ds(2, PLANES)] = main[:, LANES:].reshape(PLANES, SPAN, LANES)

    def laplace(field, slot, which, e):
        result = []
        at = 2 + 2 * e

        def own(k):
            return field[slot, at + k, pl.ds(PAD, SPAN)]

        other = {k: jnp.where(lower, halves[which, at + k], halves[which, at + k + 2]) for k in (-2, -1, 0, 1)}
        along_z = (
            ((own(1), other[-1]), (other[0], other[-2]), (other[1], own(-1)), (own(2), own(-2))),
            ((other[0], own(0)), (other[1], other[-1]), (own(2), other[-2]), (own(3), own(-1))),
        )
        for i in range(2):
            total = 2.0 * stencil_weights[0] * own(i) + along_y[which, at + i - 2]
            for k in range(1, 5):
                some = along_z[i][k - 1][0] + along_z[i][k - 1][1]
                some = some + field[slot, at + i, pl.ds(PAD + k, SPAN)]
                some = some + field[slot, at + i, pl.ds(PAD - k, SPAN)]
                total = total + stencil_weights[k] * some
            result.append(total)
        return result

    def residual(k, p):
        return summed_r[pl.ds(pl.multiple_of(p * SPAN, SPAN), SPAN), pl.ds(LANES * k, LANES)]

    def to_lam(p, carry):
        lams[0, p + 2, pl.ds(PAD, SPAN)] = residual(0, p)
        return carry

    lax.fori_loop(0, PLANES, to_lam, 0)

    def ckpt_wait(k, carry):
        origin = lax.rem(part + k, PARTS)
        ckpt_copy(0, part, origin).wait_recv()
        ckpt_copy(1, part, origin).wait_recv()
        return carry

    lax.fori_loop(1, PARTS, ckpt_wait, 0)

    def ckpt_sent(k, carry):
        to = lax.rem(part + k, PARTS)
        ckpt_copy(0, to, part).wait_send()
        ckpt_copy(1, to, part).wait_send()
        return carry

    lax.fori_loop(1, PARTS, ckpt_sent, 0)
    for far in FAR_FIRST:
        model_copy(along(far), level).wait_send()
        rows_copy(along(far), level).wait_send()

    prepare(fields, 0, 0)
    prepare(lams, 0, 1)

    def first(e, carry):
        for which, field in ((0, fields), (1, lams)):
            for i, value in enumerate(laplace(field, 0, which, e)):
                first_lap[which, 2 * e + i] = value
        return carry

    lax.fori_loop(0, PARTS, first, 0)

    def window_wait(k, carry):
        window_copy(me, lax.rem(me + k, peers)).wait_recv()
        return carry

    lax.fori_loop(1, peers, window_wait, 0)

    turn = offx[shot] & 63

    def make_c2v(p, carry):
        arrived[p, pl.ds(SPAN, SPAN)] = arrived[p, pl.ds(0, SPAN)]
        speed = arrived[p, pl.ds(turn, SPAN)]
        speeds[p] = speed
        scaled = courant * speed
        c2v[p] = scaled * scaled
        return carry

    lax.fori_loop(0, PLANES, make_c2v, 0)

    flat = place[0]
    zc = lax.shift_right_logical(flat, 14)
    sy = (flat & 255) - (OWN * part - HALO)
    s_plane = lax.shift_right_logical(zc, 2) * 2 + (zc & 1)
    s_lane = jnp.where((sy >= 0) & (sy < 64), (lax.shift_right_logical(zc, 1) & 1) * 64 + sy, -1)
    at_source = (lane == s_lane) & (iota((SPAN, LANES), 0) == (lax.shift_right_logical(flat, 8) & 63))

    def accel_of(value, p, n):
        strength = jnp.where(p == s_plane, pulse[0, n], 0.0)
        return c2v[p] * value + jnp.where(at_source, strength, 0.0)

    inner = pl.ds(PAD, SPAN)

    def step_loop(n):
        now, old = n % 2, 1 - n % 2
        if n:
            prepare(fields, now, 0)
            if n < STEPS - 1:
                prepare(lams, n, 1)

        def step(e, carry):
            laps = laplace(fields, now, 0, e) if n else [first_lap[0, 2 * e + i] for i in range(2)]
            accel = [accel_of(laps[i], 2 * e + i, n) for i in range(2)]
            if n < STEPS - 1:
                laps = laplace(lams, n, 1, e) if n else [first_lap[1, 2 * e + i] for i in range(2)]
            for i in range(2):
                p = 2 * e + i
                if n < STEPS - 1:
                    fields[old, p + 2, inner] = (
                        2.0 * fields[now, p + 2, inner] - fields[old, p + 2, inner] + accel[i]
                    )
                    lam = lams[n, p + 2, inner]
                    newer = 2.0 * lam + c2v[p] * laps[i] + residual(n + 1, p)
                    if n:
                        newer = newer - lams[n - 1, p + 2, inner]
                if n < STEPS - 2:
                    accels[n, p] = accel[i]
                    lams[n + 1, p + 2, inner] = newer
                elif n == STEPS - 2:
                    partial[p] = newer * accels[0, p] + lam * accels[1, p] + lams[1, p + 2, inner] * accel[i]
            if n == STEPS - 1:
                send_parts(e, [
                    (partial[2 * e + i] + lams[0, 2 * e + i + 2, inner] * accel[i]) * 2.0 / speeds[2 * e + i]
                    for i in range(2)
                ])
            return carry

        if n < STEPS - 1:
            lax.fori_loop(0, PARTS, step, 0)
            return
        for half in range(2):
            lax.fori_loop(half * PARTS // 2, (half + 1) * PARTS // 2, step, 0)
            for far in FAR_FIRST:
                z_copy(along(far), level, half).start()

    def send_parts(e, parts):
        both = jnp.where((lane & 63) < OWN, pltpu.roll(parts[0], LANES - HALO, 1), pltpu.roll(parts[1], OWN - HALO, 1))
        packed[e, pl.ds(0, SPAN)] = both
        packed[e, pl.ds(SPAN, SPAN)] = both
        outgoing[e] = packed[e, pl.ds((SPAN - turn) & 63, SPAN)]
        for to in range(near):
            for j in range(2):
                z_out[to, pl.ds(8 * e + 4 * j, 4)] = outgoing[e, pl.ds(2 * to + j, 4, stride=ROWS)]

    def z_copy(to, origin, half):
        return pltpu.make_async_remote_copy(
            src_ref=z_out.at[to, pl.ds(OWN * half, OWN)],
            dst_ref=z_in.at[pl.ds(SPAN * origin + OWN * half, OWN)],
            send_sem=z_send.at[half, to], recv_sem=z_recv.at[half, origin],
            device_id=(LOCAL * to + group, part), device_id_type=MESH,
        )

    for n in range(STEPS):
        step_loop(n)
    z_in[pl.ds(pl.multiple_of(SPAN * level, SPAN), SPAN)] = z_out[level]

    def out_copy(to, origin):
        return pltpu.make_async_remote_copy(
            src_ref=outgoing_2.at[to], dst_ref=landed.at[origin],
            send_sem=o_send.at[to], recv_sem=o_recv.at[origin],
            device_id=device(to), device_id_type=MESH,
        )

    def out_start(e, carry):
        for b in range(LOCAL):
            for j in range(2):
                outgoing_2[b * PARTS + e, pl.ds(8 * j, 8)] = z_in[pl.ds(8 * e + 4 * j + b, 8, stride=SPAN)]
            @pl.when(b * PARTS + e != me)
            def _():
                out_copy(b * PARTS + e, me).start()
        return carry

    def windows_sent(k, carry):
        window_copy(lax.rem(me + k, peers), me).wait_send()
        return carry

    lax.fori_loop(1, peers, windows_sent, 0)
    for half in range(2):
        for far in FAR_FIRST:
            z_copy(level, along(far), half).wait_recv()
        lax.fori_loop(half * PARTS // 2, (half + 1) * PARTS // 2, out_start, 0)
    landed[me] = outgoing_2[me]

    def out_wait(k, carry):
        out_copy(me, lax.rem(me + k, peers)).wait_recv()
        return carry

    lax.fori_loop(1, peers, out_wait, 0)

    group_of = lax.shift_right_logical(tile_lane, 5)

    def put(b, carry):
        for j in range(2):
            for k in range(2):
                pieces = [landed[b * PARTS + 4 * k + c, pl.ds(8 * j, 8)] for c in range(4)]
                for plane in range(4):
                    total = None
                    for c in range(4):
                        by = (OWN * (c - plane)) % LANES
                        piece = pltpu.roll(pieces[c], by, 1) if by else pieces[c]
                        total = piece if total is None else jnp.where(group_of == c, piece, total)
                    by_shot[k, pl.ds(8 * (2 * plane + j), 8)] = total
        for z in range(near):
            at = offy[LOCAL * z + b] & 127
            keep = tile_lane >= at
            first, second = (pltpu.roll(by_shot[k, pl.ds(z, 8, stride=8)], at, 1) for k in range(2))
            placed[b * near + z, 2] = jnp.where(keep, first, 0.0)
            placed[b * near + z, 3] = jnp.where(keep, second, first)
            placed[b * near + z, 4] = jnp.where(keep, 0.0, second)
        return carry

    lax.fori_loop(0, LOCAL, put, 0)

    def add_up(k, sums):
        block, rest, tile, _ = spot(LOCAL * lax.rem(k, near) + lax.div(k, near))
        block = jnp.where(odd >= rest, block, block + 1)
        cells = placed[k, pl.ds(2 - tile, 4)]
        return tuple(total + jnp.where(block == q, cells, 0.0) for q, total in enumerate(sums))

    zero = jnp.zeros((4, 8, LANES), F32)
    for q, total in enumerate(lax.fori_loop(0, LOCAL * near, add_up, (zero,) * near)):
        totals[q] = total.reshape(OWN, LANES)

    def sum_copy(to, origin):
        return pltpu.make_async_remote_copy(
            src_ref=totals.at[to], dst_ref=sums.at[pl.ds(OWN * origin, OWN)],
            send_sem=s_send.at[to], recv_sem=s_recv.at[origin],
            device_id=(LOCAL * to + group, part), device_id_type=MESH,
        )

    for step in FAR_FIRST:
        sum_copy(along(step), level).start()
    sums[pl.ds(pl.multiple_of(OWN * level, OWN), OWN)] = totals[level]

    def outs_sent(k, carry):
        out_copy(lax.rem(me + k, peers), me).wait_send()
        return carry

    lax.fori_loop(1, peers, outs_sent, 0)
    for far in FAR_FIRST:
        for half in range(2):
            z_copy(along(far), level, half).wait_send()
    for step in FAR_FIRST:
        sum_copy(level, along(step)).wait_recv()
    for plane in range(4):
        for tile in range(4):
            for j in range(2):
                final[plane, tile, pl.ds(j, near, stride=2)] = (
                    sums[pl.ds(8 * tile + 2 * plane + j, near, stride=OWN)]
                )
        speed = model[plane]
        total = jnp.concatenate([final[plane, tile] for tile in range(4)], axis=-1)
        scaling = (speed - lower_bound) * (upper_bound - speed) / (upper_bound - lower_bound)
        limit = barrier_weight / (upper_bound - speed) - barrier_weight / (speed - lower_bound)
        out[plane] = scaling * (total + limit)

    for far in FAR_FIRST:
        sum_copy(along(far), level).wait_send()


def on_device(near, model, offsets_x, offsets_y, ckpt_prev, ckpt_cur, wavelet, source, receivers, traces):
    peers = LOCAL * PARTS
    vmem = pl.BlockSpec(memory_space=pltpu.VMEM)
    smem = pl.BlockSpec(memory_space=pltpu.SMEM)
    padded = (PLANES + 4, SPAN + 2 * PAD, LANES)
    plain = (PLANES, SPAN, LANES)
    dma = pltpu.SemaphoreType.DMA
    return pl.pallas_call(
        functools.partial(kernel, near),
        out_shape=jax.ShapeDtypeStruct(model.shape, F32),
        in_specs=[smem] * 4 + [pl.BlockSpec(memory_space=pltpu.HBM)] * 5,
        out_specs=vmem,
        scratch_shapes=[
            *(pltpu.VMEM(a.shape, a.dtype) for a in (model, ckpt_prev, ckpt_cur, receivers, traces)),
            pltpu.VMEM((near, 4, 8, LANES), F32),
            pltpu.VMEM((near, 4, 8, LANES), F32),
            pltpu.VMEM((near, SPAN, LANES), F32),
            pltpu.VMEM((near * SPAN, LANES), F32),
            pltpu.VMEM((4, 2, ROWS, LANES), F32),
            pltpu.VMEM((2, PARTS, 2, SPAN, LANES), F32),
            pltpu.VMEM((2,) + padded, F32),
            pltpu.VMEM((3,) + padded, F32),
            pltpu.VMEM((3 * LANES, 2 * LANES), BF16),
            pltpu.VMEM((2,) + plain, F32),
            pltpu.VMEM((2, PLANES + 4, SPAN, LANES), F32),
            pltpu.VMEM((STEPS * LANES, 2 * CHUNK), BF16),
            pltpu.VMEM((PLANES * SPAN, STEPS * LANES), F32),
            pltpu.VMEM((peers, 2, ROWS, LANES), F32),
            pltpu.VMEM((PLANES, 2 * SPAN, LANES), F32),
            pltpu.VMEM(plain, F32),
            pltpu.VMEM(plain, F32),
            pltpu.VMEM((2,) + plain, F32),
            pltpu.VMEM((2,) + plain, F32),
            pltpu.VMEM(plain, F32),
            pltpu.VMEM((PARTS, 2 * SPAN, LANES), F32),
            pltpu.VMEM((PARTS, SPAN, LANES), F32),
            pltpu.VMEM((near, SPAN, LANES), F32),
            pltpu.VMEM((near * SPAN, LANES), F32),
            pltpu.VMEM((peers, ROWS, LANES), F32),
            pltpu.VMEM((peers, ROWS, LANES), F32),
            pltpu.VMEM((2, SPAN, LANES), F32),
            pltpu.VMEM((LOCAL * near, 6, 8, LANES), F32),
            pltpu.VMEM((near, OWN, LANES), F32),
            pltpu.VMEM((near * OWN, LANES), F32),
            pltpu.VMEM((4, 4, ROWS, LANES), F32),
            dma((5,)),
            dma((near,)), dma((near,)), dma((near,)), dma((near,)),
            dma((2, PARTS)), dma((2, PARTS)),
            dma((peers,)), dma((peers,)), dma((peers,)), dma((peers,)),
            dma((2, near)), dma((2, near)), dma((near,)), dma((near,)),
        ],
        compiler_params=pltpu.CompilerParams(
            collective_id=0, has_side_effects=True, vmem_limit_bytes=62 * 1024 * 1024
        ),
    )(offsets_x, offsets_y, wavelet, source, model, ckpt_prev, ckpt_cur, receivers, traces)


def solution(mesh):
    placed = (
        P("depth", "shots", None),
        P(),
        P(),
        P("shots", "depth", None, None),
        P("shots", "depth", None, None),
        P("shots", None),
        P("shots"),
        P("shots", None),
        P("shots", None, None),
    )
    near = mesh.shape["shots"] // LOCAL
    return jax.shard_map(
        functools.partial(on_device, near),
        mesh=mesh, in_specs=placed, out_specs=P("depth", "shots", None), check_vma=False,
    )
```

```python
import functools

import jax
import jax.numpy as jnp
import numpy as np
from jax import lax
from jax.experimental import pallas as pl
from jax.experimental.pallas import tpu as pltpu
from jax.sharding import PartitionSpec as P

MESH = pl.DeviceIdType.MESH
F32 = jnp.float32
BF16 = jnp.bfloat16
STEPS = 4

stencil_weights = (-205.0 / 72.0, 8.0 / 5.0, -1.0 / 5.0, 8.0 / 315.0, -1.0 / 560.0)
courant = 0.095
lower_bound = 1.0
upper_bound = 5.0
barrier_weight = 0.5

PARTS = 8
LOCAL = 4
PLANES = 16
SPAN = 64
LANES = 128
ROWS = 16
HALO = 16
OWN = 32
CHUNK = 512
PAD = 8
FAR_FIRST = (4, 3, 5, 2, 6, 1, 7)
PIECES = 2
FIRST = 2
SECOND = 4


def iota(shape, dim):
    return lax.broadcasted_iota(jnp.int32, shape, dim)


def window(first, second, part):
    rows = first[0].shape[0]
    lane = iota((rows, LANES), 1)
    zero = jnp.zeros((rows, LANES), F32)
    start = OWN * part - HALO
    tile, at = start // LANES, start % LANES

    def pick(tiles, k):
        return tiles[k] if 0 <= k < 2 else zero

    if at <= 64:
        low = pick(first, tile)
        in_low = (lane >= at) & (lane < at + 64)
        high = pick(second, tile)
    else:
        low = jnp.where(lane >= at, pick(first, tile), pick(first, tile + 1))
        in_low = (lane >= at) | (lane < at - 64)
        own = (lane + 64) % LANES
        high = jnp.where(own >= at, pick(second, tile), pick(second, tile + 1))
    both = jnp.where(in_low, low, high)
    return pltpu.roll(both, (LANES - at) % LANES, 1) if at else both


def make_bands(bands):
    r, c = iota((LANES, LANES), 0), iota((LANES, LANES), 1)
    distance = jnp.where((r < 64) == (c < 64), jnp.abs(r - c), LANES)
    main = jnp.zeros((LANES, LANES), F32)
    rest = main
    for k, weight in enumerate(stencil_weights):
        rounded = float(np.float32(weight).astype(BF16))
        main = jnp.where(distance == k, rounded, main)
        rest = jnp.where(distance == k, float(np.float32(weight)) - rounded, rest)
    swap = (jnp.abs(r - c) == 64).astype(F32).astype(BF16)
    for half in range(2):
        bands[pl.ds(LANES * half, LANES), pl.ds(0, LANES)] = main.astype(BF16)
        bands[pl.ds(LANES * half, LANES), pl.ds(LANES, LANES)] = swap
    bands[pl.ds(2 * LANES, LANES), pl.ds(0, LANES)] = rest.astype(BF16)
    bands[pl.ds(2 * LANES, LANES), pl.ds(LANES, LANES)] = jnp.zeros((LANES, LANES), BF16)


def kernel(
    near,
    offx, offy, pulse, place, model_in, prev_in, cur_in, listing_in, record_in,
    out,
    model, prev, cur, listing, record,
    m_out, cyclic, rows_out, rows_in, rows_16, stage, fields, lams, bands, along_y, halves, onto, summed_r, windows, arrived, speeds, c2v, first_lap,
    accels, partial, packed, outgoing, z_out, z_in, outgoing_2, landed, by_shot, placed, totals, sums, final,
    in_sems,
    m_send, m_recv, r_send, r_recv, ck_send, ck_recv, w_send, w_recv, o_send, o_recv,
    z_send, z_recv, s_send, s_recv,
):
    shot = lax.axis_index("shots")
    part = lax.axis_index("depth")
    level = lax.div(shot, LOCAL)
    group = lax.rem(shot, LOCAL)
    me = group * PARTS + part
    peers = LOCAL * PARTS
    lane = iota((SPAN, LANES), 1)
    lower = lane < 64

    def along(step):
        return lax.rem(level + step, near)

    def device(k):
        return (LOCAL * level + lax.div(k, PARTS), lax.rem(k, PARTS))

    inputs = [
        pltpu.make_async_copy(model_in, model, in_sems.at[0]),
        pltpu.make_async_copy(cur_in, cur, in_sems.at[1]),
        pltpu.make_async_copy(prev_in, prev, in_sems.at[2]),
        pltpu.make_async_copy(listing_in, listing, in_sems.at[3]),
        pltpu.make_async_copy(record_in, record, in_sems.at[4]),
    ]
    for copy in inputs:
        copy.start()

    barrier = pltpu.get_barrier_semaphore()

    def greet(k, carry):
        pl.semaphore_signal(barrier, inc=1, device_id=device(lax.rem(me + k, peers)), device_id_type=MESH)
        return carry

    for step in FAR_FIRST:
        pl.semaphore_signal(barrier, inc=1, device_id=(LOCAL * along(step) + group, part), device_id_type=MESH)
    lax.fori_loop(1, peers, greet, 0)

    inputs[0].wait()
    for to in range(near):
        for tile in range(4):
            for plane in range(4):
                m_out[to, tile, pl.ds(2 * plane, 2)] = model[plane, pl.ds(2 * to, 2), pl.ds(LANES * tile, LANES)]
    pl.semaphore_wait(barrier, peers - 1 + len(FAR_FIRST))

    def model_copy(to, origin):
        return pltpu.make_async_remote_copy(
            src_ref=m_out.at[to], dst_ref=cyclic.at[origin],
            send_sem=m_send.at[to], recv_sem=m_recv.at[origin],
            device_id=(LOCAL * to + group, part), device_id_type=MESH,
        )

    def rows_copy(to, origin):
        return pltpu.make_async_remote_copy(
            src_ref=rows_out.at[to], dst_ref=rows_in.at[pl.ds(SPAN * origin, SPAN)],
            send_sem=r_send.at[to], recv_sem=r_recv.at[origin],
            device_id=(LOCAL * to + group, part), device_id_type=MESH,
        )

    def ckpt_copy(which, to, origin):
        return pltpu.make_async_remote_copy(
            src_ref=stage.at[which, to],
            dst_ref=fields.at[which, pl.ds(2 + 2 * origin, 2), pl.ds(PAD, SPAN)],
            send_sem=ck_send.at[which, to], recv_sem=ck_recv.at[which, origin],
            device_id=(shot, to), device_id_type=MESH,
        )

    for step in FAR_FIRST:
        model_copy(along(step), level).start()
    cyclic[level] = m_out[level]

    for which, source in ((0, cur), (1, prev)):
        inputs[1 + which].wait()
        for i in range(2):
            low = [source[0, i, :, pl.ds(LANES * k, LANES)] for k in range(2)]
            high = [pltpu.roll(source[0, 2 + i, :, pl.ds(LANES * k, LANES)], 64, 1) for k in range(2)]
            for to in range(PARTS):
                stage[which, to, i] = window(low, high, to)

        def ckpt_start(k, carry, which=which):
            ckpt_copy(which, lax.rem(part + k, PARTS), part).start()
            return carry

        lax.fori_loop(1, PARTS, ckpt_start, 0)

    make_bands(bands)

    for edge in (0, 1, PLANES + 2, PLANES + 3):
        for which in range(2):
            halves[which, edge] = jnp.zeros((SPAN, LANES), F32)
    for ref, slots in ((fields, 2), (lams, 3)):
        for slot in range(slots):
            for edge in (0, 1, PLANES + 2, PLANES + 3):
                ref[slot, edge] = jnp.zeros((SPAN + 2 * PAD, LANES), F32)
            for edge in range(2, PLANES + 2):
                ref[slot, edge, pl.ds(0, PAD)] = jnp.zeros((PAD, LANES), F32)
                ref[slot, edge, pl.ds(PAD + SPAN, PAD)] = jnp.zeros((PAD, LANES), F32)
    for which in range(2):
        fields[which, pl.ds(2 + 2 * part, 2), pl.ds(PAD, SPAN)] = stage[which, part]
    for tile in (0, 1, 5):
        placed[:, tile] = jnp.zeros((LOCAL * near, 8, LANES), F32)

    summed_r[...] = jnp.zeros(summed_r.shape, F32)

    def receivers(step):
        at = pl.ds(pl.multiple_of(step * CHUNK, CHUNK), CHUNK)
        flat = listing[:, at]
        zc = lax.shift_right_logical(flat, 14)
        x = lax.shift_right_logical(flat, 8) & 63
        y = (flat & 255) - (OWN * part - HALO)
        row = (lax.shift_right_logical(zc, 2) * 2 + (zc & 1)) * SPAN + x
        column = jnp.where((y >= 0) & (y < 64), (lax.shift_right_logical(zc, 1) & 1) * 64 + y, -1)
        hot = (iota((PLANES * SPAN, CHUNK), 0) == row).astype(F32).astype(BF16)
        match = iota((LANES, CHUNK), 0) == column
        for k in range(STEPS):
            value = record[0, pl.ds(k, 1), at]
            high = value.astype(BF16).astype(F32)
            rest = value - high
            onto[pl.ds(LANES * k, LANES), pl.ds(0, CHUNK)] = jnp.where(match, high, 0.0).astype(BF16)
            onto[pl.ds(LANES * k, LANES), pl.ds(CHUNK, CHUNK)] = jnp.where(match, rest, 0.0).astype(BF16)
        dims = (((1,), (1,)), ((), ()))
        both = jnp.concatenate([hot, hot], axis=1)
        summed_r[...] += lax.dot_general(both, onto[...], dims, preferred_element_type=F32)

    def more(step, carry):
        receivers(step)
        return carry

    inputs[3].wait()
    inputs[4].wait()
    lax.fori_loop(0, FIRST, more, 0)

    for step in FAR_FIRST:
        model_copy(level, along(step)).wait_recv()

    tile_lane = iota((8, LANES), 1)
    odd = iota((8, LANES), 0) & 1

    def spot(shot_k):
        t = offx[shot_k] - (ROWS * group + 2 * level) + SPAN
        oy = offy[shot_k]
        return lax.shift_right_logical(t, 6) - 1, t & 63, lax.shift_right_logical(oy, 7), oy & 127

    def cut(step, carry):
        to = lax.rem(level + near + lax.div(near - step, 2) * (1 - 2 * lax.rem(step, 2)), near)
        for b in range(LOCAL):
            block, rest, tile, at = spot(LOCAL * to + b)
            upper_rows = odd >= rest
            q0, q1 = jnp.maximum(block, 0), jnp.minimum(block + 1, near - 1)
            back = lax.rem(LANES - at, LANES)
            keep = tile_lane < LANES - at
            turned = []
            for k in range(3):
                t = jnp.minimum(tile + k, 3)
                turned.append(pltpu.roll(jnp.where(upper_rows, cyclic[q0, t], cyclic[q1, t]), back, 1))
            for k in range(2):
                rows_out[to, pl.ds(8 * (2 * b + k), 8)] = jnp.where(keep, turned[k], turned[k + 1])
        @pl.when(to != level)
        def _():
            rows_copy(to, level).start()
        return carry

    lax.fori_loop(0, near, cut, 0)
    rows_in[pl.ds(pl.multiple_of(SPAN * level, SPAN), SPAN)] = rows_out[level]
    lax.fori_loop(FIRST, SECOND, more, 0)
    for step in FAR_FIRST:
        rows_copy(level, along(step)).wait_recv()

    def window_copy(to, origin):
        return pltpu.make_async_remote_copy(
            src_ref=windows.at[to],
            dst_ref=arrived.at[pl.ds(2 * lax.rem(origin, PARTS), 2), pl.ds(ROWS * lax.div(origin, PARTS), ROWS)],
            send_sem=w_send.at[to], recv_sem=w_recv.at[origin],
            device_id=device(to), device_id_type=MESH,
        )

    def share(b, carry):
        for plane in range(4):
            for k in range(2):
                for j in range(2):
                    rows_16[plane, k, pl.ds(j, 8, stride=2)] = (
                        rows_in[pl.ds(8 * (2 * b + k) + 2 * plane + j, 8, stride=SPAN)]
                    )
        for i in range(2):
            low = [rows_16[i, k] for k in range(2)]
            high = [pltpu.roll(rows_16[2 + i, k], 64, 1) for k in range(2)]
            for to in range(PARTS):
                windows[b * PARTS + to, i] = window(low, high, to)
        for to in range(PARTS):
            @pl.when(b * PARTS + to != me)
            def _():
                window_copy(b * PARTS + to, me).start()
        return carry

    lax.fori_loop(0, LOCAL, share, 0)
    arrived[pl.ds(2 * part, 2), pl.ds(ROWS * group, ROWS)] = windows[me]
    lax.fori_loop(SECOND, listing.shape[1] // CHUNK, more, 0)

    def prepare(field, slot, which):
        value = field[slot, pl.ds(2, PLANES), pl.ds(PAD, SPAN)].reshape(PLANES * SPAN, LANES)
        high = value.astype(BF16)
        rest = (value - high.astype(F32)).astype(BF16)
        dims = (((1,), (0,)), ((), ()))
        main = lax.dot_general(
            jnp.concatenate([high, rest], axis=1), bands[pl.ds(0, 2 * LANES)], dims, preferred_element_type=F32
        )
        minor = lax.dot_general(high, bands[pl.ds(2 * LANES, LANES), pl.ds(0, LANES)], dims, preferred_element_type=F32)
        along_y[which] = (main[:, :LANES] + minor).reshape(PLANES, SPAN, LANES)
        halves[which, pl.ds(2, PLANES)] = main[:, LANES:].reshape(PLANES, SPAN, LANES)

    def laplace(field, slot, which, e):
        result = []
        at = 2 + 2 * e

        def own(k):
            return field[slot, at + k, pl.ds(PAD, SPAN)]

        other = {k: jnp.where(lower, halves[which, at + k], halves[which, at + k + 2]) for k in (-2, -1, 0, 1)}
        along_z = (
            ((own(1), other[-1]), (other[0], other[-2]), (other[1], own(-1)), (own(2), own(-2))),
            ((other[0], own(0)), (other[1], other[-1]), (own(2), other[-2]), (own(3), own(-1))),
        )
        for i in range(2):
            total = 2.0 * stencil_weights[0] * own(i) + along_y[which, at + i - 2]
            for k in range(1, 5):
                some = along_z[i][k - 1][0] + along_z[i][k - 1][1]
                some = some + field[slot, at + i, pl.ds(PAD + k, SPAN)]
                some = some + field[slot, at + i, pl.ds(PAD - k, SPAN)]
                total = total + stencil_weights[k] * some
            result.append(total)
        return result

    def residual(k, p):
        return summed_r[pl.ds(pl.multiple_of(p * SPAN, SPAN), SPAN), pl.ds(LANES * k, LANES)]

    def to_lam(p, carry):
        lams[0, p + 2, pl.ds(PAD, SPAN)] = residual(0, p)
        return carry

    lax.fori_loop(0, PLANES, to_lam, 0)

    def ckpt_wait(k, carry):
        origin = lax.rem(part + k, PARTS)
        ckpt_copy(0, part, origin).wait_recv()
        ckpt_copy(1, part, origin).wait_recv()
        return carry

    lax.fori_loop(1, PARTS, ckpt_wait, 0)

    def ckpt_sent(k, carry):
        to = lax.rem(part + k, PARTS)
        ckpt_copy(0, to, part).wait_send()
        ckpt_copy(1, to, part).wait_send()
        return carry

    lax.fori_loop(1, PARTS, ckpt_sent, 0)
    for far in FAR_FIRST:
        model_copy(along(far), level).wait_send()
        rows_copy(along(far), level).wait_send()

    prepare(fields, 0, 0)
    prepare(lams, 0, 1)

    def first(e, carry):
        for which, field in ((0, fields), (1, lams)):
            for i, value in enumerate(laplace(field, 0, which, e)):
                first_lap[which, 2 * e + i] = value
        return carry

    lax.fori_loop(0, PARTS, first, 0)

    def window_wait(k, carry):
        window_copy(me, lax.rem(me + k, peers)).wait_recv()
        return carry

    lax.fori_loop(1, peers, window_wait, 0)

    turn = offx[shot] & 63

    def make_c2v(p, carry):
        arrived[p, pl.ds(SPAN, SPAN)] = arrived[p, pl.ds(0, SPAN)]
        speed = arrived[p, pl.ds(turn, SPAN)]
        speeds[p] = speed
        scaled = courant * speed
        c2v[p] = scaled * scaled
        return carry

    lax.fori_loop(0, PLANES, make_c2v, 0)

    flat = place[0]
    zc = lax.shift_right_logical(flat, 14)
    sy = (flat & 255) - (OWN * part - HALO)
    s_plane = lax.shift_right_logical(zc, 2) * 2 + (zc & 1)
    s_lane = jnp.where((sy >= 0) & (sy < 64), (lax.shift_right_logical(zc, 1) & 1) * 64 + sy, -1)
    at_source = (lane == s_lane) & (iota((SPAN, LANES), 0) == (lax.shift_right_logical(flat, 8) & 63))

    def accel_of(value, p, n):
        strength = jnp.where(p == s_plane, pulse[0, n], 0.0)
        return c2v[p] * value + jnp.where(at_source, strength, 0.0)

    inner = pl.ds(PAD, SPAN)

    def step_loop(n):
        now, old = n % 2, 1 - n % 2
        if n:
            prepare(fields, now, 0)
            if n < STEPS - 1:
                prepare(lams, n, 1)

        def step(e, carry):
            laps = laplace(fields, now, 0, e) if n else [first_lap[0, 2 * e + i] for i in range(2)]
            accel = [accel_of(laps[i], 2 * e + i, n) for i in range(2)]
            if n < STEPS - 1:
                laps = laplace(lams, n, 1, e) if n else [first_lap[1, 2 * e + i] for i in range(2)]
            for i in range(2):
                p = 2 * e + i
                if n < STEPS - 1:
                    fields[old, p + 2, inner] = (
                        2.0 * fields[now, p + 2, inner] - fields[old, p + 2, inner] + accel[i]
                    )
                    lam = lams[n, p + 2, inner]
                    newer = 2.0 * lam + c2v[p] * laps[i] + residual(n + 1, p)
                    if n:
                        newer = newer - lams[n - 1, p + 2, inner]
                if n < STEPS - 2:
                    accels[n, p] = accel[i]
                    lams[n + 1, p + 2, inner] = newer
                elif n == STEPS - 2:
                    partial[p] = newer * accels[0, p] + lam * accels[1, p] + lams[1, p + 2, inner] * accel[i]
            if n == STEPS - 1:
                send_parts(e, [
                    (partial[2 * e + i] + lams[0, 2 * e + i + 2, inner] * accel[i]) * 2.0 / speeds[2 * e + i]
                    for i in range(2)
                ])
            return carry

        if n < STEPS - 1:
            lax.fori_loop(0, PARTS, step, 0)
            return
        for piece in range(PIECES):
            lax.fori_loop(piece * PARTS // PIECES, (piece + 1) * PARTS // PIECES, step, 0)
            for far in FAR_FIRST:
                z_copy(along(far), level, piece).start()

    def send_parts(e, parts):
        both = jnp.where((lane & 63) < OWN, pltpu.roll(parts[0], LANES - HALO, 1), pltpu.roll(parts[1], OWN - HALO, 1))
        packed[e, pl.ds(0, SPAN)] = both
        packed[e, pl.ds(SPAN, SPAN)] = both
        outgoing[e] = packed[e, pl.ds((SPAN - turn) & 63, SPAN)]
        for to in range(near):
            for j in range(2):
                z_out[to, pl.ds(8 * e + 4 * j, 4)] = outgoing[e, pl.ds(2 * to + j, 4, stride=ROWS)]

    def z_copy(to, origin, piece):
        rows = SPAN // PIECES
        return pltpu.make_async_remote_copy(
            src_ref=z_out.at[to, pl.ds(rows * piece, rows)],
            dst_ref=z_in.at[pl.ds(SPAN * origin + rows * piece, rows)],
            send_sem=z_send.at[piece, to], recv_sem=z_recv.at[piece, origin],
            device_id=(LOCAL * to + group, part), device_id_type=MESH,
        )

    for n in range(STEPS):
        step_loop(n)
    z_in[pl.ds(pl.multiple_of(SPAN * level, SPAN), SPAN)] = z_out[level]

    def out_copy(to, origin):
        return pltpu.make_async_remote_copy(
            src_ref=outgoing_2.at[to], dst_ref=landed.at[origin],
            send_sem=o_send.at[to], recv_sem=o_recv.at[origin],
            device_id=device(to), device_id_type=MESH,
        )

    def out_start(e, carry):
        for b in range(LOCAL):
            for j in range(2):
                outgoing_2[b * PARTS + e, pl.ds(8 * j, 8)] = z_in[pl.ds(8 * e + 4 * j + b, 8, stride=SPAN)]
            @pl.when(b * PARTS + e != me)
            def _():
                out_copy(b * PARTS + e, me).start()
        return carry

    def windows_sent(k, carry):
        window_copy(lax.rem(me + k, peers), me).wait_send()
        return carry

    lax.fori_loop(1, peers, windows_sent, 0)
    for piece in range(PIECES):
        for far in FAR_FIRST:
            z_copy(level, along(far), piece).wait_recv()
        lax.fori_loop(piece * PARTS // PIECES, (piece + 1) * PARTS // PIECES, out_start, 0)
    landed[me] = outgoing_2[me]

    def out_wait(k, carry):
        out_copy(me, lax.rem(me + k, peers)).wait_recv()
        return carry

    lax.fori_loop(1, peers, out_wait, 0)

    group_of = lax.shift_right_logical(tile_lane, 5)

    def put(b, carry):
        for j in range(2):
            for k in range(2):
                pieces = [landed[b * PARTS + 4 * k + c, pl.ds(8 * j, 8)] for c in range(4)]
                for plane in range(4):
                    total = None
                    for c in range(4):
                        by = (OWN * (c - plane)) % LANES
                        piece = pltpu.roll(pieces[c], by, 1) if by else pieces[c]
                        total = piece if total is None else jnp.where(group_of == c, piece, total)
                    by_shot[k, pl.ds(8 * (2 * plane + j), 8)] = total
        for z in range(near):
            at = offy[LOCAL * z + b] & 127
            keep = tile_lane >= at
            first, second = (pltpu.roll(by_shot[k, pl.ds(z, 8, stride=8)], at, 1) for k in range(2))
            placed[b * near + z, 2] = jnp.where(keep, first, 0.0)
            placed[b * near + z, 3] = jnp.where(keep, second, first)
            placed[b * near + z, 4] = jnp.where(keep, 0.0, second)
        return carry

    lax.fori_loop(0, LOCAL, put, 0)

    def add_up(k, sums):
        block, rest, tile, _ = spot(LOCAL * lax.rem(k, near) + lax.div(k, near))
        block = jnp.where(odd >= rest, block, block + 1)
        cells = placed[k, pl.ds(2 - tile, 4)]
        return tuple(total + jnp.where(block == q, cells, 0.0) for q, total in enumerate(sums))

    zero = jnp.zeros((4, 8, LANES), F32)
    for q, total in enumerate(lax.fori_loop(0, LOCAL * near, add_up, (zero,) * near)):
        totals[q] = total.reshape(OWN, LANES)

    def sum_copy(to, origin):
        return pltpu.make_async_remote_copy(
            src_ref=totals.at[to], dst_ref=sums.at[pl.ds(OWN * origin, OWN)],
            send_sem=s_send.at[to], recv_sem=s_recv.at[origin],
            device_id=(LOCAL * to + group, part), device_id_type=MESH,
        )

    for step in FAR_FIRST:
        sum_copy(along(step), level).start()
    sums[pl.ds(pl.multiple_of(OWN * level, OWN), OWN)] = totals[level]

    def outs_sent(k, carry):
        out_copy(lax.rem(me + k, peers), me).wait_send()
        return carry

    lax.fori_loop(1, peers, outs_sent, 0)
    for far in FAR_FIRST:
        for piece in range(PIECES):
            z_copy(along(far), level, piece).wait_send()
    for step in FAR_FIRST:
        sum_copy(level, along(step)).wait_recv()
    for plane in range(4):
        for tile in range(4):
            for j in range(2):
                final[plane, tile, pl.ds(j, near, stride=2)] = (
                    sums[pl.ds(8 * tile + 2 * plane + j, near, stride=OWN)]
                )
        speed = model[plane]
        total = jnp.concatenate([final[plane, tile] for tile in range(4)], axis=-1)
        scaling = (speed - lower_bound) * (upper_bound - speed) / (upper_bound - lower_bound)
        limit = barrier_weight / (upper_bound - speed) - barrier_weight / (speed - lower_bound)
        out[plane] = scaling * (total + limit)

    for far in FAR_FIRST:
        sum_copy(along(far), level).wait_send()


def on_device(near, model, offsets_x, offsets_y, ckpt_prev, ckpt_cur, wavelet, source, receivers, traces):
    peers = LOCAL * PARTS
    vmem = pl.BlockSpec(memory_space=pltpu.VMEM)
    smem = pl.BlockSpec(memory_space=pltpu.SMEM)
    padded = (PLANES + 4, SPAN + 2 * PAD, LANES)
    plain = (PLANES, SPAN, LANES)
    dma = pltpu.SemaphoreType.DMA
    return pl.pallas_call(
        functools.partial(kernel, near),
        out_shape=jax.ShapeDtypeStruct(model.shape, F32),
        in_specs=[smem] * 4 + [pl.BlockSpec(memory_space=pltpu.HBM)] * 5,
        out_specs=vmem,
        scratch_shapes=[
            *(pltpu.VMEM(a.shape, a.dtype) for a in (model, ckpt_prev, ckpt_cur, receivers, traces)),
            pltpu.VMEM((near, 4, 8, LANES), F32),
            pltpu.VMEM((near, 4, 8, LANES), F32),
            pltpu.VMEM((near, SPAN, LANES), F32),
            pltpu.VMEM((near * SPAN, LANES), F32),
            pltpu.VMEM((4, 2, ROWS, LANES), F32),
            pltpu.VMEM((2, PARTS, 2, SPAN, LANES), F32),
            pltpu.VMEM((2,) + padded, F32),
            pltpu.VMEM((3,) + padded, F32),
            pltpu.VMEM((3 * LANES, 2 * LANES), BF16),
            pltpu.VMEM((2,) + plain, F32),
            pltpu.VMEM((2, PLANES + 4, SPAN, LANES), F32),
            pltpu.VMEM((STEPS * LANES, 2 * CHUNK), BF16),
            pltpu.VMEM((PLANES * SPAN, STEPS * LANES), F32),
            pltpu.VMEM((peers, 2, ROWS, LANES), F32),
            pltpu.VMEM((PLANES, 2 * SPAN, LANES), F32),
            pltpu.VMEM(plain, F32),
            pltpu.VMEM(plain, F32),
            pltpu.VMEM((2,) + plain, F32),
            pltpu.VMEM((2,) + plain, F32),
            pltpu.VMEM(plain, F32),
            pltpu.VMEM((PARTS, 2 * SPAN, LANES), F32),
            pltpu.VMEM((PARTS, SPAN, LANES), F32),
            pltpu.VMEM((near, SPAN, LANES), F32),
            pltpu.VMEM((near * SPAN, LANES), F32),
            pltpu.VMEM((peers, ROWS, LANES), F32),
            pltpu.VMEM((peers, ROWS, LANES), F32),
            pltpu.VMEM((2, SPAN, LANES), F32),
            pltpu.VMEM((LOCAL * near, 6, 8, LANES), F32),
            pltpu.VMEM((near, OWN, LANES), F32),
            pltpu.VMEM((near * OWN, LANES), F32),
            pltpu.VMEM((4, 4, ROWS, LANES), F32),
            dma((5,)),
            dma((near,)), dma((near,)), dma((near,)), dma((near,)),
            dma((2, PARTS)), dma((2, PARTS)),
            dma((peers,)), dma((peers,)), dma((peers,)), dma((peers,)),
            dma((PIECES, near)), dma((PIECES, near)), dma((near,)), dma((near,)),
        ],
        compiler_params=pltpu.CompilerParams(
            collective_id=0, has_side_effects=True, vmem_limit_bytes=62 * 1024 * 1024
        ),
    )(offsets_x, offsets_y, wavelet, source, model, ckpt_prev, ckpt_cur, receivers, traces)


def solution(mesh):
    placed = (
        P("depth", "shots", None),
        P(),
        P(),
        P("shots", "depth", None, None),
        P("shots", "depth", None, None),
        P("shots", None),
        P("shots"),
        P("shots", None),
        P("shots", None, None),
    )
    near = mesh.shape["shots"] // LOCAL
    return jax.shard_map(
        functools.partial(on_device, near),
        mesh=mesh, in_specs=placed, out_specs=P("depth", "shots", None), check_vma=False,
    )
```

```python
import functools

import jax
import jax.numpy as jnp
import numpy as np
from jax import lax
from jax.experimental import pallas as pl
from jax.experimental.pallas import tpu as pltpu
from jax.sharding import PartitionSpec as P

MESH = pl.DeviceIdType.MESH
F32 = jnp.float32
BF16 = jnp.bfloat16
STEPS = 4

stencil_weights = (-205.0 / 72.0, 8.0 / 5.0, -1.0 / 5.0, 8.0 / 315.0, -1.0 / 560.0)
courant = 0.095
lower_bound = 1.0
upper_bound = 5.0
barrier_weight = 0.5

PARTS = 8
LOCAL = 4
PLANES = 16
SPAN = 64
LANES = 128
ROWS = 16
HALO = 16
OWN = 32
CHUNK = 512
PAD = 8
FAR_FIRST = (4, 3, 5, 2, 6, 1, 7)
PIECES = 2
FIRST = 2
SECOND = 4


def iota(shape, dim):
    return lax.broadcasted_iota(jnp.int32, shape, dim)


def window(first, second, part):
    rows = first[0].shape[0]
    lane = iota((rows, LANES), 1)
    zero = jnp.zeros((rows, LANES), F32)
    start = OWN * part - HALO
    tile, at = start // LANES, start % LANES

    def pick(tiles, k):
        return tiles[k] if 0 <= k < 2 else zero

    if at <= 64:
        low = pick(first, tile)
        in_low = (lane >= at) & (lane < at + 64)
        high = pick(second, tile)
    else:
        low = jnp.where(lane >= at, pick(first, tile), pick(first, tile + 1))
        in_low = (lane >= at) | (lane < at - 64)
        own = (lane + 64) % LANES
        high = jnp.where(own >= at, pick(second, tile), pick(second, tile + 1))
    both = jnp.where(in_low, low, high)
    return pltpu.roll(both, (LANES - at) % LANES, 1) if at else both


def make_bands(bands):
    r, c = iota((LANES, LANES), 0), iota((LANES, LANES), 1)
    distance = jnp.where((r < 64) == (c < 64), jnp.abs(r - c), LANES)
    main = jnp.zeros((LANES, LANES), F32)
    rest = main
    for k, weight in enumerate(stencil_weights):
        rounded = float(np.float32(weight).astype(BF16))
        main = jnp.where(distance == k, rounded, main)
        rest = jnp.where(distance == k, float(np.float32(weight)) - rounded, rest)
    swap = (jnp.abs(r - c) == 64).astype(F32).astype(BF16)
    for half in range(2):
        bands[pl.ds(LANES * half, LANES), pl.ds(0, LANES)] = main.astype(BF16)
        bands[pl.ds(LANES * half, LANES), pl.ds(LANES, LANES)] = swap
    bands[pl.ds(2 * LANES, LANES), pl.ds(0, LANES)] = rest.astype(BF16)
    bands[pl.ds(2 * LANES, LANES), pl.ds(LANES, LANES)] = jnp.zeros((LANES, LANES), BF16)


def kernel(
    near,
    offx, offy, pulse, place, model_in, prev_in, cur_in, listing_in, record_in,
    out,
    model, prev, cur, listing, record,
    m_out, cyclic, rows_out, rows_in, rows_16, stage, fields, lams, bands, along_y, halves, onto, summed_r, windows, arrived, doubled, speeds, c2v, first_lap,
    accels, partial, packed, outgoing, z_out, z_in, outgoing_2, landed, by_shot, placed, totals, sums, final,
    in_sems,
    m_send, m_recv, r_send, r_recv, ck_send, ck_recv, w_send, w_recv, o_send, o_recv,
    z_send, z_recv, s_send, s_recv,
):
    shot = lax.axis_index("shots")
    part = lax.axis_index("depth")
    level = lax.div(shot, LOCAL)
    group = lax.rem(shot, LOCAL)
    me = group * PARTS + part
    peers = LOCAL * PARTS
    lane = iota((SPAN, LANES), 1)
    lower = lane < 64

    def along(step):
        return lax.rem(level + step, near)

    def device(k):
        return (LOCAL * level + lax.div(k, PARTS), lax.rem(k, PARTS))

    inputs = [
        pltpu.make_async_copy(model_in, model, in_sems.at[0]),
        pltpu.make_async_copy(cur_in, cur, in_sems.at[1]),
        pltpu.make_async_copy(prev_in, prev, in_sems.at[2]),
        pltpu.make_async_copy(listing_in, listing, in_sems.at[3]),
        pltpu.make_async_copy(record_in, record, in_sems.at[4]),
    ]
    for copy in inputs:
        copy.start()

    barrier = pltpu.get_barrier_semaphore()

    def greet(k, carry):
        pl.semaphore_signal(barrier, inc=1, device_id=device(lax.rem(me + k, peers)), device_id_type=MESH)
        return carry

    for step in FAR_FIRST:
        pl.semaphore_signal(barrier, inc=1, device_id=(LOCAL * along(step) + group, part), device_id_type=MESH)
    lax.fori_loop(1, peers, greet, 0)

    inputs[0].wait()
    for to in range(near):
        for tile in range(4):
            for plane in range(4):
                m_out[to, tile, pl.ds(2 * plane, 2)] = model[plane, pl.ds(2 * to, 2), pl.ds(LANES * tile, LANES)]
    pl.semaphore_wait(barrier, peers - 1 + len(FAR_FIRST))

    def model_copy(to, origin):
        return pltpu.make_async_remote_copy(
            src_ref=m_out.at[to], dst_ref=cyclic.at[origin],
            send_sem=m_send.at[to], recv_sem=m_recv.at[origin],
            device_id=(LOCAL * to + group, part), device_id_type=MESH,
        )

    def rows_copy(to, origin):
        return pltpu.make_async_remote_copy(
            src_ref=rows_out.at[to], dst_ref=rows_in.at[pl.ds(SPAN * origin, SPAN)],
            send_sem=r_send.at[to], recv_sem=r_recv.at[origin],
            device_id=(LOCAL * to + group, part), device_id_type=MESH,
        )

    def ckpt_copy(which, to, origin):
        return pltpu.make_async_remote_copy(
            src_ref=stage.at[which, to],
            dst_ref=fields.at[which, pl.ds(2 + 2 * origin, 2), pl.ds(PAD, SPAN)],
            send_sem=ck_send.at[which, to], recv_sem=ck_recv.at[which, origin],
            device_id=(shot, to), device_id_type=MESH,
        )

    for step in FAR_FIRST:
        model_copy(along(step), level).start()
    cyclic[level] = m_out[level]

    for which, source in ((0, cur), (1, prev)):
        inputs[1 + which].wait()
        for i in range(2):
            low = [source[0, i, :, pl.ds(LANES * k, LANES)] for k in range(2)]
            high = [pltpu.roll(source[0, 2 + i, :, pl.ds(LANES * k, LANES)], 64, 1) for k in range(2)]
            for to in range(PARTS):
                stage[which, to, i] = window(low, high, to)

        def ckpt_start(k, carry, which=which):
            ckpt_copy(which, lax.rem(part + k, PARTS), part).start()
            return carry

        lax.fori_loop(1, PARTS, ckpt_start, 0)

    make_bands(bands)

    for edge in (0, 1, PLANES + 2, PLANES + 3):
        for which in range(2):
            halves[which, edge] = jnp.zeros((SPAN, LANES), F32)
    for ref, slots in ((fields, 2), (lams, 3)):
        for slot in range(slots):
            for edge in (0, 1, PLANES + 2, PLANES + 3):
                ref[slot, edge] = jnp.zeros((SPAN + 2 * PAD, LANES), F32)
            for edge in range(2, PLANES + 2):
                ref[slot, edge, pl.ds(0, PAD)] = jnp.zeros((PAD, LANES), F32)
                ref[slot, edge, pl.ds(PAD + SPAN, PAD)] = jnp.zeros((PAD, LANES), F32)
    for which in range(2):
        fields[which, pl.ds(2 + 2 * part, 2), pl.ds(PAD, SPAN)] = stage[which, part]
    for tile in (0, 1, 5):
        placed[:, tile] = jnp.zeros((LOCAL * near, 8, LANES), F32)

    summed_r[...] = jnp.zeros(summed_r.shape, F32)

    def receivers(step):
        at = pl.ds(pl.multiple_of(step * CHUNK, CHUNK), CHUNK)
        flat = listing[:, at]
        zc = lax.shift_right_logical(flat, 14)
        x = lax.shift_right_logical(flat, 8) & 63
        y = (flat & 255) - (OWN * part - HALO)
        row = (lax.shift_right_logical(zc, 2) * 2 + (zc & 1)) * SPAN + x
        column = jnp.where((y >= 0) & (y < 64), (lax.shift_right_logical(zc, 1) & 1) * 64 + y, -1)
        hot = (iota((PLANES * SPAN, CHUNK), 0) == row).astype(F32).astype(BF16)
        match = iota((LANES, CHUNK), 0) == column
        for k in range(STEPS):
            value = record[0, pl.ds(k, 1), at]
            high = value.astype(BF16).astype(F32)
            rest = value - high
            onto[pl.ds(LANES * k, LANES), pl.ds(0, CHUNK)] = jnp.where(match, high, 0.0).astype(BF16)
            onto[pl.ds(LANES * k, LANES), pl.ds(CHUNK, CHUNK)] = jnp.where(match, rest, 0.0).astype(BF16)
        dims = (((1,), (1,)), ((), ()))
        both = jnp.concatenate([hot, hot], axis=1)
        summed_r[...] += lax.dot_general(both, onto[...], dims, preferred_element_type=F32)

    def more(step, carry):
        receivers(step)
        return carry

    inputs[3].wait()
    inputs[4].wait()
    lax.fori_loop(0, FIRST, more, 0)

    for step in FAR_FIRST:
        model_copy(level, along(step)).wait_recv()

    tile_lane = iota((8, LANES), 1)
    odd = iota((8, LANES), 0) & 1

    def spot(shot_k):
        t = offx[shot_k] - (ROWS * group + 2 * level) + SPAN
        oy = offy[shot_k]
        return lax.shift_right_logical(t, 6) - 1, t & 63, lax.shift_right_logical(oy, 7), oy & 127

    def cut(step, carry):
        to = lax.rem(level + near + lax.div(near - step, 2) * (1 - 2 * lax.rem(step, 2)), near)
        for b in range(LOCAL):
            block, rest, tile, at = spot(LOCAL * to + b)
            upper_rows = odd >= rest
            q0, q1 = jnp.maximum(block, 0), jnp.minimum(block + 1, near - 1)
            back = lax.rem(LANES - at, LANES)
            keep = tile_lane < LANES - at
            turned = []
            for k in range(3):
                t = jnp.minimum(tile + k, 3)
                turned.append(pltpu.roll(jnp.where(upper_rows, cyclic[q0, t], cyclic[q1, t]), back, 1))
            for k in range(2):
                rows_out[to, pl.ds(8 * (2 * b + k), 8)] = jnp.where(keep, turned[k], turned[k + 1])
        @pl.when(to != level)
        def _():
            rows_copy(to, level).start()
        return carry

    lax.fori_loop(0, near, cut, 0)
    rows_in[pl.ds(pl.multiple_of(SPAN * level, SPAN), SPAN)] = rows_out[level]
    lax.fori_loop(FIRST, SECOND, more, 0)
    for step in FAR_FIRST:
        rows_copy(level, along(step)).wait_recv()

    def window_copy(to, origin):
        return pltpu.make_async_remote_copy(
            src_ref=windows.at[to],
            dst_ref=arrived.at[pl.ds(2 * lax.rem(origin, PARTS), 2), pl.ds(ROWS * lax.div(origin, PARTS), ROWS)],
            send_sem=w_send.at[to], recv_sem=w_recv.at[origin],
            device_id=device(to), device_id_type=MESH,
        )

    def share(b, carry):
        for plane in range(4):
            for k in range(2):
                for j in range(2):
                    rows_16[plane, k, pl.ds(j, 8, stride=2)] = (
                        rows_in[pl.ds(8 * (2 * b + k) + 2 * plane + j, 8, stride=SPAN)]
                    )
        for i in range(2):
            low = [rows_16[i, k] for k in range(2)]
            high = [pltpu.roll(rows_16[2 + i, k], 64, 1) for k in range(2)]
            for to in range(PARTS):
                windows[b * PARTS + to, i] = window(low, high, to)
        for to in range(PARTS):
            @pl.when(b * PARTS + to != me)
            def _():
                window_copy(b * PARTS + to, me).start()
        return carry

    lax.fori_loop(0, LOCAL, share, 0)
    arrived[pl.ds(2 * part, 2), pl.ds(ROWS * group, ROWS)] = windows[me]
    lax.fori_loop(SECOND, listing.shape[1] // CHUNK, more, 0)

    def prepare(field, slot, which):
        value = field[slot, pl.ds(2, PLANES), pl.ds(PAD, SPAN)].reshape(PLANES * SPAN, LANES)
        high = value.astype(BF16)
        rest = (value - high.astype(F32)).astype(BF16)
        dims = (((1,), (0,)), ((), ()))
        main = lax.dot_general(
            jnp.concatenate([high, rest], axis=1), bands[pl.ds(0, 2 * LANES)], dims, preferred_element_type=F32
        )
        minor = lax.dot_general(high, bands[pl.ds(2 * LANES, LANES), pl.ds(0, LANES)], dims, preferred_element_type=F32)
        along_y[which] = (main[:, :LANES] + minor).reshape(PLANES, SPAN, LANES)
        halves[which, pl.ds(2, PLANES)] = main[:, LANES:].reshape(PLANES, SPAN, LANES)

    def laplace(field, slot, which, e):
        result = []
        at = 2 + 2 * e

        def own(k):
            return field[slot, at + k, pl.ds(PAD, SPAN)]

        other = {k: jnp.where(lower, halves[which, at + k], halves[which, at + k + 2]) for k in (-2, -1, 0, 1)}
        along_z = (
            ((own(1), other[-1]), (other[0], other[-2]), (other[1], own(-1)), (own(2), own(-2))),
            ((other[0], own(0)), (other[1], other[-1]), (own(2), other[-2]), (own(3), own(-1))),
        )
        for i in range(2):
            total = 2.0 * stencil_weights[0] * own(i) + along_y[which, at + i - 2]
            for k in range(1, 5):
                some = along_z[i][k - 1][0] + along_z[i][k - 1][1]
                some = some + field[slot, at + i, pl.ds(PAD + k, SPAN)]
                some = some + field[slot, at + i, pl.ds(PAD - k, SPAN)]
                total = total + stencil_weights[k] * some
            result.append(total)
        return result

    def residual(k, p):
        return summed_r[pl.ds(pl.multiple_of(p * SPAN, SPAN), SPAN), pl.ds(LANES * k, LANES)]

    def to_lam(p, carry):
        lams[0, p + 2, pl.ds(PAD, SPAN)] = residual(0, p)
        return carry

    lax.fori_loop(0, PLANES, to_lam, 0)

    def ckpt_wait(k, carry):
        origin = lax.rem(part + k, PARTS)
        ckpt_copy(0, part, origin).wait_recv()
        ckpt_copy(1, part, origin).wait_recv()
        return carry

    lax.fori_loop(1, PARTS, ckpt_wait, 0)

    def ckpt_sent(k, carry):
        to = lax.rem(part + k, PARTS)
        ckpt_copy(0, to, part).wait_send()
        ckpt_copy(1, to, part).wait_send()
        return carry

    lax.fori_loop(1, PARTS, ckpt_sent, 0)
    for far in FAR_FIRST:
        model_copy(along(far), level).wait_send()
        rows_copy(along(far), level).wait_send()

    prepare(fields, 0, 0)
    prepare(lams, 0, 1)

    def first(e, carry):
        for which, field in ((0, fields), (1, lams)):
            for i, value in enumerate(laplace(field, 0, which, e)):
                first_lap[which, 2 * e + i] = value
        return carry

    lax.fori_loop(0, PARTS, first, 0)

    turn = offx[shot] & 63

    def make_c2v(k):
        e = lax.rem(part + k, PARTS)
        for b in range(LOCAL):
            @pl.when(b * PARTS + e != me)
            def _():
                window_copy(me, b * PARTS + e).wait_recv()
        for i in range(2):
            p = 2 * e + i
            rows = arrived[p]
            doubled[i, pl.ds(0, SPAN)] = rows
            doubled[i, pl.ds(SPAN, SPAN)] = rows
            speed = doubled[i, pl.ds(turn, SPAN)]
            speeds[p] = speed
            scaled = courant * speed
            c2v[p] = scaled * scaled
        return e

    flat = place[0]
    zc = lax.shift_right_logical(flat, 14)
    sy = (flat & 255) - (OWN * part - HALO)
    s_plane = lax.shift_right_logical(zc, 2) * 2 + (zc & 1)
    s_lane = jnp.where((sy >= 0) & (sy < 64), (lax.shift_right_logical(zc, 1) & 1) * 64 + sy, -1)
    at_source = (lane == s_lane) & (iota((SPAN, LANES), 0) == (lax.shift_right_logical(flat, 8) & 63))

    def accel_of(value, p, n):
        strength = jnp.where(p == s_plane, pulse[0, n], 0.0)
        return c2v[p] * value + jnp.where(at_source, strength, 0.0)

    inner = pl.ds(PAD, SPAN)

    def step_loop(n):
        now, old = n % 2, 1 - n % 2
        if n:
            prepare(fields, now, 0)
            if n < STEPS - 1:
                prepare(lams, n, 1)

        def step(e, carry):
            if not n:
                e = make_c2v(e)
            laps = laplace(fields, now, 0, e) if n else [first_lap[0, 2 * e + i] for i in range(2)]
            accel = [accel_of(laps[i], 2 * e + i, n) for i in range(2)]
            if n < STEPS - 1:
                laps = laplace(lams, n, 1, e) if n else [first_lap[1, 2 * e + i] for i in range(2)]
            for i in range(2):
                p = 2 * e + i
                if n < STEPS - 1:
                    fields[old, p + 2, inner] = (
                        2.0 * fields[now, p + 2, inner] - fields[old, p + 2, inner] + accel[i]
                    )
                    lam = lams[n, p + 2, inner]
                    newer = 2.0 * lam + c2v[p] * laps[i] + residual(n + 1, p)
                    if n:
                        newer = newer - lams[n - 1, p + 2, inner]
                if n < STEPS - 2:
                    accels[n, p] = accel[i]
                    lams[n + 1, p + 2, inner] = newer
                elif n == STEPS - 2:
                    partial[p] = newer * accels[0, p] + lam * accels[1, p] + lams[1, p + 2, inner] * accel[i]
            if n == STEPS - 1:
                send_parts(e, [
                    (partial[2 * e + i] + lams[0, 2 * e + i + 2, inner] * accel[i]) * 2.0 / speeds[2 * e + i]
                    for i in range(2)
                ])
            return carry

        if n < STEPS - 1:
            lax.fori_loop(0, PARTS, step, 0)
            return
        for piece in range(PIECES):
            lax.fori_loop(piece * PARTS // PIECES, (piece + 1) * PARTS // PIECES, step, 0)
            for far in FAR_FIRST:
                z_copy(along(far), level, piece).start()

    def send_parts(e, parts):
        both = jnp.where((lane & 63) < OWN, pltpu.roll(parts[0], LANES - HALO, 1), pltpu.roll(parts[1], OWN - HALO, 1))
        packed[e, pl.ds(0, SPAN)] = both
        packed[e, pl.ds(SPAN, SPAN)] = both
        outgoing[e] = packed[e, pl.ds((SPAN - turn) & 63, SPAN)]
        for to in range(near):
            for j in range(2):
                z_out[to, pl.ds(8 * e + 4 * j, 4)] = outgoing[e, pl.ds(2 * to + j, 4, stride=ROWS)]

    def z_copy(to, origin, piece):
        rows = SPAN // PIECES
        return pltpu.make_async_remote_copy(
            src_ref=z_out.at[to, pl.ds(rows * piece, rows)],
            dst_ref=z_in.at[pl.ds(SPAN * origin + rows * piece, rows)],
            send_sem=z_send.at[piece, to], recv_sem=z_recv.at[piece, origin],
            device_id=(LOCAL * to + group, part), device_id_type=MESH,
        )

    for n in range(STEPS):
        step_loop(n)
    z_in[pl.ds(pl.multiple_of(SPAN * level, SPAN), SPAN)] = z_out[level]

    def out_copy(to, origin):
        return pltpu.make_async_remote_copy(
            src_ref=outgoing_2.at[to], dst_ref=landed.at[origin],
            send_sem=o_send.at[to], recv_sem=o_recv.at[origin],
            device_id=device(to), device_id_type=MESH,
        )

    def out_start(e, carry):
        for b in range(LOCAL):
            for j in range(2):
                outgoing_2[b * PARTS + e, pl.ds(8 * j, 8)] = z_in[pl.ds(8 * e + 4 * j + b, 8, stride=SPAN)]
            @pl.when(b * PARTS + e != me)
            def _():
                out_copy(b * PARTS + e, me).start()
        return carry

    def windows_sent(k, carry):
        window_copy(lax.rem(me + k, peers), me).wait_send()
        return carry

    lax.fori_loop(1, peers, windows_sent, 0)
    for piece in range(PIECES):
        for far in FAR_FIRST:
            z_copy(level, along(far), piece).wait_recv()
        lax.fori_loop(piece * PARTS // PIECES, (piece + 1) * PARTS // PIECES, out_start, 0)
    landed[me] = outgoing_2[me]


    group_of = lax.shift_right_logical(tile_lane, 5)

    def put(k, carry):
        b = lax.rem(group + k, LOCAL)
        for c in range(PARTS):
            @pl.when(b * PARTS + c != me)
            def _():
                out_copy(me, b * PARTS + c).wait_recv()
        for j in range(2):
            for k in range(2):
                pieces = [landed[b * PARTS + 4 * k + c, pl.ds(8 * j, 8)] for c in range(4)]
                for plane in range(4):
                    total = None
                    for c in range(4):
                        by = (OWN * (c - plane)) % LANES
                        piece = pltpu.roll(pieces[c], by, 1) if by else pieces[c]
                        total = piece if total is None else jnp.where(group_of == c, piece, total)
                    by_shot[k, pl.ds(8 * (2 * plane + j), 8)] = total
        for z in range(near):
            at = offy[LOCAL * z + b] & 127
            keep = tile_lane >= at
            first, second = (pltpu.roll(by_shot[k, pl.ds(z, 8, stride=8)], at, 1) for k in range(2))
            placed[b * near + z, 2] = jnp.where(keep, first, 0.0)
            placed[b * near + z, 3] = jnp.where(keep, second, first)
            placed[b * near + z, 4] = jnp.where(keep, 0.0, second)
        return carry

    lax.fori_loop(0, LOCAL, put, 0)

    def add_up(k, sums):
        block, rest, tile, _ = spot(LOCAL * lax.rem(k, near) + lax.div(k, near))
        block = jnp.where(odd >= rest, block, block + 1)
        cells = placed[k, pl.ds(2 - tile, 4)]
        return tuple(total + jnp.where(block == q, cells, 0.0) for q, total in enumerate(sums))

    zero = jnp.zeros((4, 8, LANES), F32)
    for q, total in enumerate(lax.fori_loop(0, LOCAL * near, add_up, (zero,) * near)):
        totals[q] = total.reshape(OWN, LANES)

    def sum_copy(to, origin):
        return pltpu.make_async_remote_copy(
            src_ref=totals.at[to], dst_ref=sums.at[pl.ds(OWN * origin, OWN)],
            send_sem=s_send.at[to], recv_sem=s_recv.at[origin],
            device_id=(LOCAL * to + group, part), device_id_type=MESH,
        )

    for step in FAR_FIRST:
        sum_copy(along(step), level).start()
    sums[pl.ds(pl.multiple_of(OWN * level, OWN), OWN)] = totals[level]

    def outs_sent(k, carry):
        out_copy(lax.rem(me + k, peers), me).wait_send()
        return carry

    lax.fori_loop(1, peers, outs_sent, 0)
    for far in FAR_FIRST:
        for piece in range(PIECES):
            z_copy(along(far), level, piece).wait_send()
    for step in FAR_FIRST:
        sum_copy(level, along(step)).wait_recv()
    for plane in range(4):
        for tile in range(4):
            for j in range(2):
                final[plane, tile, pl.ds(j, near, stride=2)] = (
                    sums[pl.ds(8 * tile + 2 * plane + j, near, stride=OWN)]
                )
        speed = model[plane]
        total = jnp.concatenate([final[plane, tile] for tile in range(4)], axis=-1)
        scaling = (speed - lower_bound) * (upper_bound - speed) / (upper_bound - lower_bound)
        limit = barrier_weight / (upper_bound - speed) - barrier_weight / (speed - lower_bound)
        out[plane] = scaling * (total + limit)

    for far in FAR_FIRST:
        sum_copy(along(far), level).wait_send()


def on_device(near, model, offsets_x, offsets_y, ckpt_prev, ckpt_cur, wavelet, source, receivers, traces):
    peers = LOCAL * PARTS
    vmem = pl.BlockSpec(memory_space=pltpu.VMEM)
    smem = pl.BlockSpec(memory_space=pltpu.SMEM)
    padded = (PLANES + 4, SPAN + 2 * PAD, LANES)
    plain = (PLANES, SPAN, LANES)
    dma = pltpu.SemaphoreType.DMA
    return pl.pallas_call(
        functools.partial(kernel, near),
        out_shape=jax.ShapeDtypeStruct(model.shape, F32),
        in_specs=[smem] * 4 + [pl.BlockSpec(memory_space=pltpu.HBM)] * 5,
        out_specs=vmem,
        scratch_shapes=[
            *(pltpu.VMEM(a.shape, a.dtype) for a in (model, ckpt_prev, ckpt_cur, receivers, traces)),
            pltpu.VMEM((near, 4, 8, LANES), F32),
            pltpu.VMEM((near, 4, 8, LANES), F32),
            pltpu.VMEM((near, SPAN, LANES), F32),
            pltpu.VMEM((near * SPAN, LANES), F32),
            pltpu.VMEM((4, 2, ROWS, LANES), F32),
            pltpu.VMEM((2, PARTS, 2, SPAN, LANES), F32),
            pltpu.VMEM((2,) + padded, F32),
            pltpu.VMEM((3,) + padded, F32),
            pltpu.VMEM((3 * LANES, 2 * LANES), BF16),
            pltpu.VMEM((2,) + plain, F32),
            pltpu.VMEM((2, PLANES + 4, SPAN, LANES), F32),
            pltpu.VMEM((STEPS * LANES, 2 * CHUNK), BF16),
            pltpu.VMEM((PLANES * SPAN, STEPS * LANES), F32),
            pltpu.VMEM((peers, 2, ROWS, LANES), F32),
            pltpu.VMEM(plain, F32),
            pltpu.VMEM((2, 2 * SPAN, LANES), F32),
            pltpu.VMEM(plain, F32),
            pltpu.VMEM(plain, F32),
            pltpu.VMEM((2,) + plain, F32),
            pltpu.VMEM((2,) + plain, F32),
            pltpu.VMEM(plain, F32),
            pltpu.VMEM((PARTS, 2 * SPAN, LANES), F32),
            pltpu.VMEM((PARTS, SPAN, LANES), F32),
            pltpu.VMEM((near, SPAN, LANES), F32),
            pltpu.VMEM((near * SPAN, LANES), F32),
            pltpu.VMEM((peers, ROWS, LANES), F32),
            pltpu.VMEM((peers, ROWS, LANES), F32),
            pltpu.VMEM((2, SPAN, LANES), F32),
            pltpu.VMEM((LOCAL * near, 6, 8, LANES), F32),
            pltpu.VMEM((near, OWN, LANES), F32),
            pltpu.VMEM((near * OWN, LANES), F32),
            pltpu.VMEM((4, 4, ROWS, LANES), F32),
            dma((5,)),
            dma((near,)), dma((near,)), dma((near,)), dma((near,)),
            dma((2, PARTS)), dma((2, PARTS)),
            dma((peers,)), dma((peers,)), dma((peers,)), dma((peers,)),
            dma((PIECES, near)), dma((PIECES, near)), dma((near,)), dma((near,)),
        ],
        compiler_params=pltpu.CompilerParams(
            collective_id=0, has_side_effects=True, vmem_limit_bytes=62 * 1024 * 1024
        ),
    )(offsets_x, offsets_y, wavelet, source, model, ckpt_prev, ckpt_cur, receivers, traces)


def solution(mesh):
    placed = (
        P("depth", "shots", None),
        P(),
        P(),
        P("shots", "depth", None, None),
        P("shots", "depth", None, None),
        P("shots", None),
        P("shots"),
        P("shots", None),
        P("shots", None, None),
    )
    near = mesh.shape["shots"] // LOCAL
    return jax.shard_map(
        functools.partial(on_device, near),
        mesh=mesh, in_specs=placed, out_specs=P("depth", "shots", None), check_vma=False,
    )
```

```python
import functools

import jax
import jax.numpy as jnp
import numpy as np
from jax import lax
from jax.experimental import pallas as pl
from jax.experimental.pallas import tpu as pltpu
from jax.sharding import PartitionSpec as P

MESH = pl.DeviceIdType.MESH
F32 = jnp.float32
BF16 = jnp.bfloat16
STEPS = 4

stencil_weights = (-205.0 / 72.0, 8.0 / 5.0, -1.0 / 5.0, 8.0 / 315.0, -1.0 / 560.0)
courant = 0.095
lower_bound = 1.0
upper_bound = 5.0
barrier_weight = 0.5

PARTS = 8
LOCAL = 4
PLANES = 16
SPAN = 64
LANES = 128
ROWS = 16
HALO = 16
OWN = 32
CHUNK = 512
PAD = 8
FAR_FIRST = (4, 3, 5, 2, 6, 1, 7)
PIECES = 2
FIRST = 2
SECOND = 4


def iota(shape, dim):
    return lax.broadcasted_iota(jnp.int32, shape, dim)


def window(first, second, part):
    rows = first[0].shape[0]
    lane = iota((rows, LANES), 1)
    zero = jnp.zeros((rows, LANES), F32)
    start = OWN * part - HALO
    tile, at = start // LANES, start % LANES

    def pick(tiles, k):
        return tiles[k] if 0 <= k < 2 else zero

    if at <= 64:
        low = pick(first, tile)
        in_low = (lane >= at) & (lane < at + 64)
        high = pick(second, tile)
    else:
        low = jnp.where(lane >= at, pick(first, tile), pick(first, tile + 1))
        in_low = (lane >= at) | (lane < at - 64)
        own = (lane + 64) % LANES
        high = jnp.where(own >= at, pick(second, tile), pick(second, tile + 1))
    both = jnp.where(in_low, low, high)
    return pltpu.roll(both, (LANES - at) % LANES, 1) if at else both


def make_bands(bands):
    r, c = iota((LANES, LANES), 0), iota((LANES, LANES), 1)
    distance = jnp.where((r < 64) == (c < 64), jnp.abs(r - c), LANES)
    main = jnp.zeros((LANES, LANES), F32)
    rest = main
    for k, weight in enumerate(stencil_weights):
        rounded = float(np.float32(weight).astype(BF16))
        main = jnp.where(distance == k, rounded, main)
        rest = jnp.where(distance == k, float(np.float32(weight)) - rounded, rest)
    swap = (jnp.abs(r - c) == 64).astype(F32).astype(BF16)
    for half in range(2):
        bands[pl.ds(LANES * half, LANES), pl.ds(0, LANES)] = main.astype(BF16)
        bands[pl.ds(LANES * half, LANES), pl.ds(LANES, LANES)] = swap
    bands[pl.ds(2 * LANES, LANES), pl.ds(0, LANES)] = rest.astype(BF16)
    bands[pl.ds(2 * LANES, LANES), pl.ds(LANES, LANES)] = jnp.zeros((LANES, LANES), BF16)


def kernel(
    near,
    offx, offy, pulse, place, model_in, prev_in, cur_in, listing_in, record_in,
    out,
    model, prev, cur, listing, record,
    m_out, cyclic, rows_out, rows_in, rows_16, stage, fields, lams, bands, along_y, halves, onto, summed_r, windows, arrived, doubled, speeds, c2v, first_lap,
    accels, partial, packed, outgoing, z_out, z_in, outgoing_2, landed, by_shot, placed, totals, sums, final,
    in_sems,
    m_send, m_recv, r_send, r_recv, ck_send, ck_recv, w_send, w_recv, o_send, o_recv,
    z_send, z_recv, s_send, s_recv,
):
    shot = lax.axis_index("shots")
    part = lax.axis_index("depth")
    level = lax.div(shot, LOCAL)
    group = lax.rem(shot, LOCAL)
    me = group * PARTS + part
    peers = LOCAL * PARTS
    lane = iota((SPAN, LANES), 1)
    lower = lane < 64

    def along(step):
        return lax.rem(level + step, near)

    def device(k):
        return (LOCAL * level + lax.div(k, PARTS), lax.rem(k, PARTS))

    inputs = [
        pltpu.make_async_copy(model_in, model, in_sems.at[0]),
        pltpu.make_async_copy(cur_in, cur, in_sems.at[1]),
        pltpu.make_async_copy(prev_in, prev, in_sems.at[2]),
        pltpu.make_async_copy(listing_in, listing, in_sems.at[3]),
        pltpu.make_async_copy(record_in, record, in_sems.at[4]),
    ]
    for copy in inputs:
        copy.start()

    barrier = pltpu.get_barrier_semaphore()

    def greet(k, carry):
        pl.semaphore_signal(barrier, inc=1, device_id=device(lax.rem(me + k, peers)), device_id_type=MESH)
        return carry

    for step in FAR_FIRST:
        pl.semaphore_signal(barrier, inc=1, device_id=(LOCAL * along(step) + group, part), device_id_type=MESH)
    lax.fori_loop(1, peers, greet, 0)

    inputs[0].wait()
    for to in range(near):
        for tile in range(4):
            for plane in range(4):
                m_out[to, tile, pl.ds(2 * plane, 2)] = model[plane, pl.ds(2 * to, 2), pl.ds(LANES * tile, LANES)]
    pl.semaphore_wait(barrier, peers - 1 + len(FAR_FIRST))

    def model_copy(to, origin):
        return pltpu.make_async_remote_copy(
            src_ref=m_out.at[to], dst_ref=cyclic.at[origin],
            send_sem=m_send.at[to], recv_sem=m_recv.at[origin],
            device_id=(LOCAL * to + group, part), device_id_type=MESH,
        )

    def rows_copy(to, origin):
        return pltpu.make_async_remote_copy(
            src_ref=rows_out.at[to], dst_ref=rows_in.at[pl.ds(SPAN * origin, SPAN)],
            send_sem=r_send.at[to], recv_sem=r_recv.at[origin],
            device_id=(LOCAL * to + group, part), device_id_type=MESH,
        )

    def ckpt_copy(which, to, origin):
        return pltpu.make_async_remote_copy(
            src_ref=stage.at[which, to],
            dst_ref=fields.at[which, pl.ds(2 + 2 * origin, 2), pl.ds(PAD, SPAN)],
            send_sem=ck_send.at[which, to], recv_sem=ck_recv.at[which, origin],
            device_id=(shot, to), device_id_type=MESH,
        )

    for step in FAR_FIRST:
        model_copy(along(step), level).start()
    cyclic[level] = m_out[level]

    for which, source in ((0, cur), (1, prev)):
        inputs[1 + which].wait()
        for i in range(2):
            low = [source[0, i, :, pl.ds(LANES * k, LANES)] for k in range(2)]
            high = [pltpu.roll(source[0, 2 + i, :, pl.ds(LANES * k, LANES)], 64, 1) for k in range(2)]
            for to in range(PARTS):
                stage[which, to, i] = window(low, high, to)

        def ckpt_start(k, carry, which=which):
            ckpt_copy(which, lax.rem(part + k, PARTS), part).start()
            return carry

        lax.fori_loop(1, PARTS, ckpt_start, 0)

    make_bands(bands)

    for edge in (0, 1, PLANES + 2, PLANES + 3):
        for which in range(2):
            halves[which, edge] = jnp.zeros((SPAN, LANES), F32)
    for ref, slots in ((fields, 2), (lams, 3)):
        for slot in range(slots):
            for edge in (0, 1, PLANES + 2, PLANES + 3):
                ref[slot, edge] = jnp.zeros((SPAN + 2 * PAD, LANES), F32)
            for edge in range(2, PLANES + 2):
                ref[slot, edge, pl.ds(0, PAD)] = jnp.zeros((PAD, LANES), F32)
                ref[slot, edge, pl.ds(PAD + SPAN, PAD)] = jnp.zeros((PAD, LANES), F32)
    for which in range(2):
        fields[which, pl.ds(2 + 2 * part, 2), pl.ds(PAD, SPAN)] = stage[which, part]
    for tile in (0, 1, 5):
        placed[:, tile] = jnp.zeros((LOCAL * near, 8, LANES), F32)

    summed_r[...] = jnp.zeros(summed_r.shape, F32)

    def receivers(step):
        at = pl.ds(pl.multiple_of(step * CHUNK, CHUNK), CHUNK)
        flat = listing[:, at]
        zc = lax.shift_right_logical(flat, 14)
        x = lax.shift_right_logical(flat, 8) & 63
        y = (flat & 255) - (OWN * part - HALO)
        row = (lax.shift_right_logical(zc, 2) * 2 + (zc & 1)) * SPAN + x
        column = jnp.where((y >= 0) & (y < 64), (lax.shift_right_logical(zc, 1) & 1) * 64 + y, -1)
        hot = (iota((PLANES * SPAN, CHUNK), 0) == row).astype(F32).astype(BF16)
        match = iota((LANES, CHUNK), 0) == column
        for k in range(STEPS):
            value = record[0, pl.ds(k, 1), at]
            high = value.astype(BF16).astype(F32)
            rest = value - high
            onto[pl.ds(LANES * k, LANES), pl.ds(0, CHUNK)] = jnp.where(match, high, 0.0).astype(BF16)
            onto[pl.ds(LANES * k, LANES), pl.ds(CHUNK, CHUNK)] = jnp.where(match, rest, 0.0).astype(BF16)
        dims = (((1,), (1,)), ((), ()))
        both = jnp.concatenate([hot, hot], axis=1)
        summed_r[...] += lax.dot_general(both, onto[...], dims, preferred_element_type=F32)

    def more(step, carry):
        receivers(step)
        return carry

    inputs[3].wait()
    inputs[4].wait()
    lax.fori_loop(0, FIRST, more, 0)

    for step in FAR_FIRST:
        model_copy(level, along(step)).wait_recv()

    tile_lane = iota((8, LANES), 1)
    odd = iota((8, LANES), 0) & 1

    def spot(shot_k):
        t = offx[shot_k] - (ROWS * group + 2 * level) + SPAN
        oy = offy[shot_k]
        return lax.shift_right_logical(t, 6) - 1, t & 63, lax.shift_right_logical(oy, 7), oy & 127

    def cut(step, carry):
        to = lax.rem(level + near + lax.div(near - step, 2) * (1 - 2 * lax.rem(step, 2)), near)
        for b in range(LOCAL):
            block, rest, tile, at = spot(LOCAL * to + b)
            upper_rows = odd >= rest
            q0, q1 = jnp.maximum(block, 0), jnp.minimum(block + 1, near - 1)
            back = lax.rem(LANES - at, LANES)
            keep = tile_lane < LANES - at
            turned = []
            for k in range(3):
                t = jnp.minimum(tile + k, 3)
                turned.append(pltpu.roll(jnp.where(upper_rows, cyclic[q0, t], cyclic[q1, t]), back, 1))
            for k in range(2):
                rows_out[to, pl.ds(8 * (2 * b + k), 8)] = jnp.where(keep, turned[k], turned[k + 1])
        @pl.when(to != level)
        def _():
            rows_copy(to, level).start()
        return carry

    lax.fori_loop(0, near, cut, 0)
    rows_in[pl.ds(pl.multiple_of(SPAN * level, SPAN), SPAN)] = rows_out[level]
    lax.fori_loop(FIRST, SECOND, more, 0)
    for step in FAR_FIRST:
        rows_copy(level, along(step)).wait_recv()

    def window_copy(to, origin):
        return pltpu.make_async_remote_copy(
            src_ref=windows.at[to],
            dst_ref=arrived.at[pl.ds(2 * lax.rem(origin, PARTS), 2), pl.ds(ROWS * lax.div(origin, PARTS), ROWS)],
            send_sem=w_send.at[to], recv_sem=w_recv.at[origin],
            device_id=device(to), device_id_type=MESH,
        )

    def share(b, carry):
        for plane in range(4):
            for k in range(2):
                for j in range(2):
                    rows_16[plane, k, pl.ds(j, 8, stride=2)] = (
                        rows_in[pl.ds(8 * (2 * b + k) + 2 * plane + j, 8, stride=SPAN)]
                    )
        for i in range(2):
            low = [rows_16[i, k, pl.ds(0, ROWS)] for k in range(2)]
            high = [pltpu.roll(rows_16[2 + i, k, pl.ds(0, ROWS)], 64, 1) for k in range(2)]
            for to in range(PARTS):
                windows[b * PARTS + to, i] = window(low, high, to)
        for to in range(PARTS):
            @pl.when(b * PARTS + to != me)
            def _():
                window_copy(b * PARTS + to, me).start()
        return carry

    lax.fori_loop(0, LOCAL, share, 0)
    arrived[pl.ds(2 * part, 2), pl.ds(ROWS * group, ROWS)] = windows[me]
    lax.fori_loop(SECOND, listing.shape[1] // CHUNK, more, 0)

    def prepare(field, slot, which):
        value = field[slot, pl.ds(2, PLANES), pl.ds(PAD, SPAN)].reshape(PLANES * SPAN, LANES)
        high = value.astype(BF16)
        rest = (value - high.astype(F32)).astype(BF16)
        dims = (((1,), (0,)), ((), ()))
        main = lax.dot_general(
            jnp.concatenate([high, rest], axis=1), bands[pl.ds(0, 2 * LANES)], dims, preferred_element_type=F32
        )
        minor = lax.dot_general(high, bands[pl.ds(2 * LANES, LANES), pl.ds(0, LANES)], dims, preferred_element_type=F32)
        along_y[which] = (main[:, :LANES] + minor).reshape(PLANES, SPAN, LANES)
        halves[which, pl.ds(2, PLANES)] = main[:, LANES:].reshape(PLANES, SPAN, LANES)

    def laplace(field, slot, which, e):
        result = []
        at = 2 + 2 * e

        def own(k):
            return field[slot, at + k, pl.ds(PAD, SPAN)]

        other = {k: jnp.where(lower, halves[which, at + k], halves[which, at + k + 2]) for k in (-2, -1, 0, 1)}
        along_z = (
            ((own(1), other[-1]), (other[0], other[-2]), (other[1], own(-1)), (own(2), own(-2))),
            ((other[0], own(0)), (other[1], other[-1]), (own(2), other[-2]), (own(3), own(-1))),
        )
        for i in range(2):
            total = 2.0 * stencil_weights[0] * own(i) + along_y[which, at + i - 2]
            for k in range(1, 5):
                some = along_z[i][k - 1][0] + along_z[i][k - 1][1]
                some = some + field[slot, at + i, pl.ds(PAD + k, SPAN)]
                some = some + field[slot, at + i, pl.ds(PAD - k, SPAN)]
                total = total + stencil_weights[k] * some
            result.append(total)
        return result

    def residual(k, p):
        return summed_r[pl.ds(pl.multiple_of(p * SPAN, SPAN), SPAN), pl.ds(LANES * k, LANES)]

    def to_lam(p, carry):
        lams[0, p + 2, pl.ds(PAD, SPAN)] = residual(0, p)
        return carry

    lax.fori_loop(0, PLANES, to_lam, 0)

    def ckpt_wait(which):
        def one(k, carry):
            ckpt_copy(which, part, lax.rem(part + k, PARTS)).wait_recv()
            return carry

        lax.fori_loop(1, PARTS, one, 0)

    ckpt_wait(0)

    def ckpt_sent(k, carry):
        to = lax.rem(part + k, PARTS)
        ckpt_copy(0, to, part).wait_send()
        ckpt_copy(1, to, part).wait_send()
        return carry

    prepare(fields, 0, 0)
    prepare(lams, 0, 1)

    def first(e, carry):
        for which, field in ((0, fields), (1, lams)):
            for i, value in enumerate(laplace(field, 0, which, e)):
                first_lap[which, 2 * e + i] = value
        return carry

    lax.fori_loop(0, PARTS, first, 0)

    ckpt_wait(1)
    lax.fori_loop(1, PARTS, ckpt_sent, 0)
    for far in FAR_FIRST:
        model_copy(along(far), level).wait_send()
        rows_copy(along(far), level).wait_send()

    turn = offx[shot] & 63

    def make_c2v(k):
        e = lax.rem(part + k, PARTS)
        for b in range(LOCAL):
            @pl.when(b * PARTS + e != me)
            def _():
                window_copy(me, b * PARTS + e).wait_recv()
        for i in range(2):
            p = 2 * e + i
            rows = arrived[p]
            doubled[i, pl.ds(0, SPAN)] = rows
            doubled[i, pl.ds(SPAN, SPAN)] = rows
            speed = doubled[i, pl.ds(turn, SPAN)]
            speeds[p] = speed
            scaled = courant * speed
            c2v[p] = scaled * scaled
        return e

    flat = place[0]
    zc = lax.shift_right_logical(flat, 14)
    sy = (flat & 255) - (OWN * part - HALO)
    s_plane = lax.shift_right_logical(zc, 2) * 2 + (zc & 1)
    s_lane = jnp.where((sy >= 0) & (sy < 64), (lax.shift_right_logical(zc, 1) & 1) * 64 + sy, -1)
    at_source = (lane == s_lane) & (iota((SPAN, LANES), 0) == (lax.shift_right_logical(flat, 8) & 63))

    def accel_of(value, p, n):
        strength = jnp.where(p == s_plane, pulse[0, n], 0.0)
        return c2v[p] * value + jnp.where(at_source, strength, 0.0)

    inner = pl.ds(PAD, SPAN)

    def step_loop(n):
        now, old = n % 2, 1 - n % 2
        if n:
            prepare(fields, now, 0)
            if n < STEPS - 1:
                prepare(lams, n, 1)

        def step(e, carry):
            if not n:
                e = make_c2v(e)
            laps = laplace(fields, now, 0, e) if n else [first_lap[0, 2 * e + i] for i in range(2)]
            accel = [accel_of(laps[i], 2 * e + i, n) for i in range(2)]
            if n < STEPS - 1:
                laps = laplace(lams, n, 1, e) if n else [first_lap[1, 2 * e + i] for i in range(2)]
            for i in range(2):
                p = 2 * e + i
                if n < STEPS - 1:
                    fields[old, p + 2, inner] = (
                        2.0 * fields[now, p + 2, inner] - fields[old, p + 2, inner] + accel[i]
                    )
                    lam = lams[n, p + 2, inner]
                    newer = 2.0 * lam + c2v[p] * laps[i] + residual(n + 1, p)
                    if n:
                        newer = newer - lams[n - 1, p + 2, inner]
                if n < STEPS - 2:
                    accels[n, p] = accel[i]
                    lams[n + 1, p + 2, inner] = newer
                elif n == STEPS - 2:
                    partial[p] = newer * accels[0, p] + lam * accels[1, p] + lams[1, p + 2, inner] * accel[i]
            if n == STEPS - 1:
                send_parts(e, [
                    (partial[2 * e + i] + lams[0, 2 * e + i + 2, inner] * accel[i]) * 2.0 / speeds[2 * e + i]
                    for i in range(2)
                ])
            return carry

        if n < STEPS - 1:
            lax.fori_loop(0, PARTS, step, 0)
            return
        for piece in range(PIECES):
            lax.fori_loop(piece * PARTS // PIECES, (piece + 1) * PARTS // PIECES, step, 0)
            for far in FAR_FIRST:
                z_copy(along(far), level, piece).start()

    def send_parts(e, parts):
        both = jnp.where((lane & 63) < OWN, pltpu.roll(parts[0], LANES - HALO, 1), pltpu.roll(parts[1], OWN - HALO, 1))
        packed[e, pl.ds(0, SPAN)] = both
        packed[e, pl.ds(SPAN, SPAN)] = both
        outgoing[e, pl.ds(0, SPAN)] = packed[e, pl.ds((SPAN - turn) & 63, SPAN)]
        for to in range(near):
            for j in range(2):
                z_out[to, pl.ds(8 * e + 4 * j, 4)] = outgoing[e, pl.ds(2 * to + j, 4, stride=ROWS)]

    def z_copy(to, origin, piece):
        rows = SPAN // PIECES
        return pltpu.make_async_remote_copy(
            src_ref=z_out.at[to, pl.ds(rows * piece, rows)],
            dst_ref=z_in.at[pl.ds(SPAN * origin + rows * piece, rows)],
            send_sem=z_send.at[piece, to], recv_sem=z_recv.at[piece, origin],
            device_id=(LOCAL * to + group, part), device_id_type=MESH,
        )

    for n in range(STEPS):
        step_loop(n)
    z_in[pl.ds(pl.multiple_of(SPAN * level, SPAN), SPAN)] = z_out[level]

    def out_copy(to, origin):
        return pltpu.make_async_remote_copy(
            src_ref=outgoing_2.at[to], dst_ref=landed.at[origin],
            send_sem=o_send.at[to], recv_sem=o_recv.at[origin],
            device_id=device(to), device_id_type=MESH,
        )

    def out_start(e, carry):
        for b in range(LOCAL):
            for j in range(2):
                outgoing_2[b * PARTS + e, pl.ds(8 * j, 8)] = z_in[pl.ds(8 * e + 4 * j + b, 8, stride=SPAN)]
            @pl.when(b * PARTS + e != me)
            def _():
                out_copy(b * PARTS + e, me).start()
        return carry

    def windows_sent(k, carry):
        window_copy(lax.rem(me + k, peers), me).wait_send()
        return carry

    lax.fori_loop(1, peers, windows_sent, 0)
    for piece in range(PIECES):
        for far in FAR_FIRST:
            z_copy(level, along(far), piece).wait_recv()
        lax.fori_loop(piece * PARTS // PIECES, (piece + 1) * PARTS // PIECES, out_start, 0)
    landed[me] = outgoing_2[me]


    group_of = lax.shift_right_logical(tile_lane, 5)

    def put(k, carry):
        b = lax.rem(group + k, LOCAL)
        for c in range(PARTS):
            @pl.when(b * PARTS + c != me)
            def _():
                out_copy(me, b * PARTS + c).wait_recv()
        for j in range(2):
            for k in range(2):
                pieces = [landed[b * PARTS + 4 * k + c, pl.ds(8 * j, 8)] for c in range(4)]
                for plane in range(4):
                    total = None
                    for c in range(4):
                        by = (OWN * (c - plane)) % LANES
                        piece = pltpu.roll(pieces[c], by, 1) if by else pieces[c]
                        total = piece if total is None else jnp.where(group_of == c, piece, total)
                    by_shot[k, pl.ds(8 * (2 * plane + j), 8)] = total
        for z in range(near):
            at = offy[LOCAL * z + b] & 127
            keep = tile_lane >= at
            first, second = (pltpu.roll(by_shot[k, pl.ds(z, 8, stride=8)], at, 1) for k in range(2))
            placed[b * near + z, 2] = jnp.where(keep, first, 0.0)
            placed[b * near + z, 3] = jnp.where(keep, second, first)
            placed[b * near + z, 4] = jnp.where(keep, 0.0, second)
        return carry

    lax.fori_loop(0, LOCAL, put, 0)

    def add_up(k, sums):
        block, rest, tile, _ = spot(LOCAL * lax.rem(k, near) + lax.div(k, near))
        block = jnp.where(odd >= rest, block, block + 1)
        cells = placed[k, pl.ds(2 - tile, 4)]
        return tuple(total + jnp.where(block == q, cells, 0.0) for q, total in enumerate(sums))

    zero = jnp.zeros((4, 8, LANES), F32)
    for q, total in enumerate(lax.fori_loop(0, LOCAL * near, add_up, (zero,) * near)):
        totals[q] = total.reshape(OWN, LANES)

    def sum_copy(to, origin):
        return pltpu.make_async_remote_copy(
            src_ref=totals.at[to], dst_ref=sums.at[pl.ds(OWN * origin, OWN)],
            send_sem=s_send.at[to], recv_sem=s_recv.at[origin],
            device_id=(LOCAL * to + group, part), device_id_type=MESH,
        )

    for step in FAR_FIRST:
        sum_copy(along(step), level).start()
    sums[pl.ds(pl.multiple_of(OWN * level, OWN), OWN)] = totals[level]

    def outs_sent(k, carry):
        out_copy(lax.rem(me + k, peers), me).wait_send()
        return carry

    lax.fori_loop(1, peers, outs_sent, 0)
    for far in FAR_FIRST:
        for piece in range(PIECES):
            z_copy(along(far), level, piece).wait_send()
    for step in FAR_FIRST:
        sum_copy(level, along(step)).wait_recv()
    for plane in range(4):
        for tile in range(4):
            for j in range(2):
                final[plane, tile, pl.ds(j, near, stride=2)] = (
                    sums[pl.ds(8 * tile + 2 * plane + j, near, stride=OWN)]
                )
        speed = model[plane]
        total = jnp.concatenate([final[plane, tile, pl.ds(0, ROWS)] for tile in range(4)], axis=-1)
        scaling = (speed - lower_bound) * (upper_bound - speed) / (upper_bound - lower_bound)
        limit = barrier_weight / (upper_bound - speed) - barrier_weight / (speed - lower_bound)
        out[plane] = scaling * (total + limit)

    for far in FAR_FIRST:
        sum_copy(along(far), level).wait_send()


def on_device(near, model, offsets_x, offsets_y, ckpt_prev, ckpt_cur, wavelet, source, receivers, traces):
    peers = LOCAL * PARTS
    vmem = pl.BlockSpec(memory_space=pltpu.VMEM)
    smem = pl.BlockSpec(memory_space=pltpu.SMEM)
    padded = (PLANES + 4, SPAN + 2 * PAD, LANES)
    plain = (PLANES, SPAN, LANES)
    dma = pltpu.SemaphoreType.DMA
    return pl.pallas_call(
        functools.partial(kernel, near),
        out_shape=jax.ShapeDtypeStruct(model.shape, F32),
        in_specs=[smem] * 4 + [pl.BlockSpec(memory_space=pltpu.HBM)] * 5,
        out_specs=vmem,
        scratch_shapes=[
            *(pltpu.VMEM(a.shape, a.dtype) for a in (model, ckpt_prev, ckpt_cur, receivers, traces)),
            pltpu.VMEM((near, 4, 8, LANES), F32),
            pltpu.VMEM((near, 4, 8, LANES), F32),
            pltpu.VMEM((near, SPAN, LANES), F32),
            pltpu.VMEM((near * SPAN + SPAN, LANES), F32),
            pltpu.VMEM((4, 2, ROWS + PAD, LANES), F32),
            pltpu.VMEM((2, PARTS, 2, SPAN, LANES), F32),
            pltpu.VMEM((2,) + padded, F32),
            pltpu.VMEM((3,) + padded, F32),
            pltpu.VMEM((3 * LANES, 2 * LANES), BF16),
            pltpu.VMEM((2,) + plain, F32),
            pltpu.VMEM((2, PLANES + 4, SPAN, LANES), F32),
            pltpu.VMEM((STEPS * LANES, 2 * CHUNK), BF16),
            pltpu.VMEM((PLANES * SPAN, STEPS * LANES), F32),
            pltpu.VMEM((peers, 2, ROWS, LANES), F32),
            pltpu.VMEM(plain, F32),
            pltpu.VMEM((2, 2 * SPAN, LANES), F32),
            pltpu.VMEM(plain, F32),
            pltpu.VMEM(plain, F32),
            pltpu.VMEM((2,) + plain, F32),
            pltpu.VMEM((2,) + plain, F32),
            pltpu.VMEM(plain, F32),
            pltpu.VMEM((PARTS, 2 * SPAN, LANES), F32),
            pltpu.VMEM((PARTS, SPAN + ROWS, LANES), F32),
            pltpu.VMEM((near, SPAN, LANES), F32),
            pltpu.VMEM((near * SPAN + SPAN, LANES), F32),
            pltpu.VMEM((peers, ROWS, LANES), F32),
            pltpu.VMEM((peers, ROWS, LANES), F32),
            pltpu.VMEM((2, SPAN + PAD, LANES), F32),
            pltpu.VMEM((LOCAL * near, 6, 8, LANES), F32),
            pltpu.VMEM((near, OWN, LANES), F32),
            pltpu.VMEM((near * OWN + OWN, LANES), F32),
            pltpu.VMEM((4, 4, ROWS + PAD, LANES), F32),
            dma((5,)),
            dma((near,)), dma((near,)), dma((near,)), dma((near,)),
            dma((2, PARTS)), dma((2, PARTS)),
            dma((peers,)), dma((peers,)), dma((peers,)), dma((peers,)),
            dma((PIECES, near)), dma((PIECES, near)), dma((near,)), dma((near,)),
        ],
        compiler_params=pltpu.CompilerParams(
            collective_id=0, has_side_effects=True, vmem_limit_bytes=62 * 1024 * 1024
        ),
    )(offsets_x, offsets_y, wavelet, source, model, ckpt_prev, ckpt_cur, receivers, traces)


def solution(mesh):
    placed = (
        P("depth", "shots", None),
        P(),
        P(),
        P("shots", "depth", None, None),
        P("shots", "depth", None, None),
        P("shots", None),
        P("shots"),
        P("shots", None),
        P("shots", None, None),
    )
    near = mesh.shape["shots"] // LOCAL
    return jax.shard_map(
        functools.partial(on_device, near),
        mesh=mesh, in_specs=placed, out_specs=P("depth", "shots", None), check_vma=False,
    )
```

```python
import functools

import jax
import jax.numpy as jnp
import numpy as np
from jax import lax
from jax.experimental import pallas as pl
from jax.experimental.pallas import tpu as pltpu
from jax.sharding import PartitionSpec as P

MESH = pl.DeviceIdType.MESH
F32 = jnp.float32
BF16 = jnp.bfloat16
STEPS = 4

stencil_weights = (-205.0 / 72.0, 8.0 / 5.0, -1.0 / 5.0, 8.0 / 315.0, -1.0 / 560.0)
courant = 0.095
lower_bound = 1.0
upper_bound = 5.0
barrier_weight = 0.5

PARTS = 8
LOCAL = 4
PLANES = 16
SPAN = 64
LANES = 128
ROWS = 16
HALO = 16
OWN = 32
CHUNK = 512
PAD = 8
FAR_FIRST = (4, 3, 5, 2, 6, 1, 7)
PIECES = 4
FIRST = 2
SECOND = 4


def iota(shape, dim):
    return lax.broadcasted_iota(jnp.int32, shape, dim)


def window(first, second, part):
    rows = first[0].shape[0]
    lane = iota((rows, LANES), 1)
    zero = jnp.zeros((rows, LANES), F32)
    start = OWN * part - HALO
    tile, at = start // LANES, start % LANES

    def pick(tiles, k):
        return tiles[k] if 0 <= k < 2 else zero

    if at <= 64:
        low = pick(first, tile)
        in_low = (lane >= at) & (lane < at + 64)
        high = pick(second, tile)
    else:
        low = jnp.where(lane >= at, pick(first, tile), pick(first, tile + 1))
        in_low = (lane >= at) | (lane < at - 64)
        own = (lane + 64) % LANES
        high = jnp.where(own >= at, pick(second, tile), pick(second, tile + 1))
    both = jnp.where(in_low, low, high)
    return pltpu.roll(both, (LANES - at) % LANES, 1) if at else both


def make_bands(bands):
    r, c = iota((LANES, LANES), 0), iota((LANES, LANES), 1)
    distance = jnp.where((r < 64) == (c < 64), jnp.abs(r - c), LANES)
    main = jnp.zeros((LANES, LANES), F32)
    rest = main
    for k, weight in enumerate(stencil_weights):
        rounded = float(np.float32(weight).astype(BF16))
        main = jnp.where(distance == k, rounded, main)
        rest = jnp.where(distance == k, float(np.float32(weight)) - rounded, rest)
    swap = (jnp.abs(r - c) == 64).astype(F32).astype(BF16)
    for half in range(2):
        bands[pl.ds(LANES * half, LANES), pl.ds(0, LANES)] = main.astype(BF16)
        bands[pl.ds(LANES * half, LANES), pl.ds(LANES, LANES)] = swap
    bands[pl.ds(2 * LANES, LANES), pl.ds(0, LANES)] = rest.astype(BF16)
    bands[pl.ds(2 * LANES, LANES), pl.ds(LANES, LANES)] = jnp.zeros((LANES, LANES), BF16)


def kernel(
    near,
    offx, offy, pulse, place, model_in, prev_in, cur_in, listing_in, record_in,
    out,
    model, prev, cur, listing, record,
    m_out, cyclic, rows_out, rows_in, rows_16, stage, fields, lams, bands, along_y, halves, onto, summed_r, windows, arrived, doubled, speeds, c2v, first_lap,
    accels, partial, packed, outgoing, z_out, z_in, outgoing_2, landed, by_shot, placed, totals, sums, final,
    in_sems,
    m_send, m_recv, r_send, r_recv, ck_send, ck_recv, w_send, w_recv, o_send, o_recv,
    z_send, z_recv, s_send, s_recv,
):
    shot = lax.axis_index("shots")
    part = lax.axis_index("depth")
    level = lax.div(shot, LOCAL)
    group = lax.rem(shot, LOCAL)
    me = group * PARTS + part
    peers = LOCAL * PARTS
    lane = iota((SPAN, LANES), 1)
    lower = lane < 64

    def along(step):
        return lax.rem(level + step, near)

    def device(k):
        return (LOCAL * level + lax.div(k, PARTS), lax.rem(k, PARTS))

    inputs = [
        pltpu.make_async_copy(model_in, model, in_sems.at[0]),
        pltpu.make_async_copy(cur_in, cur, in_sems.at[1]),
        pltpu.make_async_copy(prev_in, prev, in_sems.at[2]),
        pltpu.make_async_copy(listing_in, listing, in_sems.at[3]),
        pltpu.make_async_copy(record_in, record, in_sems.at[4]),
    ]
    for copy in inputs:
        copy.start()

    barrier = pltpu.get_barrier_semaphore()

    def greet(k, carry):
        pl.semaphore_signal(barrier, inc=1, device_id=device(lax.rem(me + k, peers)), device_id_type=MESH)
        return carry

    for step in FAR_FIRST:
        pl.semaphore_signal(barrier, inc=1, device_id=(LOCAL * along(step) + group, part), device_id_type=MESH)
    lax.fori_loop(1, peers, greet, 0)

    inputs[0].wait()
    for to in range(near):
        for tile in range(4):
            for plane in range(4):
                m_out[to, tile, pl.ds(2 * plane, 2)] = model[plane, pl.ds(2 * to, 2), pl.ds(LANES * tile, LANES)]
    pl.semaphore_wait(barrier, peers - 1 + len(FAR_FIRST))

    def model_copy(to, origin):
        return pltpu.make_async_remote_copy(
            src_ref=m_out.at[to], dst_ref=cyclic.at[origin],
            send_sem=m_send.at[to], recv_sem=m_recv.at[origin],
            device_id=(LOCAL * to + group, part), device_id_type=MESH,
        )

    def rows_copy(to, origin):
        return pltpu.make_async_remote_copy(
            src_ref=rows_out.at[to], dst_ref=rows_in.at[pl.ds(SPAN * origin, SPAN)],
            send_sem=r_send.at[to], recv_sem=r_recv.at[origin],
            device_id=(LOCAL * to + group, part), device_id_type=MESH,
        )

    def ckpt_copy(which, to, origin):
        return pltpu.make_async_remote_copy(
            src_ref=stage.at[which, to],
            dst_ref=fields.at[which, pl.ds(2 + 2 * origin, 2), pl.ds(PAD, SPAN)],
            send_sem=ck_send.at[which, to], recv_sem=ck_recv.at[which, origin],
            device_id=(shot, to), device_id_type=MESH,
        )

    for step in FAR_FIRST:
        model_copy(along(step), level).start()
    cyclic[level] = m_out[level]

    for which, source in ((0, cur), (1, prev)):
        inputs[1 + which].wait()
        for i in range(2):
            low = [source[0, i, :, pl.ds(LANES * k, LANES)] for k in range(2)]
            high = [pltpu.roll(source[0, 2 + i, :, pl.ds(LANES * k, LANES)], 64, 1) for k in range(2)]
            for to in range(PARTS):
                stage[which, to, i] = window(low, high, to)

        def ckpt_start(k, carry, which=which):
            ckpt_copy(which, lax.rem(part + k, PARTS), part).start()
            return carry

        lax.fori_loop(1, PARTS, ckpt_start, 0)

    make_bands(bands)

    for edge in (0, 1, PLANES + 2, PLANES + 3):
        for which in range(2):
            halves[which, edge] = jnp.zeros((SPAN, LANES), F32)
    for ref, slots in ((fields, 2), (lams, 3)):
        for slot in range(slots):
            for edge in (0, 1, PLANES + 2, PLANES + 3):
                ref[slot, edge] = jnp.zeros((SPAN + 2 * PAD, LANES), F32)
            for edge in range(2, PLANES + 2):
                ref[slot, edge, pl.ds(0, PAD)] = jnp.zeros((PAD, LANES), F32)
                ref[slot, edge, pl.ds(PAD + SPAN, PAD)] = jnp.zeros((PAD, LANES), F32)
    for which in range(2):
        fields[which, pl.ds(2 + 2 * part, 2), pl.ds(PAD, SPAN)] = stage[which, part]
    for tile in (0, 1, 5):
        placed[:, tile] = jnp.zeros((LOCAL * near, 8, LANES), F32)

    summed_r[...] = jnp.zeros(summed_r.shape, F32)

    def receivers(step):
        at = pl.ds(pl.multiple_of(step * CHUNK, CHUNK), CHUNK)
        flat = listing[:, at]
        zc = lax.shift_right_logical(flat, 14)
        x = lax.shift_right_logical(flat, 8) & 63
        y = (flat & 255) - (OWN * part - HALO)
        row = (lax.shift_right_logical(zc, 2) * 2 + (zc & 1)) * SPAN + x
        column = jnp.where((y >= 0) & (y < 64), (lax.shift_right_logical(zc, 1) & 1) * 64 + y, -1)
        hot = (iota((PLANES * SPAN, CHUNK), 0) == row).astype(F32).astype(BF16)
        match = iota((LANES, CHUNK), 0) == column
        for k in range(STEPS):
            value = record[0, pl.ds(k, 1), at]
            high = value.astype(BF16).astype(F32)
            rest = value - high
            onto[pl.ds(LANES * k, LANES), pl.ds(0, CHUNK)] = jnp.where(match, high, 0.0).astype(BF16)
            onto[pl.ds(LANES * k, LANES), pl.ds(CHUNK, CHUNK)] = jnp.where(match, rest, 0.0).astype(BF16)
        dims = (((1,), (1,)), ((), ()))
        both = jnp.concatenate([hot, hot], axis=1)
        summed_r[...] += lax.dot_general(both, onto[...], dims, preferred_element_type=F32)

    def more(step, carry):
        receivers(step)
        return carry

    inputs[3].wait()
    inputs[4].wait()
    lax.fori_loop(0, FIRST, more, 0)

    for step in FAR_FIRST:
        model_copy(level, along(step)).wait_recv()

    tile_lane = iota((8, LANES), 1)
    odd = iota((8, LANES), 0) & 1

    def spot(shot_k):
        t = offx[shot_k] - (ROWS * group + 2 * level) + SPAN
        oy = offy[shot_k]
        return lax.shift_right_logical(t, 6) - 1, t & 63, lax.shift_right_logical(oy, 7), oy & 127

    def cut(step, carry):
        to = lax.rem(level + near + lax.div(near - step, 2) * (1 - 2 * lax.rem(step, 2)), near)
        for b in range(LOCAL):
            block, rest, tile, at = spot(LOCAL * to + b)
            upper_rows = odd >= rest
            q0, q1 = jnp.maximum(block, 0), jnp.minimum(block + 1, near - 1)
            back = lax.rem(LANES - at, LANES)
            keep = tile_lane < LANES - at
            turned = []
            for k in range(3):
                t = jnp.minimum(tile + k, 3)
                turned.append(pltpu.roll(jnp.where(upper_rows, cyclic[q0, t], cyclic[q1, t]), back, 1))
            for k in range(2):
                rows_out[to, pl.ds(8 * (2 * b + k), 8)] = jnp.where(keep, turned[k], turned[k + 1])
        @pl.when(to != level)
        def _():
            rows_copy(to, level).start()
        return carry

    lax.fori_loop(0, near, cut, 0)
    rows_in[pl.ds(pl.multiple_of(SPAN * level, SPAN), SPAN)] = rows_out[level]
    lax.fori_loop(FIRST, SECOND, more, 0)
    for step in FAR_FIRST:
        rows_copy(level, along(step)).wait_recv()

    def window_copy(to, origin):
        return pltpu.make_async_remote_copy(
            src_ref=windows.at[to],
            dst_ref=arrived.at[pl.ds(2 * lax.rem(origin, PARTS), 2), pl.ds(ROWS * lax.div(origin, PARTS), ROWS)],
            send_sem=w_send.at[to], recv_sem=w_recv.at[origin],
            device_id=device(to), device_id_type=MESH,
        )

    def share(b, carry):
        for plane in range(4):
            for k in range(2):
                for j in range(2):
                    rows_16[plane, k, pl.ds(j, 8, stride=2)] = (
                        rows_in[pl.ds(8 * (2 * b + k) + 2 * plane + j, 8, stride=SPAN)]
                    )
        for i in range(2):
            low = [rows_16[i, k, pl.ds(0, ROWS)] for k in range(2)]
            high = [pltpu.roll(rows_16[2 + i, k, pl.ds(0, ROWS)], 64, 1) for k in range(2)]
            for to in range(PARTS):
                windows[b * PARTS + to, i] = window(low, high, to)
        for to in range(PARTS):
            @pl.when(b * PARTS + to != me)
            def _():
                window_copy(b * PARTS + to, me).start()
        return carry

    lax.fori_loop(0, LOCAL, share, 0)
    arrived[pl.ds(2 * part, 2), pl.ds(ROWS * group, ROWS)] = windows[me]
    lax.fori_loop(SECOND, listing.shape[1] // CHUNK, more, 0)

    def prepare(field, slot, which):
        value = field[slot, pl.ds(2, PLANES), pl.ds(PAD, SPAN)].reshape(PLANES * SPAN, LANES)
        high = value.astype(BF16)
        rest = (value - high.astype(F32)).astype(BF16)
        dims = (((1,), (0,)), ((), ()))
        main = lax.dot_general(
            jnp.concatenate([high, rest], axis=1), bands[pl.ds(0, 2 * LANES)], dims, preferred_element_type=F32
        )
        minor = lax.dot_general(high, bands[pl.ds(2 * LANES, LANES), pl.ds(0, LANES)], dims, preferred_element_type=F32)
        along_y[which] = (main[:, :LANES] + minor).reshape(PLANES, SPAN, LANES)
        halves[which, pl.ds(2, PLANES)] = main[:, LANES:].reshape(PLANES, SPAN, LANES)

    def laplace(field, slot, which, e):
        result = []
        at = 2 + 2 * e

        def own(k):
            return field[slot, at + k, pl.ds(PAD, SPAN)]

        other = {k: jnp.where(lower, halves[which, at + k], halves[which, at + k + 2]) for k in (-2, -1, 0, 1)}
        along_z = (
            ((own(1), other[-1]), (other[0], other[-2]), (other[1], own(-1)), (own(2), own(-2))),
            ((other[0], own(0)), (other[1], other[-1]), (own(2), other[-2]), (own(3), own(-1))),
        )
        for i in range(2):
            total = 2.0 * stencil_weights[0] * own(i) + along_y[which, at + i - 2]
            for k in range(1, 5):
                some = along_z[i][k - 1][0] + along_z[i][k - 1][1]
                some = some + field[slot, at + i, pl.ds(PAD + k, SPAN)]
                some = some + field[slot, at + i, pl.ds(PAD - k, SPAN)]
                total = total + stencil_weights[k] * some
            result.append(total)
        return result

    def residual(k, p):
        return summed_r[pl.ds(pl.multiple_of(p * SPAN, SPAN), SPAN), pl.ds(LANES * k, LANES)]

    def to_lam(p, carry):
        lams[0, p + 2, pl.ds(PAD, SPAN)] = residual(0, p)
        return carry

    lax.fori_loop(0, PLANES, to_lam, 0)

    def ckpt_wait(which):
        def one(k, carry):
            ckpt_copy(which, part, lax.rem(part + k, PARTS)).wait_recv()
            return carry

        lax.fori_loop(1, PARTS, one, 0)

    ckpt_wait(0)

    def ckpt_sent(k, carry):
        to = lax.rem(part + k, PARTS)
        ckpt_copy(0, to, part).wait_send()
        ckpt_copy(1, to, part).wait_send()
        return carry

    prepare(fields, 0, 0)
    prepare(lams, 0, 1)

    def first(e, carry):
        for which, field in ((0, fields), (1, lams)):
            for i, value in enumerate(laplace(field, 0, which, e)):
                first_lap[which, 2 * e + i] = value
        return carry

    lax.fori_loop(0, PARTS, first, 0)

    ckpt_wait(1)
    lax.fori_loop(1, PARTS, ckpt_sent, 0)
    for far in FAR_FIRST:
        model_copy(along(far), level).wait_send()
        rows_copy(along(far), level).wait_send()

    turn = offx[shot] & 63

    def make_c2v(k):
        e = lax.rem(part + k, PARTS)
        for b in range(LOCAL):
            @pl.when(b * PARTS + e != me)
            def _():
                window_copy(me, b * PARTS + e).wait_recv()
        for i in range(2):
            p = 2 * e + i
            rows = arrived[p]
            doubled[i, pl.ds(0, SPAN)] = rows
            doubled[i, pl.ds(SPAN, SPAN)] = rows
            speed = doubled[i, pl.ds(turn, SPAN)]
            speeds[p] = speed
            scaled = courant * speed
            c2v[p] = scaled * scaled
        return e

    flat = place[0]
    zc = lax.shift_right_logical(flat, 14)
    sy = (flat & 255) - (OWN * part - HALO)
    s_plane = lax.shift_right_logical(zc, 2) * 2 + (zc & 1)
    s_lane = jnp.where((sy >= 0) & (sy < 64), (lax.shift_right_logical(zc, 1) & 1) * 64 + sy, -1)
    at_source = (lane == s_lane) & (iota((SPAN, LANES), 0) == (lax.shift_right_logical(flat, 8) & 63))

    def accel_of(value, p, n):
        strength = jnp.where(p == s_plane, pulse[0, n], 0.0)
        return c2v[p] * value + jnp.where(at_source, strength, 0.0)

    inner = pl.ds(PAD, SPAN)

    def step_loop(n):
        now, old = n % 2, 1 - n % 2
        if n:
            prepare(fields, now, 0)
            if n < STEPS - 1:
                prepare(lams, n, 1)

        def step(e, carry):
            if not n:
                e = make_c2v(e)
            laps = laplace(fields, now, 0, e) if n else [first_lap[0, 2 * e + i] for i in range(2)]
            accel = [accel_of(laps[i], 2 * e + i, n) for i in range(2)]
            if n < STEPS - 1:
                laps = laplace(lams, n, 1, e) if n else [first_lap[1, 2 * e + i] for i in range(2)]
            for i in range(2):
                p = 2 * e + i
                if n < STEPS - 1:
                    fields[old, p + 2, inner] = (
                        2.0 * fields[now, p + 2, inner] - fields[old, p + 2, inner] + accel[i]
                    )
                    lam = lams[n, p + 2, inner]
                    newer = 2.0 * lam + c2v[p] * laps[i] + residual(n + 1, p)
                    if n:
                        newer = newer - lams[n - 1, p + 2, inner]
                if n < STEPS - 2:
                    accels[n, p] = accel[i]
                    lams[n + 1, p + 2, inner] = newer
                elif n == STEPS - 2:
                    partial[p] = newer * accels[0, p] + lam * accels[1, p] + lams[1, p + 2, inner] * accel[i]
            if n == STEPS - 1:
                send_parts(e, [
                    (partial[2 * e + i] + lams[0, 2 * e + i + 2, inner] * accel[i]) * 2.0 / speeds[2 * e + i]
                    for i in range(2)
                ])
            return carry

        if n < STEPS - 1:
            lax.fori_loop(0, PARTS, step, 0)
            return
        for piece in range(PIECES):
            lax.fori_loop(piece * PARTS // PIECES, (piece + 1) * PARTS // PIECES, step, 0)
            for far in FAR_FIRST:
                z_copy(along(far), level, piece).start()

    def send_parts(e, parts):
        both = jnp.where((lane & 63) < OWN, pltpu.roll(parts[0], LANES - HALO, 1), pltpu.roll(parts[1], OWN - HALO, 1))
        packed[e, pl.ds(0, SPAN)] = both
        packed[e, pl.ds(SPAN, SPAN)] = both
        outgoing[e, pl.ds(0, SPAN)] = packed[e, pl.ds((SPAN - turn) & 63, SPAN)]
        for to in range(near):
            for j in range(2):
                z_out[to, pl.ds(8 * e + 4 * j, 4)] = outgoing[e, pl.ds(2 * to + j, 4, stride=ROWS)]

    def z_copy(to, origin, piece):
        rows = SPAN // PIECES
        return pltpu.make_async_remote_copy(
            src_ref=z_out.at[to, pl.ds(rows * piece, rows)],
            dst_ref=z_in.at[pl.ds(SPAN * origin + rows * piece, rows)],
            send_sem=z_send.at[piece, to], recv_sem=z_recv.at[piece, origin],
            device_id=(LOCAL * to + group, part), device_id_type=MESH,
        )

    for n in range(STEPS):
        step_loop(n)
    z_in[pl.ds(pl.multiple_of(SPAN * level, SPAN), SPAN)] = z_out[level]

    def out_copy(to, origin):
        return pltpu.make_async_remote_copy(
            src_ref=outgoing_2.at[to], dst_ref=landed.at[origin],
            send_sem=o_send.at[to], recv_sem=o_recv.at[origin],
            device_id=device(to), device_id_type=MESH,
        )

    def out_start(e, carry):
        for b in range(LOCAL):
            for j in range(2):
                outgoing_2[b * PARTS + e, pl.ds(8 * j, 8)] = z_in[pl.ds(8 * e + 4 * j + b, 8, stride=SPAN)]
            @pl.when(b * PARTS + e != me)
            def _():
                out_copy(b * PARTS + e, me).start()
        return carry

    def windows_sent(k, carry):
        window_copy(lax.rem(me + k, peers), me).wait_send()
        return carry

    lax.fori_loop(1, peers, windows_sent, 0)
    for piece in range(PIECES):
        for far in FAR_FIRST:
            z_copy(level, along(far), piece).wait_recv()
        lax.fori_loop(piece * PARTS // PIECES, (piece + 1) * PARTS // PIECES, out_start, 0)
    landed[me] = outgoing_2[me]


    group_of = lax.shift_right_logical(tile_lane, 5)

    def put(k, carry):
        b = lax.rem(group + k, LOCAL)
        for c in range(PARTS):
            @pl.when(b * PARTS + c != me)
            def _():
                out_copy(me, b * PARTS + c).wait_recv()
        for j in range(2):
            for k in range(2):
                pieces = [landed[b * PARTS + 4 * k + c, pl.ds(8 * j, 8)] for c in range(4)]
                for plane in range(4):
                    total = None
                    for c in range(4):
                        by = (OWN * (c - plane)) % LANES
                        piece = pltpu.roll(pieces[c], by, 1) if by else pieces[c]
                        total = piece if total is None else jnp.where(group_of == c, piece, total)
                    by_shot[k, pl.ds(8 * (2 * plane + j), 8)] = total
        for z in range(near):
            at = offy[LOCAL * z + b] & 127
            keep = tile_lane >= at
            first, second = (pltpu.roll(by_shot[k, pl.ds(z, 8, stride=8)], at, 1) for k in range(2))
            placed[b * near + z, 2] = jnp.where(keep, first, 0.0)
            placed[b * near + z, 3] = jnp.where(keep, second, first)
            placed[b * near + z, 4] = jnp.where(keep, 0.0, second)
        return carry

    lax.fori_loop(0, LOCAL, put, 0)

    def add_up(k, sums):
        block, rest, tile, _ = spot(LOCAL * lax.rem(k, near) + lax.div(k, near))
        block = jnp.where(odd >= rest, block, block + 1)
        cells = placed[k, pl.ds(2 - tile, 4)]
        return tuple(total + jnp.where(block == q, cells, 0.0) for q, total in enumerate(sums))

    zero = jnp.zeros((4, 8, LANES), F32)
    for q, total in enumerate(lax.fori_loop(0, LOCAL * near, add_up, (zero,) * near)):
        totals[q] = total.reshape(OWN, LANES)

    def sum_copy(to, origin):
        return pltpu.make_async_remote_copy(
            src_ref=totals.at[to], dst_ref=sums.at[pl.ds(OWN * origin, OWN)],
            send_sem=s_send.at[to], recv_sem=s_recv.at[origin],
            device_id=(LOCAL * to + group, part), device_id_type=MESH,
        )

    for step in FAR_FIRST:
        sum_copy(along(step), level).start()
    sums[pl.ds(pl.multiple_of(OWN * level, OWN), OWN)] = totals[level]

    def outs_sent(k, carry):
        out_copy(lax.rem(me + k, peers), me).wait_send()
        return carry

    lax.fori_loop(1, peers, outs_sent, 0)
    for far in FAR_FIRST:
        for piece in range(PIECES):
            z_copy(along(far), level, piece).wait_send()
    for step in FAR_FIRST:
        sum_copy(level, along(step)).wait_recv()
    for plane in range(4):
        for tile in range(4):
            for j in range(2):
                final[plane, tile, pl.ds(j, near, stride=2)] = (
                    sums[pl.ds(8 * tile + 2 * plane + j, near, stride=OWN)]
                )
        speed = model[plane]
        total = jnp.concatenate([final[plane, tile, pl.ds(0, ROWS)] for tile in range(4)], axis=-1)
        scaling = (speed - lower_bound) * (upper_bound - speed) / (upper_bound - lower_bound)
        limit = barrier_weight / (upper_bound - speed) - barrier_weight / (speed - lower_bound)
        out[plane] = scaling * (total + limit)

    for far in FAR_FIRST:
        sum_copy(along(far), level).wait_send()


def on_device(near, model, offsets_x, offsets_y, ckpt_prev, ckpt_cur, wavelet, source, receivers, traces):
    peers = LOCAL * PARTS
    vmem = pl.BlockSpec(memory_space=pltpu.VMEM)
    smem = pl.BlockSpec(memory_space=pltpu.SMEM)
    padded = (PLANES + 4, SPAN + 2 * PAD, LANES)
    plain = (PLANES, SPAN, LANES)
    dma = pltpu.SemaphoreType.DMA
    return pl.pallas_call(
        functools.partial(kernel, near),
        out_shape=jax.ShapeDtypeStruct(model.shape, F32),
        in_specs=[smem] * 4 + [pl.BlockSpec(memory_space=pltpu.HBM)] * 5,
        out_specs=vmem,
        scratch_shapes=[
            *(pltpu.VMEM(a.shape, a.dtype) for a in (model, ckpt_prev, ckpt_cur, receivers, traces)),
            pltpu.VMEM((near, 4, 8, LANES), F32),
            pltpu.VMEM((near, 4, 8, LANES), F32),
            pltpu.VMEM((near, SPAN, LANES), F32),
            pltpu.VMEM((near * SPAN + SPAN, LANES), F32),
            pltpu.VMEM((4, 2, ROWS + PAD, LANES), F32),
            pltpu.VMEM((2, PARTS, 2, SPAN, LANES), F32),
            pltpu.VMEM((2,) + padded, F32),
            pltpu.VMEM((3,) + padded, F32),
            pltpu.VMEM((3 * LANES, 2 * LANES), BF16),
            pltpu.VMEM((2,) + plain, F32),
            pltpu.VMEM((2, PLANES + 4, SPAN, LANES), F32),
            pltpu.VMEM((STEPS * LANES, 2 * CHUNK), BF16),
            pltpu.VMEM((PLANES * SPAN, STEPS * LANES), F32),
            pltpu.VMEM((peers, 2, ROWS, LANES), F32),
            pltpu.VMEM(plain, F32),
            pltpu.VMEM((2, 2 * SPAN, LANES), F32),
            pltpu.VMEM(plain, F32),
            pltpu.VMEM(plain, F32),
            pltpu.VMEM((2,) + plain, F32),
            pltpu.VMEM((2,) + plain, F32),
            pltpu.VMEM(plain, F32),
            pltpu.VMEM((PARTS, 2 * SPAN, LANES), F32),
            pltpu.VMEM((PARTS, SPAN + ROWS, LANES), F32),
            pltpu.VMEM((near, SPAN, LANES), F32),
            pltpu.VMEM((near * SPAN + SPAN, LANES), F32),
            pltpu.VMEM((peers, ROWS, LANES), F32),
            pltpu.VMEM((peers, ROWS, LANES), F32),
            pltpu.VMEM((2, SPAN + PAD, LANES), F32),
            pltpu.VMEM((LOCAL * near, 6, 8, LANES), F32),
            pltpu.VMEM((near, OWN, LANES), F32),
            pltpu.VMEM((near * OWN + OWN, LANES), F32),
            pltpu.VMEM((4, 4, ROWS + PAD, LANES), F32),
            dma((5,)),
            dma((near,)), dma((near,)), dma((near,)), dma((near,)),
            dma((2, PARTS)), dma((2, PARTS)),
            dma((peers,)), dma((peers,)), dma((peers,)), dma((peers,)),
            dma((PIECES, near)), dma((PIECES, near)), dma((near,)), dma((near,)),
        ],
        compiler_params=pltpu.CompilerParams(
            collective_id=0, has_side_effects=True, vmem_limit_bytes=62 * 1024 * 1024
        ),
    )(offsets_x, offsets_y, wavelet, source, model, ckpt_prev, ckpt_cur, receivers, traces)


def solution(mesh):
    placed = (
        P("depth", "shots", None),
        P(),
        P(),
        P("shots", "depth", None, None),
        P("shots", "depth", None, None),
        P("shots", None),
        P("shots"),
        P("shots", None),
        P("shots", None, None),
    )
    near = mesh.shape["shots"] // LOCAL
    return jax.shard_map(
        functools.partial(on_device, near),
        mesh=mesh, in_specs=placed, out_specs=P("depth", "shots", None), check_vma=False,
    )
```
